32 devices in a mesh: ens: 2 (over y), dom: 4 (over z), feat: 2 (over x), rep: 2 (over core).
Axes of the slice: x: 2, y: 2, z: 4, core: 2. Of those that a mesh axis runs over, the one named last changes fastest.
Arguments:
- grid_state: bfloat16 [8192, 512], P(('ens', 'dom', 'feat', 'rep')), parts along dimension 0, may hold values from -6 to 6
- mesh_base: bfloat16 [2048, 512], P('dom'), may hold values from -6 to 6
- edge_state: bfloat16 [16384, 512], P(('dom', 'feat', 'rep')), may hold values from -6 to 6
- enc_weight: bfloat16 [512, 512], P(('feat', 'rep')), may hold values from -0.25 to 0.25
- edge_in_weight: bfloat16 [1536, 512], P(('feat', 'rep')), may hold values from -0.15625 to 0.15625
- edge_out_weight: bfloat16 [512, 512], P(('feat', 'rep')), may hold values from -0.25 to 0.25
- node_in_weight: bfloat16 [1024, 512], P(('feat', 'rep')), may hold values from -0.1875 to 0.1875
- node_out_weight: bfloat16 [512, 512], P(('feat', 'rep')), may hold values from -0.25 to 0.25
- node_grad: bfloat16 [4096, 512], P(('ens', 'dom')), parts along dimension 0, may hold values from -6 to 6
- edge_grad: bfloat16 [32768, 512], P(('ens', 'dom', 'feat', 'rep')), parts along dimension 0, may hold values from -6 to 6
- halo_rows: int32 [4, 4, 128], P('dom'), may hold values from 0 to 511
- edge_send: int32 [16384], P(('dom', 'feat', 'rep')), may hold values from 0 to 1023
- edge_recv: int32 [16384], P(('dom', 'feat', 'rep')), may hold values from 0 to 511
- grid_send: int32 [16, 4, 128], P(('dom', 'feat', 'rep')), may hold values from 0 to 256, as said below
- grid_recv: int32 [16, 4, 128], P(('dom', 'feat', 'rep')), may hold values from 0 to 512, as said below
Outputs:
- grid_adjoint: float32 [8192, 512], P(('ens', 'dom', 'feat', 'rep')), parts along dimension 0
The draws below stay inside these ranges and needn't reach their ends.
There are 2 independent parts, one for each index of `ens`. The reference program is written for one: setup_inputs(seed, part) draws one part's arguments, and reference() takes and returns one part's arrays. A program takes and returns all parts, laid end to end along the dimension named above; an argument that names none is the same for every part. Nothing has to cross between parts.
Inputs may be any that keep to these rules, and one draw needn't show every extreme that they name: `edge_send`: values below 512 name local nodes; the others name halo rows. `grid_send`: 256 marks an empty slot; each of a device's 256 rows fills exactly one slot; every device fills all 128 slots to its own partition and to one partition that is the same for all devices (when these are the same partition, the device's other rows may go to any partitions). `grid_recv`: 512 stands exactly where the matching grid_send slot is empty.
All inputs are finite; a program needn't handle non-finite values.
Results may differ from the reference program's by a relative error of at most 0.02.
Values may be sent and summed in bfloat16 or wider, within the bound.
No kernel may reach another device: no remote copies, remote signals or barrier semaphores. Data moves between devices by JAX's collectives and lax.ppermute only.
A program may use at most 64 MiB of HBM per device.

```python
import jax
import jax.numpy as jnp

D = 512
NODE_DEV = 512
EDGE_DEV = 1024
GRID_DEV = 256
HALO_SLOTS = 128
GRID_SLOTS = 128
NODES = 2048
EDGES = 16384
GRID = 4096
N_DOM = 4
N_FEAT = 2
N_REP = 2


def grid_tables(key):
    members = N_FEAT * N_REP
    slot_total = N_DOM * GRID_SLOTS
    crowded = jax.random.randint(jax.random.fold_in(key, 7), (), 0, N_DOM)

    def one_device(device_index):
        device_key = jax.random.fold_in(key, device_index + 100)
        home_dom = device_index // members
        target_dom = jnp.arange(slot_total, dtype=jnp.int32) // GRID_SLOTS
        priority = jnp.logical_or(target_dom == home_dom, target_dom == crowded).astype(jnp.int32)
        jitter = jax.random.randint(jax.random.fold_in(device_key, 1), (slot_total,), 0, 1024)
        slot_score = (priority * 1024 + jitter) * slot_total + jnp.arange(slot_total, dtype=jnp.int32)
        slot_order = jnp.argsort(-slot_score)
        row_perm = jax.random.permutation(jax.random.fold_in(device_key, 2), GRID_DEV).astype(jnp.int32)
        send_table = jnp.full((slot_total,), GRID_DEV, jnp.int32).at[slot_order[:GRID_DEV]].set(row_perm)
        node_draw = jax.random.randint(jax.random.fold_in(device_key, 3), (slot_total,), 0, NODE_DEV)
        recv_table = jnp.where(send_table < GRID_DEV, node_draw, NODE_DEV).astype(jnp.int32)
        return (send_table.reshape(N_DOM, GRID_SLOTS), recv_table.reshape(N_DOM, GRID_SLOTS))
    return jax.vmap(one_device)(jnp.arange(N_DOM * members, dtype=jnp.int32))


def draw_grid_send(key, part):
    send_table, recv_table = grid_tables(key)
    return send_table


def draw_grid_recv(key, part):
    send_table, recv_table = grid_tables(key)
    members = N_FEAT * N_REP
    arranged = recv_table.reshape(N_DOM, members, N_DOM, GRID_SLOTS).transpose(2, 1, 0, 3)
    return arranged.reshape(N_DOM * members, N_DOM, GRID_SLOTS)


def set_ends(values, key, smallest, top_value):
    index_at = [jax.random.randint(jax.random.fold_in(key, axis), (), 0, length) for axis, length in enumerate(values.shape)]
    widest = values.shape.index(max(values.shape))
    beside = index_at[:widest] + [(index_at[widest] + 1) % values.shape[widest]] + index_at[widest + 1:]
    return values.at[tuple(index_at)].set(smallest).at[tuple(beside)].set(top_value)


def shard_levels(rng, extent, cuts, smallest, high):
    def one(axis_at, parts):
        steps = jax.random.uniform(jax.random.fold_in(jax.random.fold_in(rng, 6), axis_at), (parts,), jnp.float32, smallest / len(cuts), high / len(cuts))
        return jnp.repeat(jnp.exp(steps), extent[axis_at] // parts).reshape((-1,) + (1,) * (len(extent) - axis_at - 1))

    factor_of = one(*cuts[0])
    for cut in cuts[1:]:
        factor_of = factor_of * one(*cut)
    return factor_of


def gaussian(rng, extent, scale, bound, shards=(), held_as=jnp.bfloat16):
    drawn = jax.random.normal(rng, extent, jnp.float32) * scale
    if len(shards) > 0:
        drawn = shard_levels(rng, extent, shards, -0.22, 0.18) * drawn
    return jnp.clip(drawn, min=-bound, max=bound).astype(held_as)


def setup_inputs(seed: int = 0, part: int = 0) -> dict:
    splits = jax.random.split(jax.random.key(seed), 16)
    part_keys = jax.random.split(jax.random.fold_in(splits[15], part), 16)
    return {
        "grid_state": gaussian(part_keys[0], (GRID, D), 1.0, 6.0, ((0, 16),)),
        "mesh_base": gaussian(splits[1], (NODES, D), 1.0, 6.0, ((0, 4),)),
        "edge_state": gaussian(splits[2], (EDGES, D), 1.0, 6.0, ((0, 16),)),
        "enc_weight": gaussian(splits[3], (D, D), D ** -0.5, 0.25, ((0, 4),)),
        "edge_in_weight": gaussian(splits[4], (3 * D, D), (3 * D) ** -0.5, 0.15625, ((0, 4),)),
        "edge_out_weight": gaussian(splits[5], (D, D), D ** -0.5, 0.25, ((0, 4),)),
        "node_in_weight": gaussian(splits[6], (2 * D, D), (2 * D) ** -0.5, 0.1875, ((0, 4),)),
        "node_out_weight": gaussian(splits[7], (D, D), D ** -0.5, 0.25, ((0, 4),)),
        "node_grad": gaussian(part_keys[8], (NODES, D), 1.0, 6.0, ((0, 4),)),
        "edge_grad": gaussian(part_keys[9], (EDGES, D), 1.0, 6.0, ((0, 16),)),
        "halo_rows": set_ends(jax.random.randint(splits[10], (N_DOM, N_DOM, HALO_SLOTS), 0, NODE_DEV), jax.random.fold_in(splits[10], 1), 0, NODE_DEV - 1).astype(jnp.int32),
        "edge_send": set_ends(jax.random.randint(splits[11], (EDGES,), 0, 2 * NODE_DEV), jax.random.fold_in(splits[11], 1), 0, (2 * NODE_DEV) - 1).astype(jnp.int32),
        "edge_recv": set_ends(jax.random.randint(splits[12], (EDGES,), 0, NODE_DEV), jax.random.fold_in(splits[12], 1), 0, NODE_DEV - 1).astype(jnp.int32),
        "grid_send": draw_grid_send(jax.random.fold_in(splits[15], 71), part),
        "grid_recv": draw_grid_recv(jax.random.fold_in(splits[15], 71), part),
    }


def silu_slope(values):
    logistic = jax.nn.sigmoid(values)
    return logistic * (1.0 + values * (1.0 - logistic))


def matmul(first_op, second_op):
    return jnp.dot(first_op, second_op, preferred_element_type=jnp.float32)


def grid_owner(grid_send, grid_recv):
    members = N_FEAT * N_REP
    devices = jnp.arange(N_DOM * members, dtype=jnp.int32)
    source_dom = devices // members
    member = devices % members
    targets = jnp.arange(N_DOM, dtype=jnp.int32)
    slot_index = jnp.arange(GRID_SLOTS, dtype=jnp.int32)
    receiving = targets[None, :, None] * members + member[:, None, None]
    local_nodes = grid_recv[receiving, source_dom[:, None, None], slot_index[None, None, :]]
    filled = grid_send < GRID_DEV
    global_rows = jnp.where(filled, devices[:, None, None] * GRID_DEV + grid_send, GRID)
    global_nodes = targets[None, :, None] * NODE_DEV + local_nodes
    owner_map = jnp.zeros((GRID,), jnp.int32)
    return owner_map.at[global_rows.reshape(-1)].set(global_nodes.reshape(-1).astype(jnp.int32), mode="drop")


def edge_ends(halo_rows, edge_send, edge_recv):
    home_dom = jnp.arange(EDGES, dtype=jnp.int32) // (EDGE_DEV * N_FEAT * N_REP)
    halo_offset = jnp.maximum(edge_send - NODE_DEV, 0)
    peer_dom = jnp.minimum(halo_offset // HALO_SLOTS, N_DOM - 1)
    peer_slot = halo_offset % HALO_SLOTS
    remote = peer_dom * NODE_DEV + halo_rows[peer_dom, home_dom, peer_slot]
    senders = jnp.where(edge_send < NODE_DEV, home_dom * NODE_DEV + edge_send, remote)
    receivers = home_dom * NODE_DEV + edge_recv
    return senders.astype(jnp.int32), receivers.astype(jnp.int32)


def reference(grid_state, mesh_base, edge_state, enc_weight, edge_in_weight, edge_out_weight, node_in_weight, node_out_weight, node_grad, edge_grad, halo_rows, edge_send, edge_recv, grid_send, grid_recv):
    owner_map = grid_owner(grid_send, grid_recv)
    senders, receivers = edge_ends(halo_rows, edge_send, edge_recv)
    grid_pre = matmul(grid_state, enc_weight)
    grid_message = jax.nn.silu(grid_pre).astype(jnp.bfloat16)
    encoded = jnp.zeros((NODES, D), jnp.float32).at[owner_map].add(grid_message.astype(jnp.float32))
    mesh_state = (mesh_base.astype(jnp.float32) + encoded).astype(jnp.bfloat16)
    edge_pre = matmul(edge_state, edge_in_weight[:D]) + matmul(mesh_state[senders], edge_in_weight[D:2 * D]) + matmul(mesh_state[receivers], edge_in_weight[2 * D:])
    edge_hidden = jax.nn.silu(edge_pre).astype(jnp.bfloat16)
    edge_new = (edge_state.astype(jnp.float32) + matmul(edge_hidden, edge_out_weight)).astype(jnp.bfloat16)
    aggregate = jnp.zeros((NODES, D), jnp.float32).at[receivers].add(edge_new.astype(jnp.float32)).astype(jnp.bfloat16)
    node_pre = matmul(mesh_state, node_in_weight[:D]) + matmul(aggregate, node_in_weight[D:])
    node_dpre = (matmul(node_grad, node_out_weight.T) * silu_slope(node_pre)).astype(jnp.bfloat16)
    node_dinput = matmul(node_dpre, node_in_weight.T)
    edge_cot = (edge_grad.astype(jnp.float32) + node_dinput[receivers, D:]).astype(jnp.bfloat16)
    edge_dpre = (matmul(edge_cot, edge_out_weight.T) * silu_slope(edge_pre)).astype(jnp.bfloat16)
    edge_dnodes = matmul(edge_dpre, edge_in_weight[D:].T)
    mesh_cot = node_grad.astype(jnp.float32) + node_dinput[:, :D]
    mesh_cot = mesh_cot.at[senders].add(edge_dnodes[:, :D]).at[receivers].add(edge_dnodes[:, D:])
    grid_dpre = (mesh_cot[owner_map] * silu_slope(grid_pre)).astype(jnp.bfloat16)
    return matmul(grid_dpre, enc_weight.T)
```

```python
import jax
import jax.numpy as jnp
from jax import lax
from jax.experimental import pallas as pl
from jax.experimental.pallas import tpu as pltpu
from jax.sharding import PartitionSpec as P

BF = jnp.bfloat16
F32 = jnp.float32
SMEM = pl.BlockSpec(memory_space=pltpu.SMEM)
VMEM = pl.BlockSpec(memory_space=pltpu.VMEM)


def dot(a, b):
    return jnp.dot(a, b, preferred_element_type=F32)


def dot_t(a, b):
    return lax.dot_general(a, b, (((1,), (1,)), ((), ())), preferred_element_type=F32)


def silu_slope(values):
    logistic = jax.nn.sigmoid(values)
    return logistic * (1.0 + values * (1.0 - logistic))


def to_column(row):
    return jnp.transpose(jnp.broadcast_to(row, (8, row.shape[1])))[:, :1]


def hot_rows(row, depth):
    length = row.shape[1]
    return (to_column(row) == lax.broadcasted_iota(jnp.int32, (length, depth), 1)).astype(BF)


def hot_columns(row, depth):
    length = row.shape[1]
    return (row == lax.broadcasted_iota(jnp.int32, (depth, length), 0)).astype(BF)


def column_pick(me, depth, cols):
    at = lax.broadcasted_iota(jnp.int32, (depth, cols), 0) - me * cols
    return (at == lax.broadcasted_iota(jnp.int32, (depth, cols), 1)).astype(BF)


def rows_at(index, count):
    return pl.ds(pl.multiple_of(index * count, count), count)


def lanes(parts):
    return parts[0] if len(parts) == 1 else jnp.concatenate(parts, axis=1)


def stack(parts):
    return parts[0] if len(parts) == 1 else jnp.concatenate(parts, axis=0)


def call(body, name, me, ins, outs, scratch=(), flops=0):
    size = lambda s: s.size * s.dtype.itemsize
    moved = sum(size(x) for x in ins) + sum(size(x) for x in outs)
    return pl.pallas_call(
        body,
        out_shape=list(outs),
        in_specs=[SMEM] + [VMEM] * len(ins),
        out_specs=[VMEM] * len(outs),
        scratch_shapes=list(scratch),
        compiler_params=pltpu.CompilerParams(vmem_limit_bytes=48 * 2**20),
        cost_estimate=pl.CostEstimate(flops=flops, bytes_accessed=moved, transcendentals=0),
        name=name,
    )(me, *ins)


def shape(dims, dtype=BF):
    return jax.ShapeDtypeStruct(tuple(dims), dtype)


def make_per_device(mesh):
    n_dom, n_feat, n_rep = mesh.shape["dom"], mesh.shape["feat"], mesh.shape["rep"]
    M = n_feat * n_rep

    def member_swap(x, k):
        return lax.ppermute(x, ("feat", "rep"), [(i, i ^ k) for i in range(M)])

    def dom_swap(x, k):
        return lax.ppermute(x, "dom", [(i, i ^ k) for i in range(n_dom)])

    def member_gather(x):
        return [x] + [member_swap(x, k) for k in range(1, M)]

    def member_gather_chips(x):
        parts = [None] * M
        for kf in range(n_feat):
            parts[kf * n_rep] = member_swap(x, kf * n_rep) if kf else x
        for kf in range(n_feat):
            for kr in range(1, n_rep):
                parts[kf * n_rep + kr] = member_swap(parts[kf * n_rep], kr)
        return parts

    def member_trade(parts):
        return [parts[0]] + [member_swap(parts[k], k) for k in range(1, M)]

    def dom_trade(parts):
        return [parts[0]] + [dom_swap(parts[k], k) for k in range(1, n_dom)]

    def dom_order(table, dom):
        bit = 1
        while bit < n_dom:
            pairs = table.reshape((n_dom // (2 * bit), 2, bit) + table.shape[1:])
            swapped = pairs[:, ::-1].reshape(table.shape)
            table = jnp.where((dom & bit) != 0, swapped, table)
            bit *= 2
        return table

    def per_device(
        grid_state,
        mesh_base,
        edge_state,
        enc_weight,
        edge_in_weight,
        edge_out_weight,
        node_in_weight,
        node_out_weight,
        node_grad,
        edge_grad,
        halo_rows,
        edge_send,
        edge_recv,
        grid_send,
        grid_recv,
    ):
        D = mesh_base.shape[1]
        N = mesh_base.shape[0]
        E = edge_state.shape[0]
        G = grid_state.shape[0]
        H = halo_rows.shape[2]
        S = grid_send.shape[2]
        NH = n_dom * H
        NS = n_dom * S
        C = D // M
        R = N // M
        T = 256
        rows_enc, rows_in, rows_out, rows_node = (
            enc_weight.shape[0],
            edge_in_weight.shape[0],
            edge_out_weight.shape[0],
            node_in_weight.shape[0],
        )
        me = lax.axis_index(("feat", "rep")).astype(jnp.int32)
        dom = lax.axis_index("dom").astype(jnp.int32)
        me1 = me.reshape(1)

        slots = jnp.stack(
            [dom_order(grid_send[0], dom).reshape(-1), dom_order(grid_recv[0], dom).reshape(-1)]
        )
        halo_row = dom_order(halo_rows[0], dom).reshape(1, NH)
        recv_row = edge_recv.reshape(1, E)
        away = edge_send - N
        send_row = jnp.where(away < 0, edge_send, N + ((away // H) ^ dom) * H + away % H).reshape(1, E)

        state_parts = member_gather_chips(grid_state)
        enc_parts = member_gather_chips(enc_weight)
        slot_parts = member_gather(slots)
        in_parts = member_gather_chips(edge_in_weight)
        rest = jnp.concatenate([edge_out_weight, node_in_weight, node_out_weight], axis=0)
        rest_parts = member_gather_chips(rest)

        def grid_kernel(me_ref, *refs):
            states, encs, tables = refs[:M], refs[M : 2 * M], refs[2 * M : 3 * M]
            enc_out, slope_out = refs[3 * M], refs[3 * M + 1]
            outs = refs[3 * M + 2 :]
            me = me_ref[0]
            for k in range(M):
                enc_out[rows_at(me ^ k, rows_enc), :] = encs[k][...]
            enc_cols = dot(enc_out[...], column_pick(me, D, C)).astype(BF)
            for k in range(M):
                pre = dot(states[k][...], enc_cols)
                logistic = jax.nn.sigmoid(pre)
                slope_out[k] = logistic * (1.0 + pre * (1.0 - logistic))
                message = (pre * logistic).astype(BF)
                rows = dot(hot_rows(tables[k][0:1, :], G), message).astype(BF)
                for j in range(n_dom):
                    outs[j][k * S : (k + 1) * S, :] = rows[j * S : (j + 1) * S]

        enc_full, grid_slope, *outgoing = call(
            grid_kernel,
            "grid_messages",
            me1,
            state_parts + enc_parts + slot_parts,
            [shape((D, D)), shape((M, G, C), F32)] + [shape((M * S, C))] * n_dom,
            flops=2 * M * G * D * C + 2 * M * NS * G * C,
        )
        incoming = dom_trade(outgoing)

        def encode_kernel(me_ref, base_ref, halo_ref, *refs):
            tables, arrived = refs[:M], refs[M : M + n_dom]
            state_out, outs = refs[M + n_dom], refs[M + n_dom + 1 :]
            total = dot(base_ref[...], column_pick(me_ref[0], D, C))
            for k in range(M):
                rows = stack([arrived[j][k * S : (k + 1) * S, :] for j in range(n_dom)])
                total += dot(hot_columns(tables[k][1:2, :], N), rows)
            state = total.astype(BF)
            state_out[...] = state
            rows = dot(hot_rows(halo_ref[...], N), state).astype(BF)
            for j in range(n_dom):
                outs[j][...] = rows[j * H : (j + 1) * H]

        state_cols, *halo_out = call(
            encode_kernel,
            "encode",
            me1,
            [mesh_base, halo_row] + slot_parts + incoming,
            [shape((N, C))] + [shape((H, C))] * n_dom,
            flops=2 * M * N * NS * C,
        )
        halo_in = dom_trade(halo_out)
        state_parts2 = member_gather(state_cols)
        halo_cols = jnp.concatenate(halo_in, axis=0)
        halo_parts = member_gather(halo_cols)

        def local_kernel(me_ref, es_ref, send_ref, recv_ref, *refs):
            cols, weights = refs[:M], refs[M : 2 * M]
            pre_out, state_out, w_out, parts = refs[2 * M :]
            me = me_ref[0]
            for k in range(M):
                parts[me ^ k] = cols[k][...]
                w_out[rows_at(me ^ k, rows_in), :] = weights[k][...]
            state_out[...] = lanes([parts[j] for j in range(M)])

            def step(i, _):
                at = rows_at(i, T)
                sent = dot(hot_rows(send_ref[:, at], N), state_out[...]).astype(BF)
                got = dot(hot_rows(recv_ref[:, at], N), state_out[...]).astype(BF)
                pre_out[at, :] = (
                    dot(es_ref[at, :], w_out[:D, :])
                    + dot(sent, w_out[D : 2 * D, :])
                    + dot(got, w_out[2 * D :, :])
                )
                return 0

            lax.fori_loop(0, E // T, step, 0)

        local_pre, mesh_state, in_full = call(
            local_kernel,
            "edge_local",
            me1,
            [edge_state, send_row, recv_row] + state_parts2 + in_parts,
            [shape((E, D), F32), shape((N, D)), shape((3 * D, D))],
            scratch=[pltpu.VMEM((M, N, C), BF)],
            flops=2 * E * D * (3 * D + 2 * N),
        )

        def node_ahead_kernel(me_ref, state_ref, grad_ref, *refs):
            weights = refs[:M]
            out_full, node_in_full, pre_out, cot_out, node_out_full = refs[M:]
            me = me_ref[0]
            for k in range(M):
                first, second = rows_out, rows_out + rows_node
                out_full[rows_at(me ^ k, rows_out), :] = weights[k][:first, :]
                node_in_full[rows_at(me ^ k, rows_node), :] = weights[k][first:second, :]
                node_out_full[rows_at(me ^ k, rows_out), :] = weights[k][second:, :]
            mine = rows_at(me, R)
            pre_out[...] = dot(state_ref[mine, :], node_in_full[:D, :])
            cot_out[...] = dot_t(grad_ref[mine, :], node_out_full[...])

        out_full, node_in_full, node_pre, node_cot = call(
            node_ahead_kernel,
            "node_ahead",
            me1,
            [mesh_state, node_grad] + rest_parts,
            [shape((D, D)), shape((2 * D, D)), shape((R, D), F32), shape((R, D), F32)],
            scratch=[pltpu.VMEM((D, D), BF)],
            flops=4 * R * D * D,
        )

        def edge_kernel(me_ref, local_ref, es_ref, send_ref, recv_ref, w_ref, out_ref, *refs):
            cols = refs[:M]
            pre_out, outs = refs[M], refs[M + 1 : 2 * M + 1]
            parts, halo, total = refs[2 * M + 1 :]
            me = me_ref[0]
            for k in range(M):
                parts[me ^ k] = cols[k][...]
            halo[...] = lanes([parts[j] for j in range(M)])
            total[...] = jnp.zeros_like(total)

            def step(i, _):
                at = rows_at(i, T)
                sent = dot(hot_rows(send_ref[:, at] - N, NH), halo[...]).astype(BF)
                pre = local_ref[at, :] + dot(sent, w_ref[D : 2 * D, :])
                pre_out[at, :] = pre
                hidden = (pre * jax.nn.sigmoid(pre)).astype(BF)
                new = (es_ref[at, :].astype(F32) + dot(hidden, out_ref[...])).astype(BF)
                total[...] += dot(hot_columns(recv_ref[:, at], N), new)
                return 0

            lax.fori_loop(0, E // T, step, 0)
            for k in range(M):
                outs[k][...] = total[rows_at(me ^ k, R), :].astype(BF)

        edge_pre, *sums = call(
            edge_kernel,
            "edge_update",
            me1,
            [local_pre, edge_state, send_row, recv_row, in_full, out_full] + halo_parts,
            [shape((E, D), F32)] + [shape((R, D))] * M,
            scratch=[pltpu.VMEM((M, NH, C), BF), pltpu.VMEM((NH, D), BF), pltpu.VMEM((N, D), F32)],
            flops=2 * E * D * (NH + D + D + N),
        )
        sums = member_trade(sums)

        def node_kernel(me_ref, pre_ref, cot_ref, w_ref, grad_ref, *refs):
            first_out, second_out = refs[M:]
            total = refs[0][...].astype(F32)
            for k in range(1, M):
                total += refs[k][...].astype(F32)
            pre = pre_ref[...] + dot(total.astype(BF), w_ref[D:, :])
            dpre = (cot_ref[...] * silu_slope(pre)).astype(BF)
            second_out[...] = dot_t(dpre, w_ref[D:, :]).astype(BF)
            mine = grad_ref[rows_at(me_ref[0], R), :].astype(F32)
            first_out[...] = mine + dot_t(dpre, w_ref[:D, :])

        node_first, node_second = call(
            node_kernel,
            "node_backward",
            me1,
            [node_pre, node_cot, node_in_full, node_grad] + sums,
            [shape((R, D), F32), shape((R, D))],
            flops=6 * R * D * D,
        )
        second_parts = member_gather(node_second)

        def edge_back_kernel(me_ref, grad_ref, pre_ref, send_ref, recv_ref, w_ref, out_ref, *refs):
            nodes = refs[:M]
            dpre_out, outs = refs[M], refs[M + 1 : 2 * M + 1]
            second, total, parts = refs[2 * M + 1 :]
            me = me_ref[0]
            for k in range(M):
                second[rows_at(me ^ k, R), :] = nodes[k][...]
            total[...] = jnp.zeros_like(total)

            def step(i, _):
                at = rows_at(i, T)
                got = dot(hot_rows(recv_ref[:, at], N), second[...])
                cot = (grad_ref[at, :].astype(F32) + got).astype(BF)
                dpre = (dot_t(cot, out_ref[...]) * silu_slope(pre_ref[at, :])).astype(BF)
                dpre_out[at, :] = dpre
                total[...] += dot(hot_columns(send_ref[:, at] - N, NH), dpre)
                return 0

            lax.fori_loop(0, E // T, step, 0)
            halo = dot_t(total[...].astype(BF), w_ref[D : 2 * D, :]).astype(BF)
            for j in range(M):
                parts[j] = halo[:, j * C : (j + 1) * C]
            for k in range(M):
                outs[k][...] = parts[me ^ k]

        edge_dpre, *halo_grads = call(
            edge_back_kernel,
            "edge_backward",
            me1,
            [edge_grad, edge_pre, send_row, recv_row, in_full, out_full] + second_parts,
            [shape((E, D))] + [shape((NH, C))] * M,
            scratch=[pltpu.VMEM((N, D), BF), pltpu.VMEM((NH, D), F32), pltpu.VMEM((M, NH, C), BF)],
            flops=2 * E * D * (N + D + NH) + 2 * NH * D * D,
        )
        halo_grads = member_trade(halo_grads)

        def local_back_kernel(me_ref, dpre_ref, send_ref, recv_ref, w_ref, first_ref, *refs):
            outs, (sent, got, parts) = refs[:M], refs[M:]
            me = me_ref[0]
            sent[...] = jnp.zeros_like(sent)
            got[...] = jnp.zeros_like(got)

            def step(i, _):
                at = rows_at(i, T)
                sent[...] += dot(hot_columns(send_ref[:, at], N), dpre_ref[at, :])
                got[...] += dot(hot_columns(recv_ref[:, at], N), dpre_ref[at, :])
                return 0

            lax.fori_loop(0, E // T, step, 0)
            sent[...] = dot_t(sent[...].astype(BF), w_ref[D : 2 * D, :]) + dot_t(
                got[...].astype(BF), w_ref[2 * D :, :]
            )
            sent[rows_at(me, R), :] += first_ref[...]
            for j in range(M):
                parts[j] = sent[:, j * C : (j + 1) * C].astype(BF)
            for k in range(M):
                outs[k][...] = parts[me ^ k]

        local_grads = call(
            local_back_kernel,
            "local_backward",
            me1,
            [edge_dpre, send_row, recv_row, in_full, node_first],
            [shape((N, C))] * M,
            scratch=[pltpu.VMEM((N, D), F32), pltpu.VMEM((N, D), F32), pltpu.VMEM((M, N, C), BF)],
            flops=4 * E * D * N + 4 * N * D * D,
        )
        local_grads = member_trade(local_grads)

        def halo_sum_kernel(me_ref, *refs):
            total = refs[0][...].astype(F32)
            for k in range(1, M):
                total += refs[k][...].astype(F32)
            for j in range(n_dom):
                refs[M + j][...] = total[j * H : (j + 1) * H].astype(BF)

        halo_back = call(halo_sum_kernel, "halo_sums", me1, halo_grads, [shape((H, C))] * n_dom)
        halo_back = dom_trade(halo_back)

        def owed_kernel(me_ref, halo_ref, *refs):
            tables, local, back = refs[:M], refs[M : 2 * M], refs[2 * M : 2 * M + n_dom]
            outs = refs[2 * M + n_dom :]
            total = local[0][...].astype(F32)
            for k in range(1, M):
                total += local[k][...].astype(F32)
            rows = stack([back[j][...] for j in range(n_dom)])
            cot = (total + dot(hot_columns(halo_ref[...], N), rows)).astype(BF)
            for k in range(M):
                owed = dot(hot_rows(tables[k][1:2, :], N), cot).astype(BF)
                for j in range(n_dom):
                    outs[j][k * S : (k + 1) * S, :] = owed[j * S : (j + 1) * S]

        owed = call(
            owed_kernel,
            "owed_rows",
            me1,
            [halo_row] + slot_parts + local_grads + halo_back,
            [shape((M * S, C))] * n_dom,
            flops=2 * M * NS * N * C,
        )
        owed = dom_trade(owed)

        def grid_back_kernel(me_ref, slope_ref, *refs):
            tables, back, outs = refs[:M], refs[M : M + n_dom], refs[M + n_dom :]
            for k in range(M):
                rows = stack([back[j][k * S : (k + 1) * S, :] for j in range(n_dom)])
                cot = dot(hot_columns(tables[k][0:1, :], G), rows)
                outs[k][...] = (cot * slope_ref[k]).astype(BF)

        grid_dpre = call(
            grid_back_kernel,
            "grid_backward",
            me1,
            [grid_slope] + slot_parts + owed,
            [shape((G, C))] * M,
            flops=2 * M * G * NS * C,
        )
        grid_dpre = member_trade(grid_dpre)

        def adjoint_kernel(me_ref, enc_ref, *refs):
            cols, out, parts = refs[:M], refs[M], refs[M + 1]
            for k in range(M):
                parts[me_ref[0] ^ k] = cols[k][...]
            out[...] = dot_t(lanes([parts[j] for j in range(M)]), enc_ref[...])

        return call(
            adjoint_kernel,
            "adjoint",
            me1,
            [enc_full] + grid_dpre,
            [shape((G, D), F32)],
            scratch=[pltpu.VMEM((M, G, C), BF)],
            flops=2 * G * D * D,
        )[0]

    return per_device


def solution(mesh):
    return jax.shard_map(
        make_per_device(mesh),
        mesh=mesh,
        in_specs=(
            P(("ens", "dom", "feat", "rep"), None),
            P("dom", None),
            P(("dom", "feat", "rep"), None),
            P(("feat", "rep"), None),
            P(("feat", "rep"), None),
            P(("feat", "rep"), None),
            P(("feat", "rep"), None),
            P(("feat", "rep"), None),
            P(("ens", "dom"), None),
            P(("ens", "dom", "feat", "rep"), None),
            P("dom", None, None),
            P(("dom", "feat", "rep")),
            P(("dom", "feat", "rep")),
            P(("dom", "feat", "rep"), None, None),
            P(("dom", "feat", "rep"), None, None),
        ),
        out_specs=P(("ens", "dom", "feat", "rep"), None),
        check_vma=False,
    )
```

```python
import jax
import jax.numpy as jnp
from jax import lax
from jax.experimental import pallas as pl
from jax.experimental.pallas import tpu as pltpu
from jax.sharding import PartitionSpec as P

BF = jnp.bfloat16
F32 = jnp.float32
SMEM = pl.BlockSpec(memory_space=pltpu.SMEM)
VMEM = pl.BlockSpec(memory_space=pltpu.VMEM)
ANY = pl.BlockSpec(memory_space=pl.ANY)


def dot(a, b):
    return jnp.dot(a, b, preferred_element_type=F32)


def dot_t(a, b):
    return lax.dot_general(a, b, (((1,), (1,)), ((), ())), preferred_element_type=F32)


def silu_slope(values):
    logistic = jax.nn.sigmoid(values)
    return logistic * (1.0 + values * (1.0 - logistic))


def to_column(row):
    return jnp.transpose(jnp.broadcast_to(row, (8, row.shape[1])))[:, :1]


def hot_rows(row, depth):
    length = row.shape[1]
    return (to_column(row) == lax.broadcasted_iota(jnp.int32, (length, depth), 1)).astype(BF)


def hot_columns(row, depth):
    length = row.shape[1]
    return (row == lax.broadcasted_iota(jnp.int32, (depth, length), 0)).astype(BF)


def column_pick(me, depth, cols):
    at = lax.broadcasted_iota(jnp.int32, (depth, cols), 0) - me * cols
    return (at == lax.broadcasted_iota(jnp.int32, (depth, cols), 1)).astype(BF)


def rows_at(index, count):
    return pl.ds(pl.multiple_of(index * count, count), count)


def lanes(parts):
    return parts[0] if len(parts) == 1 else jnp.concatenate(parts, axis=1)


def stack(parts):
    return parts[0] if len(parts) == 1 else jnp.concatenate(parts, axis=0)


def call(body, name, me, ins, outs, scratch=(), flops=0, unread=0):
    size = lambda s: s.size * s.dtype.itemsize
    moved = sum(size(x) for x in ins) + sum(size(x) for x in outs)
    return pl.pallas_call(
        body,
        out_shape=list(outs),
        in_specs=[SMEM] + [VMEM] * (len(ins) - unread) + [ANY] * unread,
        out_specs=[VMEM] * len(outs),
        scratch_shapes=list(scratch),
        compiler_params=pltpu.CompilerParams(vmem_limit_bytes=24 * 2**20),
        cost_estimate=pl.CostEstimate(flops=flops, bytes_accessed=moved, transcendentals=0),
        name=name,
    )(me, *ins)


def shape(dims, dtype=BF):
    return jax.ShapeDtypeStruct(tuple(dims), dtype)


def make_per_device(mesh):
    n_dom, n_feat, n_rep = mesh.shape["dom"], mesh.shape["feat"], mesh.shape["rep"]
    M = n_feat * n_rep

    def member_swap(x, k):
        return lax.ppermute(x, ("feat", "rep"), [(i, i ^ k) for i in range(M)])

    def dom_swap(x, k):
        return lax.ppermute(x, "dom", [(i, i ^ k) for i in range(n_dom)])

    def member_gather(x):
        return [x] + [member_swap(x, k) for k in range(1, M)]

    def member_gather_chips(x):
        parts = [None] * M
        for kf in range(n_feat):
            parts[kf * n_rep] = member_swap(x, kf * n_rep) if kf else x
        for kf in range(n_feat):
            for kr in range(1, n_rep):
                parts[kf * n_rep + kr] = member_swap(parts[kf * n_rep], kr)
        return parts

    def member_trade(parts):
        return [parts[0]] + [member_swap(parts[k], k) for k in range(1, M)]

    def member_sums(parts, me1, name):
        arrived = [parts[0]] + [member_swap(parts[kr], kr) for kr in range(1, n_rep)]

        def add_kernel(me_ref, *refs):
            for kf in range(n_feat):
                total = refs[0][kf].astype(F32)
                for kr in range(1, n_rep):
                    total += refs[kr][kf].astype(F32)
                refs[n_rep + kf][...] = total.astype(BF)

        halves = call(add_kernel, name, me1, arrived, [shape(parts[0].shape[1:])] * n_feat)
        return [halves[0]] + [member_swap(halves[kf], kf * n_rep) for kf in range(1, n_feat)]

    def dom_trade(parts):
        return [parts[0]] + [dom_swap(parts[k], k) for k in range(1, n_dom)]

    def per_device(
        grid_state,
        mesh_base,
        edge_state,
        enc_weight,
        edge_in_weight,
        edge_out_weight,
        node_in_weight,
        node_out_weight,
        node_grad,
        edge_grad,
        halo_rows,
        edge_send,
        edge_recv,
        grid_send,
        grid_recv,
    ):
        D = mesh_base.shape[1]
        N = mesh_base.shape[0]
        E = edge_state.shape[0]
        G = grid_state.shape[0]
        H = halo_rows.shape[2]
        S = grid_send.shape[2]
        NH = n_dom * H
        NS = n_dom * S
        C = D // M
        R = N // M
        T = 256
        rows_enc, rows_in, rows_out, rows_node = (
            enc_weight.shape[0],
            edge_in_weight.shape[0],
            edge_out_weight.shape[0],
            node_in_weight.shape[0],
        )
        me = lax.axis_index(("feat", "rep")).astype(jnp.int32)
        dom = lax.axis_index("dom").astype(jnp.int32)
        me1 = me.reshape(1)

        where = jnp.stack([me, dom])
        recv_row = edge_recv.reshape(1, E)

        def tables_kernel(where_ref, gs_ref, gr_ref, halo_ref, send_ref, slot_out, halo_out, send_out):
            dom = where_ref[1]
            for j in range(n_dom):
                at, to = pl.ds(dom ^ j, 1), slice(j * S, (j + 1) * S)
                slot_out[0:1, to] = gs_ref[0, at, :]
                slot_out[1:2, to] = gr_ref[0, at, :]
                halo_out[:, j * H : (j + 1) * H] = halo_ref[0, at, :]
            sent = send_ref[...]
            away = jnp.maximum(sent - N, 0)
            peer = away // H
            send_out[...] = jnp.where(sent < N, sent, N + (peer ^ dom) * H + (away - peer * H))

        slots, halo_row, send_row = call(
            tables_kernel,
            "tables",
            where,
            [grid_send, grid_recv, halo_rows, edge_send.reshape(1, E)],
            [shape((2, NS), jnp.int32), shape((1, NH), jnp.int32), shape((1, E), jnp.int32)],
        )

        state_parts = member_gather_chips(grid_state)
        enc_parts = member_gather_chips(enc_weight)
        slot_parts = member_gather(slots)

        def relay_kernel(me_ref, weight_ref, arrived_ref, out_ref):
            out_ref[...] = weight_ref[...]

        edge_in_own = call(
            relay_kernel,
            "relay",
            me1,
            [edge_in_weight, state_parts[n_rep]],
            [shape((rows_in, D))],
            unread=1,
        )[0]
        in_parts = member_gather_chips(edge_in_own)

        def hots_kernel(me_ref, send_ref, recv_ref, sl_out, sh_out, r_out, slt_out, sht_out, rt_out):
            for i in range(E // T):
                at = slice(i * T, (i + 1) * T)
                sent, got = send_ref[:, at], recv_ref[:, at]
                sl_out[at, :] = hot_rows(sent, N)
                sh_out[at, :] = hot_rows(sent - N, NH)
                r_out[at, :] = hot_rows(got, N)
                slt_out[:, at] = hot_columns(sent, N)
                sht_out[:, at] = hot_columns(sent - N, NH)
                rt_out[:, at] = hot_columns(got, N)

        sl_hot, sh_hot, r_hot, slt_hot, sht_hot, rt_hot = call(
            hots_kernel,
            "edge_hots",
            me1,
            [send_row, recv_row],
            [shape((E, N)), shape((E, NH)), shape((E, N)), shape((N, E)), shape((NH, E)), shape((N, E))],
        )

        def grid_kernel(me_ref, out_ref, node_in_ref, node_out_ref, *refs):
            states, encs, tables = refs[:M], refs[M : 2 * M], refs[2 * M : 3 * M]
            enc_out, slope_out, rest_out = refs[3 * M : 3 * M + 3]
            outs = refs[3 * M + 3 :]
            me = me_ref[0]
            for k in range(M):
                enc_out[rows_at(me ^ k, rows_enc), :] = encs[k][...]
            enc_cols = dot(enc_out[...], column_pick(me, D, C)).astype(BF)
            for k in range(M):
                pre = dot(states[k][...], enc_cols)
                logistic = jax.nn.sigmoid(pre)
                slope_out[k] = logistic * (1.0 + pre * (1.0 - logistic))
                message = (pre * logistic).astype(BF)
                rows = dot(hot_rows(tables[k][0:1, :], G), message).astype(BF)
                for j in range(n_dom):
                    outs[j][k * S : (k + 1) * S, :] = rows[j * S : (j + 1) * S]
            rest_out[:rows_out, :] = out_ref[...]
            rest_out[rows_out : rows_out + rows_node, :] = node_in_ref[...]
            rest_out[rows_out + rows_node :, :] = node_out_ref[...]

        enc_full, grid_slope, rest, *outgoing = call(
            grid_kernel,
            "grid_messages",
            me1,
            [edge_out_weight, node_in_weight, node_out_weight] + state_parts + enc_parts + slot_parts,
            [shape((D, D)), shape((M, G, C), F32), shape((2 * rows_out + rows_node, D))]
            + [shape((M * S, C))] * n_dom,
            flops=2 * M * G * D * C + 2 * M * NS * G * C,
        )
        incoming = dom_trade(outgoing)
        rest_parts = member_gather_chips(rest)

        def encode_kernel(me_ref, base_ref, halo_ref, *refs):
            tables, arrived = refs[:M], refs[M : M + n_dom]
            state_out, outs = refs[M + n_dom], refs[M + n_dom + 1 :]
            total = dot(base_ref[...], column_pick(me_ref[0], D, C))
            for k in range(M):
                rows = stack([arrived[j][k * S : (k + 1) * S, :] for j in range(n_dom)])
                total += dot(hot_columns(tables[k][1:2, :], N), rows)
            state = total.astype(BF)
            state_out[...] = state
            rows = dot(hot_rows(halo_ref[...], N), state).astype(BF)
            for j in range(n_dom):
                outs[j][...] = rows[j * H : (j + 1) * H]

        state_cols, *halo_out = call(
            encode_kernel,
            "encode",
            me1,
            [mesh_base, halo_row] + slot_parts + incoming,
            [shape((N, C))] + [shape((H, C))] * n_dom,
            flops=2 * M * N * NS * C,
        )
        halo_in = dom_trade(halo_out)
        state_parts2 = member_gather_chips(state_cols)
        halo_cols = jnp.concatenate(halo_in, axis=0)
        halo_parts = member_gather_chips(halo_cols)

        def local_kernel(me_ref, es_ref, send_ref, recv_ref, *refs):
            cols, weights = refs[:M], refs[M : 2 * M]
            pre_out, state_out, w_out, parts = refs[2 * M :]
            me = me_ref[0]
            for k in range(M):
                parts[me ^ k] = cols[k][...]
                w_out[rows_at(me ^ k, rows_in), :] = weights[k][...]
            state_out[...] = lanes([parts[j] for j in range(M)])
            for i in range(E // T):
                at = slice(i * T, (i + 1) * T)
                sent = dot(send_ref[at, :], state_out[...]).astype(BF)
                got = dot(recv_ref[at, :], state_out[...]).astype(BF)
                pre_out[at, :] = (
                    dot(es_ref[at, :], w_out[:D, :])
                    + dot(sent, w_out[D : 2 * D, :])
                    + dot(got, w_out[2 * D :, :])
                )

        local_pre, mesh_state, in_full = call(
            local_kernel,
            "edge_local",
            me1,
            [edge_state, sl_hot, r_hot] + state_parts2 + in_parts,
            [shape((E, D), F32), shape((N, D)), shape((3 * D, D))],
            scratch=[pltpu.VMEM((M, N, C), BF)],
            flops=2 * E * D * (3 * D + 2 * N),
        )

        def node_ahead_kernel(me_ref, state_ref, grad_ref, *refs):
            weights = refs[:M]
            out_full, node_in_full, pre_out, cot_out, node_out_full = refs[M:]
            me = me_ref[0]
            for k in range(M):
                first, second = rows_out, rows_out + rows_node
                out_full[rows_at(me ^ k, rows_out), :] = weights[k][:first, :]
                node_in_full[rows_at(me ^ k, rows_node), :] = weights[k][first:second, :]
                node_out_full[rows_at(me ^ k, rows_out), :] = weights[k][second:, :]
            mine = rows_at(me, R)
            pre_out[...] = dot(state_ref[mine, :], node_in_full[:D, :])
            cot_out[...] = dot_t(grad_ref[mine, :], node_out_full[...])

        out_full, node_in_full, node_pre, node_cot = call(
            node_ahead_kernel,
            "node_ahead",
            me1,
            [mesh_state, node_grad] + rest_parts,
            [shape((D, D)), shape((2 * D, D)), shape((R, D), F32), shape((R, D), F32)],
            scratch=[pltpu.VMEM((D, D), BF)],
            flops=4 * R * D * D,
        )

        def edge_kernel(me_ref, local_ref, es_ref, send_ref, recv_ref, w_ref, out_ref, *refs):
            cols = refs[:M]
            pre_out, outs = refs[M], refs[M + 1 : M + 1 + n_rep]
            parts, halo, new, total = refs[M + 1 + n_rep :]
            me = me_ref[0]
            for k in range(M):
                parts[me ^ k] = cols[k][...]
            halo[...] = lanes([parts[j] for j in range(M)])
            for i in range(E // T):
                at = slice(i * T, (i + 1) * T)
                sent = dot(send_ref[at, :], halo[...]).astype(BF)
                pre = local_ref[at, :] + dot(sent, w_ref[D : 2 * D, :])
                pre_out[at, :] = pre
                hidden = (pre * jax.nn.sigmoid(pre)).astype(BF)
                new[at, :] = (es_ref[at, :].astype(F32) + dot(hidden, out_ref[...])).astype(BF)
            for i in range(N // T):
                at = slice(i * T, (i + 1) * T)
                total[at, :] = dot(recv_ref[at, :], new[...]).astype(BF)
            for kr in range(n_rep):
                for kf in range(n_feat):
                    outs[kr][kf] = total[rows_at(me ^ (kf * n_rep + kr), R), :]

        edge_pre, *sums = call(
            edge_kernel,
            "edge_update",
            me1,
            [local_pre, edge_state, sh_hot, rt_hot, in_full, out_full] + halo_parts,
            [shape((E, D), F32)] + [shape((n_feat, R, D))] * n_rep,
            scratch=[
                pltpu.VMEM((M, NH, C), BF),
                pltpu.VMEM((NH, D), BF),
                pltpu.VMEM((E, D), BF),
                pltpu.VMEM((N, D), BF),
            ],
            flops=2 * E * D * (NH + D + D + N),
        )
        sums = member_sums(sums, me1, "node_sums")

        def node_kernel(me_ref, pre_ref, cot_ref, w_ref, grad_ref, *refs):
            first_out, second_out = refs[n_feat:]
            total = refs[0][...].astype(F32)
            for k in range(1, n_feat):
                total += refs[k][...].astype(F32)
            pre = pre_ref[...] + dot(total.astype(BF), w_ref[D:, :])
            dpre = (cot_ref[...] * silu_slope(pre)).astype(BF)
            second_out[...] = dot_t(dpre, w_ref[D:, :]).astype(BF)
            mine = grad_ref[rows_at(me_ref[0], R), :].astype(F32)
            first_out[...] = mine + dot_t(dpre, w_ref[:D, :])

        node_first, node_second = call(
            node_kernel,
            "node_backward",
            me1,
            [node_pre, node_cot, node_in_full, node_grad] + sums,
            [shape((R, D), F32), shape((R, D))],
            flops=6 * R * D * D,
        )
        second_parts = member_gather_chips(node_second)

        def edge_back_kernel(me_ref, grad_ref, pre_ref, send_ref, recv_ref, w_ref, out_ref, *refs):
            nodes = refs[:M]
            dpre_out, outs = refs[M], refs[M + 1 : M + 1 + n_rep]
            second, parts = refs[M + 1 + n_rep :]
            me = me_ref[0]
            for k in range(M):
                second[rows_at(me ^ k, R), :] = nodes[k][...]
            for i in range(E // T):
                at = slice(i * T, (i + 1) * T)
                got = dot(recv_ref[at, :], second[...])
                cot = (grad_ref[at, :].astype(F32) + got).astype(BF)
                dpre_out[at, :] = (dot_t(cot, out_ref[...]) * silu_slope(pre_ref[at, :])).astype(BF)
            for i in range(NH // T):
                at = slice(i * T, (i + 1) * T)
                sent = dot(send_ref[at, :], dpre_out[...]).astype(BF)
                halo = dot_t(sent, w_ref[D : 2 * D, :]).astype(BF)
                for j in range(M):
                    parts[j, at, :] = halo[:, j * C : (j + 1) * C]
            for kr in range(n_rep):
                for kf in range(n_feat):
                    outs[kr][kf] = parts[me ^ (kf * n_rep + kr)]

        edge_dpre, *halo_grads = call(
            edge_back_kernel,
            "edge_backward",
            me1,
            [edge_grad, edge_pre, sht_hot, r_hot, in_full, out_full] + second_parts,
            [shape((E, D))] + [shape((n_feat, NH, C))] * n_rep,
            scratch=[pltpu.VMEM((N, D), BF), pltpu.VMEM((M, NH, C), BF)],
            flops=2 * E * D * (N + D + NH) + 2 * NH * D * D,
        )
        halo_grads = member_sums(halo_grads, me1, "halo_pairs")

        def local_back_kernel(me_ref, dpre_ref, send_ref, recv_ref, w_ref, first_ref, *refs):
            outs, (total, parts) = refs[:n_rep], refs[n_rep:]
            me = me_ref[0]
            for i in range(N // T):
                at = slice(i * T, (i + 1) * T)
                sent = dot(send_ref[at, :], dpre_ref[...]).astype(BF)
                got = dot(recv_ref[at, :], dpre_ref[...]).astype(BF)
                total[at, :] = dot_t(sent, w_ref[D : 2 * D, :]) + dot_t(got, w_ref[2 * D :, :])
            total[rows_at(me, R), :] += first_ref[...]
            for j in range(M):
                parts[j] = total[:, j * C : (j + 1) * C].astype(BF)
            for kr in range(n_rep):
                for kf in range(n_feat):
                    outs[kr][kf] = parts[me ^ (kf * n_rep + kr)]

        local_grads = call(
            local_back_kernel,
            "local_backward",
            me1,
            [edge_dpre, slt_hot, rt_hot, in_full, node_first],
            [shape((n_feat, N, C))] * n_rep,
            scratch=[pltpu.VMEM((N, D), F32), pltpu.VMEM((M, N, C), BF)],
            flops=4 * E * D * N + 4 * N * D * D,
        )
        local_grads = member_sums(local_grads, me1, "local_pairs")

        def halo_sum_kernel(me_ref, *refs):
            total = refs[0][...].astype(F32)
            for k in range(1, n_feat):
                total += refs[k][...].astype(F32)
            for j in range(n_dom):
                refs[n_feat + j][...] = total[j * H : (j + 1) * H].astype(BF)

        halo_back = call(halo_sum_kernel, "halo_sums", me1, halo_grads, [shape((H, C))] * n_dom)
        halo_back = dom_trade(halo_back)

        def owed_kernel(me_ref, halo_ref, *refs):
            tables, local = refs[:M], refs[M : M + n_feat]
            back, outs = refs[M + n_feat : M + n_feat + n_dom], refs[M + n_feat + n_dom :]
            total = local[0][...].astype(F32)
            for k in range(1, n_feat):
                total += local[k][...].astype(F32)
            rows = stack([back[j][...] for j in range(n_dom)])
            cot = (total + dot(hot_columns(halo_ref[...], N), rows)).astype(BF)
            for k in range(M):
                owed = dot(hot_rows(tables[k][1:2, :], N), cot).astype(BF)
                for j in range(n_dom):
                    outs[j][k * S : (k + 1) * S, :] = owed[j * S : (j + 1) * S]

        owed = call(
            owed_kernel,
            "owed_rows",
            me1,
            [halo_row] + slot_parts + local_grads + halo_back,
            [shape((M * S, C))] * n_dom,
            flops=2 * M * NS * N * C,
        )
        owed = dom_trade(owed)

        def grid_back_kernel(me_ref, slope_ref, *refs):
            tables, back, outs = refs[:M], refs[M : M + n_dom], refs[M + n_dom :]
            for k in range(M):
                rows = stack([back[j][k * S : (k + 1) * S, :] for j in range(n_dom)])
                cot = dot(hot_columns(tables[k][0:1, :], G), rows)
                outs[k][...] = (cot * slope_ref[k]).astype(BF)

        grid_dpre = call(
            grid_back_kernel,
            "grid_backward",
            me1,
            [grid_slope] + slot_parts + owed,
            [shape((G, C))] * M,
            flops=2 * M * G * NS * C,
        )
        grid_dpre = member_trade(grid_dpre)

        def adjoint_kernel(me_ref, enc_ref, *refs):
            cols, out, parts = refs[:M], refs[M], refs[M + 1]
            for k in range(M):
                parts[me_ref[0] ^ k] = cols[k][...]
            out[...] = dot_t(lanes([parts[j] for j in range(M)]), enc_ref[...])

        return call(
            adjoint_kernel,
            "adjoint",
            me1,
            [enc_full] + grid_dpre,
            [shape((G, D), F32)],
            scratch=[pltpu.VMEM((M, G, C), BF)],
            flops=2 * G * D * D,
        )[0]

    return per_device


def solution(mesh):
    return jax.shard_map(
        make_per_device(mesh),
        mesh=mesh,
        in_specs=(
            P(("ens", "dom", "feat", "rep"), None),
            P("dom", None),
            P(("dom", "feat", "rep"), None),
            P(("feat", "rep"), None),
            P(("feat", "rep"), None),
            P(("feat", "rep"), None),
            P(("feat", "rep"), None),
            P(("feat", "rep"), None),
            P(("ens", "dom"), None),
            P(("ens", "dom", "feat", "rep"), None),
            P("dom", None, None),
            P(("dom", "feat", "rep")),
            P(("dom", "feat", "rep")),
            P(("dom", "feat", "rep"), None, None),
            P(("dom", "feat", "rep"), None, None),
        ),
        out_specs=P(("ens", "dom", "feat", "rep"), None),
        check_vma=False,
    )
```

```python
import jax
import jax.numpy as jnp
from jax import lax
from jax.experimental import pallas as pl
from jax.experimental.pallas import tpu as pltpu
from jax.sharding import PartitionSpec as P

BF = jnp.bfloat16
F32 = jnp.float32
SMEM = pl.BlockSpec(memory_space=pltpu.SMEM)
VMEM = pl.BlockSpec(memory_space=pltpu.VMEM)
HBM = pl.BlockSpec(memory_space=pltpu.HBM)


def dot(a, b):
    return jnp.dot(a, b, preferred_element_type=F32)


def dot_t(a, b):
    return lax.dot_general(a, b, (((1,), (1,)), ((), ())), preferred_element_type=F32)


def silu_slope(values):
    logistic = jax.nn.sigmoid(values)
    return logistic * (1.0 + values * (1.0 - logistic))


def to_column(row):
    return jnp.transpose(jnp.broadcast_to(row, (8, row.shape[1])))[:, :1]


def hot_rows(row, depth):
    length = row.shape[1]
    return (to_column(row) == lax.broadcasted_iota(jnp.int32, (length, depth), 1)).astype(BF)


def hot_columns(row, depth):
    length = row.shape[1]
    return (row == lax.broadcasted_iota(jnp.int32, (depth, length), 0)).astype(BF)


def column_pick(me, depth, cols):
    at = lax.broadcasted_iota(jnp.int32, (depth, cols), 0) - me * cols
    return (at == lax.broadcasted_iota(jnp.int32, (depth, cols), 1)).astype(BF)


def rows_at(index, count):
    return pl.ds(pl.multiple_of(index * count, count), count)


def lanes(parts):
    return parts[0] if len(parts) == 1 else jnp.concatenate(parts, axis=1)


def stack(parts):
    return parts[0] if len(parts) == 1 else jnp.concatenate(parts, axis=0)


def call(body, name, me, ins, outs, scratch=(), flops=0, far=()):
    size = lambda s: s.size * s.dtype.itemsize
    moved = sum(size(x) for x in ins) + sum(size(x) for x in outs)
    return pl.pallas_call(
        body,
        out_shape=list(outs),
        in_specs=[SMEM] + [HBM if i in far else VMEM for i in range(len(ins))],
        out_specs=[VMEM] * len(outs),
        scratch_shapes=list(scratch),
        compiler_params=pltpu.CompilerParams(vmem_limit_bytes=24 * 2**20),
        cost_estimate=pl.CostEstimate(flops=flops, bytes_accessed=moved, transcendentals=0),
        name=name,
    )(me, *ins)


def shape(dims, dtype=BF):
    return jax.ShapeDtypeStruct(tuple(dims), dtype)


def make_per_device(mesh):
    n_dom, n_feat, n_rep = mesh.shape["dom"], mesh.shape["feat"], mesh.shape["rep"]
    M = n_feat * n_rep

    def member_swap(x, k):
        return lax.ppermute(x, ("feat", "rep"), [(i, i ^ k) for i in range(M)])

    def dom_swap(x, k):
        return lax.ppermute(x, "dom", [(i, i ^ k) for i in range(n_dom)])

    def member_gather(x):
        return [x] + [member_swap(x, k) for k in range(1, M)]

    def member_gather_chips(x):
        parts = [None] * M
        for kf in range(n_feat):
            parts[kf * n_rep] = member_swap(x, kf * n_rep) if kf else x
        for kf in range(n_feat):
            for kr in range(1, n_rep):
                parts[kf * n_rep + kr] = member_swap(parts[kf * n_rep], kr)
        return parts

    def member_trade(parts):
        return [parts[0]] + [member_swap(parts[k], k) for k in range(1, M)]

    def member_sums(parts, me1, name):
        arrived = [parts[0]] + [member_swap(parts[kr], kr) for kr in range(1, n_rep)]

        def add_kernel(me_ref, *refs):
            for kf in range(n_feat):
                total = refs[0][kf].astype(F32)
                for kr in range(1, n_rep):
                    total += refs[kr][kf].astype(F32)
                refs[n_rep + kf][...] = total.astype(BF)

        halves = call(add_kernel, name, me1, arrived, [shape(parts[0].shape[1:])] * n_feat)
        return [halves[0]] + [member_swap(halves[kf], kf * n_rep) for kf in range(1, n_feat)]

    def dom_trade(parts):
        return [parts[0]] + [dom_swap(parts[k], k) for k in range(1, n_dom)]

    def per_device(
        grid_state,
        mesh_base,
        edge_state,
        enc_weight,
        edge_in_weight,
        edge_out_weight,
        node_in_weight,
        node_out_weight,
        node_grad,
        edge_grad,
        halo_rows,
        edge_send,
        edge_recv,
        grid_send,
        grid_recv,
    ):
        D = mesh_base.shape[1]
        N = mesh_base.shape[0]
        E = edge_state.shape[0]
        G = grid_state.shape[0]
        H = halo_rows.shape[2]
        S = grid_send.shape[2]
        NH = n_dom * H
        NS = n_dom * S
        C = D // M
        R = N // M
        T = 256
        PACK = 16
        assert NS == D
        rows_enc, rows_in, rows_out, rows_node = (
            enc_weight.shape[0],
            edge_in_weight.shape[0],
            edge_out_weight.shape[0],
            node_in_weight.shape[0],
        )
        me = lax.axis_index(("feat", "rep")).astype(jnp.int32)
        dom = lax.axis_index("dom").astype(jnp.int32)
        me1 = me.reshape(1)

        where = jnp.stack([me, dom])
        recv_row = edge_recv.reshape(1, E)

        def tables_kernel(where_ref, enc_ref, gs_ref, gr_ref, halo_ref, send_ref, *refs):
            pack_out, halo_out, send_out, gs, gr, halo, sent, sems = refs
            dom = where_ref[1]
            pairs = [
                (enc_ref, pack_out.at[:rows_enc, :]),
                (gs_ref.at[0], gs),
                (gr_ref.at[0], gr),
                (halo_ref.at[0], halo),
                (send_ref, sent),
            ]
            copies = [pltpu.make_async_copy(a, b, sems.at[i]) for i, (a, b) in enumerate(pairs)]
            for copy in copies:
                copy.start()
            for copy in copies:
                copy.wait()
            order = [pl.ds(dom ^ j, 1) for j in range(n_dom)]
            sends, recvs = lanes([gs[at, :] for at in order]), lanes([gr[at, :] for at in order])
            halo_out[...] = lanes([halo[at, :] for at in order])
            fill = jnp.zeros((PACK - 3, NS), jnp.int32)
            rows = stack([sends, recvs // 2, recvs % 2, fill])
            pack_out[rows_enc:, :] = rows.astype(F32).astype(BF)
            value = sent[...]
            away = jnp.maximum(value - N, 0)
            peer = away // H
            send_out[...] = jnp.where(value < N, value, N + (peer ^ dom) * H + (away - peer * H))

        pack, halo_row, send_row = call(
            tables_kernel,
            "tables",
            where,
            [enc_weight, grid_send, grid_recv, halo_rows, edge_send.reshape(1, E)],
            [shape((rows_enc + PACK, D)), shape((1, NH), jnp.int32), shape((1, E), jnp.int32)],
            scratch=[
                pltpu.VMEM((n_dom, S), jnp.int32),
                pltpu.VMEM((n_dom, S), jnp.int32),
                pltpu.VMEM((n_dom, H), jnp.int32),
                pltpu.VMEM((1, E), jnp.int32),
                pltpu.SemaphoreType.DMA((5,)),
            ],
            far=range(5),
        )

        state_parts = member_gather_chips(grid_state)
        pack_parts = member_gather_chips(pack)
        gather = lambda w: lax.all_gather(w, ("feat", "rep"), axis=0, tiled=True)
        in_full = gather(edge_in_weight)
        out_full = gather(edge_out_weight)
        node_in_full = gather(node_in_weight)
        node_out_full = gather(node_out_weight)

        def hots_kernel(me_ref, send_ref, recv_ref, sl_out, sh_out, r_out, slt_out, sht_out, rt_out):
            for i in range(E // T):
                at = slice(i * T, (i + 1) * T)
                sent, got = send_ref[:, at], recv_ref[:, at]
                sl_out[at, :] = hot_rows(sent, N)
                sh_out[at, :] = hot_rows(sent - N, NH)
                r_out[at, :] = hot_rows(got, N)
                slt_out[:, at] = hot_columns(sent, N)
                sht_out[:, at] = hot_columns(sent - N, NH)
                rt_out[:, at] = hot_columns(got, N)

        sl_hot, sh_hot, r_hot, slt_hot, sht_hot, rt_hot = call(
            hots_kernel,
            "edge_hots",
            me1,
            [send_row, recv_row],
            [shape((E, N)), shape((E, NH)), shape((E, N)), shape((N, E)), shape((NH, E)), shape((N, E))],
        )

        def grid_kernel(me_ref, *refs):
            states, packs = refs[:M], refs[M : 2 * M]
            enc_out, slope_out, table_out = refs[2 * M : 2 * M + 3]
            outs, (own, sem) = refs[2 * M + 3 : 2 * M + 3 + n_dom], refs[2 * M + 3 + n_dom :]
            me = me_ref[0]
            copy = pltpu.make_async_copy(states[0], own, sem)
            copy.start()
            for k in range(M):
                enc_out[rows_at(me ^ k, rows_enc), :] = packs[k][:rows_enc, :]
                rows = packs[k][rows_enc:, :].astype(F32).astype(jnp.int32)
                table_out[k, 0:1, :] = rows[0:1]
                table_out[k, 1:2, :] = 2 * rows[1:2] + rows[2:3]
            enc_cols = dot(enc_out[...], column_pick(me, D, C)).astype(BF)
            for k in list(range(1, M)) + [0]:
                if k == 0:
                    copy.wait()
                pre = dot(states[k][...] if k else own[...], enc_cols)
                logistic = jax.nn.sigmoid(pre)
                slope_out[k] = logistic * (1.0 + pre * (1.0 - logistic))
                message = (pre * logistic).astype(BF)
                rows = dot(hot_rows(table_out[k, 0:1, :], G), message).astype(BF)
                for j in range(n_dom):
                    outs[j][k * S : (k + 1) * S, :] = rows[j * S : (j + 1) * S]

        enc_full, grid_slope, slots, *outgoing = call(
            grid_kernel,
            "grid_messages",
            me1,
            state_parts + pack_parts,
            [shape((D, D)), shape((M, G, C), F32), shape((M, 2, NS), jnp.int32)]
            + [shape((M * S, C))] * n_dom,
            scratch=[pltpu.VMEM((G, D), BF), pltpu.SemaphoreType.DMA(())],
            flops=2 * M * G * D * C + 2 * M * NS * G * C,
            far=(0,),
        )
        incoming = dom_trade(outgoing)

        def encode_kernel(me_ref, base_ref, halo_ref, table_ref, *refs):
            arrived, state_out, outs = refs[:n_dom], refs[n_dom], refs[n_dom + 1 :]
            total = dot(base_ref[...], column_pick(me_ref[0], D, C))
            for k in range(M):
                rows = stack([arrived[j][k * S : (k + 1) * S, :] for j in range(n_dom)])
                total += dot(hot_columns(table_ref[k, 1:2, :], N), rows)
            state = total.astype(BF)
            state_out[...] = state
            rows = dot(hot_rows(halo_ref[...], N), state).astype(BF)
            for j in range(n_dom):
                outs[j][...] = rows[j * H : (j + 1) * H]

        state_cols, *halo_out = call(
            encode_kernel,
            "encode",
            me1,
            [mesh_base, halo_row, slots] + incoming,
            [shape((N, C))] + [shape((H, C))] * n_dom,
            flops=2 * M * N * NS * C,
        )
        halo_in = dom_trade(halo_out)
        state_parts2 = member_gather_chips(state_cols)
        halo_cols = jnp.concatenate(halo_in, axis=0)
        halo_parts = member_gather_chips(halo_cols)

        def local_kernel(me_ref, es_ref, send_ref, recv_ref, w_ref, *refs):
            cols, (pre_out, state_out, parts) = refs[:M], refs[M:]
            me = me_ref[0]
            for k in range(M):
                parts[me ^ k] = cols[k][...]
            state_out[...] = lanes([parts[j] for j in range(M)])
            for i in range(E // T):
                at = slice(i * T, (i + 1) * T)
                sent = dot(send_ref[at, :], state_out[...]).astype(BF)
                got = dot(recv_ref[at, :], state_out[...]).astype(BF)
                pre_out[at, :] = (
                    dot(es_ref[at, :], w_ref[:D, :])
                    + dot(sent, w_ref[D : 2 * D, :])
                    + dot(got, w_ref[2 * D :, :])
                )

        local_pre, mesh_state = call(
            local_kernel,
            "edge_local",
            me1,
            [edge_state, sl_hot, r_hot, in_full] + state_parts2,
            [shape((E, D), F32), shape((N, D))],
            scratch=[pltpu.VMEM((M, N, C), BF)],
            flops=2 * E * D * (3 * D + 2 * N),
        )

        def node_ahead_kernel(me_ref, state_ref, grad_ref, in_ref, out_ref, pre_out, cot_out):
            mine = rows_at(me_ref[0], R)
            pre_out[...] = dot(state_ref[mine, :], in_ref[:D, :])
            cot_out[...] = dot_t(grad_ref[mine, :], out_ref[...])

        node_pre, node_cot = call(
            node_ahead_kernel,
            "node_ahead",
            me1,
            [mesh_state, node_grad, node_in_full, node_out_full],
            [shape((R, D), F32), shape((R, D), F32)],
            flops=4 * R * D * D,
        )

        def edge_kernel(me_ref, local_ref, es_ref, send_ref, recv_ref, w_ref, out_ref, *refs):
            cols = refs[:M]
            pre_out, outs = refs[M], refs[M + 1 : M + 1 + n_rep]
            parts, halo, new, total = refs[M + 1 + n_rep :]
            me = me_ref[0]
            for k in range(M):
                parts[me ^ k] = cols[k][...]
            halo[...] = lanes([parts[j] for j in range(M)])
            for i in range(E // T):
                at = slice(i * T, (i + 1) * T)
                sent = dot(send_ref[at, :], halo[...]).astype(BF)
                pre = local_ref[at, :] + dot(sent, w_ref[D : 2 * D, :])
                pre_out[at, :] = pre
                hidden = (pre * jax.nn.sigmoid(pre)).astype(BF)
                new[at, :] = (es_ref[at, :].astype(F32) + dot(hidden, out_ref[...])).astype(BF)
            for i in range(N // T):
                at = slice(i * T, (i + 1) * T)
                total[at, :] = dot(recv_ref[at, :], new[...]).astype(BF)
            for kr in range(n_rep):
                for kf in range(n_feat):
                    outs[kr][kf] = total[rows_at(me ^ (kf * n_rep + kr), R), :]

        edge_pre, *sums = call(
            edge_kernel,
            "edge_update",
            me1,
            [local_pre, edge_state, sh_hot, rt_hot, in_full, out_full] + halo_parts,
            [shape((E, D), F32)] + [shape((n_feat, R, D))] * n_rep,
            scratch=[
                pltpu.VMEM((M, NH, C), BF),
                pltpu.VMEM((NH, D), BF),
                pltpu.VMEM((E, D), BF),
                pltpu.VMEM((N, D), BF),
            ],
            flops=2 * E * D * (NH + D + D + N),
        )
        sums = member_sums(sums, me1, "node_sums")

        def node_kernel(me_ref, pre_ref, cot_ref, w_ref, grad_ref, *refs):
            first_out, second_out = refs[n_feat:]
            total = refs[0][...].astype(F32)
            for k in range(1, n_feat):
                total += refs[k][...].astype(F32)
            pre = pre_ref[...] + dot(total.astype(BF), w_ref[D:, :])
            dpre = (cot_ref[...] * silu_slope(pre)).astype(BF)
            second_out[...] = dot_t(dpre, w_ref[D:, :]).astype(BF)
            mine = grad_ref[rows_at(me_ref[0], R), :].astype(F32)
            first_out[...] = mine + dot_t(dpre, w_ref[:D, :])

        node_first, node_second = call(
            node_kernel,
            "node_backward",
            me1,
            [node_pre, node_cot, node_in_full, node_grad] + sums,
            [shape((R, D), F32), shape((R, D))],
            flops=6 * R * D * D,
        )
        second_parts = member_gather_chips(node_second)

        def edge_back_kernel(me_ref, grad_ref, pre_ref, send_ref, recv_ref, w_ref, out_ref, *refs):
            nodes = refs[:M]
            dpre_out, outs = refs[M], refs[M + 1 : M + 1 + n_rep]
            second, parts = refs[M + 1 + n_rep :]
            me = me_ref[0]
            for k in range(M):
                second[rows_at(me ^ k, R), :] = nodes[k][...]
            for i in range(E // T):
                at = slice(i * T, (i + 1) * T)
                got = dot(recv_ref[at, :], second[...])
                cot = (grad_ref[at, :].astype(F32) + got).astype(BF)
                dpre_out[at, :] = (dot_t(cot, out_ref[...]) * silu_slope(pre_ref[at, :])).astype(BF)
            for i in range(NH // T):
                at = slice(i * T, (i + 1) * T)
                sent = dot(send_ref[at, :], dpre_out[...]).astype(BF)
                halo = dot_t(sent, w_ref[D : 2 * D, :]).astype(BF)
                for j in range(M):
                    parts[j, at, :] = halo[:, j * C : (j + 1) * C]
            for kr in range(n_rep):
                for kf in range(n_feat):
                    outs[kr][kf] = parts[me ^ (kf * n_rep + kr)]

        edge_dpre, *halo_grads = call(
            edge_back_kernel,
            "edge_backward",
            me1,
            [edge_grad, edge_pre, sht_hot, r_hot, in_full, out_full] + second_parts,
            [shape((E, D))] + [shape((n_feat, NH, C))] * n_rep,
            scratch=[pltpu.VMEM((N, D), BF), pltpu.VMEM((M, NH, C), BF)],
            flops=2 * E * D * (N + D + NH) + 2 * NH * D * D,
        )
        halo_grads = member_sums(halo_grads, me1, "halo_pairs")

        def local_back_kernel(me_ref, dpre_ref, send_ref, recv_ref, w_ref, first_ref, *refs):
            outs, (total, parts) = refs[:n_rep], refs[n_rep:]
            me = me_ref[0]
            for i in range(N // T):
                at = slice(i * T, (i + 1) * T)
                sent = dot(send_ref[at, :], dpre_ref[...]).astype(BF)
                got = dot(recv_ref[at, :], dpre_ref[...]).astype(BF)
                total[at, :] = dot_t(sent, w_ref[D : 2 * D, :]) + dot_t(got, w_ref[2 * D :, :])
            total[rows_at(me, R), :] += first_ref[...]
            for j in range(M):
                parts[j] = total[:, j * C : (j + 1) * C].astype(BF)
            for kr in range(n_rep):
                for kf in range(n_feat):
                    outs[kr][kf] = parts[me ^ (kf * n_rep + kr)]

        local_grads = call(
            local_back_kernel,
            "local_backward",
            me1,
            [edge_dpre, slt_hot, rt_hot, in_full, node_first],
            [shape((n_feat, N, C))] * n_rep,
            scratch=[pltpu.VMEM((N, D), F32), pltpu.VMEM((M, N, C), BF)],
            flops=4 * E * D * N + 4 * N * D * D,
        )
        local_grads = member_sums(local_grads, me1, "local_pairs")

        def halo_sum_kernel(me_ref, *refs):
            total = refs[0][...].astype(F32)
            for k in range(1, n_feat):
                total += refs[k][...].astype(F32)
            for j in range(n_dom):
                refs[n_feat + j][...] = total[j * H : (j + 1) * H].astype(BF)

        halo_back = call(halo_sum_kernel, "halo_sums", me1, halo_grads, [shape((H, C))] * n_dom)
        halo_back = dom_trade(halo_back)

        def owed_kernel(me_ref, halo_ref, table_ref, *refs):
            local, back = refs[:n_feat], refs[n_feat : n_feat + n_dom]
            outs = refs[n_feat + n_dom :]
            total = local[0][...].astype(F32)
            for k in range(1, n_feat):
                total += local[k][...].astype(F32)
            rows = stack([back[j][...] for j in range(n_dom)])
            cot = (total + dot(hot_columns(halo_ref[...], N), rows)).astype(BF)
            for k in range(M):
                owed = dot(hot_rows(table_ref[k, 1:2, :], N), cot).astype(BF)
                for j in range(n_dom):
                    outs[j][k * S : (k + 1) * S, :] = owed[j * S : (j + 1) * S]

        owed = call(
            owed_kernel,
            "owed_rows",
            me1,
            [halo_row, slots] + local_grads + halo_back,
            [shape((M * S, C))] * n_dom,
            flops=2 * M * NS * N * C,
        )
        owed = dom_trade(owed)

        def grid_back_kernel(me_ref, slope_ref, table_ref, *refs):
            back, outs = refs[:n_dom], refs[n_dom:]
            for k in range(M):
                rows = stack([back[j][k * S : (k + 1) * S, :] for j in range(n_dom)])
                cot = dot(hot_columns(table_ref[k, 0:1, :], G), rows)
                outs[k][...] = (cot * slope_ref[k]).astype(BF)

        grid_dpre = call(
            grid_back_kernel,
            "grid_backward",
            me1,
            [grid_slope, slots] + owed,
            [shape((G, C))] * M,
            flops=2 * M * G * NS * C,
        )
        grid_dpre = member_trade(grid_dpre)

        def adjoint_kernel(me_ref, enc_ref, *refs):
            cols, out, parts = refs[:M], refs[M], refs[M + 1]
            for k in range(M):
                parts[me_ref[0] ^ k] = cols[k][...]
            out[...] = dot_t(lanes([parts[j] for j in range(M)]), enc_ref[...])

        return call(
            adjoint_kernel,
            "adjoint",
            me1,
            [enc_full] + grid_dpre,
            [shape((G, D), F32)],
            scratch=[pltpu.VMEM((M, G, C), BF)],
            flops=2 * G * D * D,
        )[0]

    return per_device


def solution(mesh):
    return jax.shard_map(
        make_per_device(mesh),
        mesh=mesh,
        in_specs=(
            P(("ens", "dom", "feat", "rep"), None),
            P("dom", None),
            P(("dom", "feat", "rep"), None),
            P(("feat", "rep"), None),
            P(("feat", "rep"), None),
            P(("feat", "rep"), None),
            P(("feat", "rep"), None),
            P(("feat", "rep"), None),
            P(("ens", "dom"), None),
            P(("ens", "dom", "feat", "rep"), None),
            P("dom", None, None),
            P(("dom", "feat", "rep")),
            P(("dom", "feat", "rep")),
            P(("dom", "feat", "rep"), None, None),
            P(("dom", "feat", "rep"), None, None),
        ),
        out_specs=P(("ens", "dom", "feat", "rep"), None),
        check_vma=False,
    )
```

```python
import jax
import jax.numpy as jnp
from jax import lax
from jax.experimental import pallas as pl
from jax.experimental.pallas import tpu as pltpu
from jax.sharding import PartitionSpec as P

BF = jnp.bfloat16
F32 = jnp.float32
SMEM = pl.BlockSpec(memory_space=pltpu.SMEM)
VMEM = pl.BlockSpec(memory_space=pltpu.VMEM)
HBM = pl.BlockSpec(memory_space=pltpu.HBM)
ANY = pl.BlockSpec(memory_space=pl.ANY)


def dot(a, b):
    return jnp.dot(a, b, preferred_element_type=F32)


def dot_t(a, b):
    return lax.dot_general(a, b, (((1,), (1,)), ((), ())), preferred_element_type=F32)


def silu_slope(values):
    logistic = jax.nn.sigmoid(values)
    return logistic * (1.0 + values * (1.0 - logistic))


def to_column(row):
    return jnp.transpose(jnp.broadcast_to(row, (8, row.shape[1])))[:, :1]


def hot_rows(row, depth):
    length = row.shape[1]
    return (to_column(row) == lax.broadcasted_iota(jnp.int32, (length, depth), 1)).astype(BF)


def hot_columns(row, depth):
    length = row.shape[1]
    return (row == lax.broadcasted_iota(jnp.int32, (depth, length), 0)).astype(BF)


def column_pick(me, depth, cols):
    at = lax.broadcasted_iota(jnp.int32, (depth, cols), 0) - me * cols
    return (at == lax.broadcasted_iota(jnp.int32, (depth, cols), 1)).astype(BF)


def rows_at(index, count):
    return pl.ds(pl.multiple_of(index * count, count), count)


def lanes(parts):
    return parts[0] if len(parts) == 1 else jnp.concatenate(parts, axis=1)


def stack(parts):
    return parts[0] if len(parts) == 1 else jnp.concatenate(parts, axis=0)


def call(body, name, me, ins, outs, scratch=(), flops=0, far=(), unread=()):
    size = lambda s: s.size * s.dtype.itemsize
    moved = sum(size(x) for x in ins) + sum(size(x) for x in outs)
    return pl.pallas_call(
        body,
        out_shape=list(outs),
        in_specs=[SMEM] + [HBM if i in far else ANY if i in unread else VMEM for i in range(len(ins))],
        out_specs=[VMEM] * len(outs),
        scratch_shapes=list(scratch),
        compiler_params=pltpu.CompilerParams(vmem_limit_bytes=24 * 2**20),
        cost_estimate=pl.CostEstimate(flops=flops, bytes_accessed=moved, transcendentals=0),
        name=name,
    )(me, *[pltpu.with_memory_space_constraint(x, pltpu.HBM) if i in far else x for i, x in enumerate(ins)])


def shape(dims, dtype=BF):
    return jax.ShapeDtypeStruct(tuple(dims), dtype)


def make_per_device(mesh):
    n_dom, n_feat, n_rep = mesh.shape["dom"], mesh.shape["feat"], mesh.shape["rep"]
    M = n_feat * n_rep

    def member_swap(x, k):
        return lax.ppermute(x, ("feat", "rep"), [(i, i ^ k) for i in range(M)])

    def dom_swap(x, k):
        return lax.ppermute(x, "dom", [(i, i ^ k) for i in range(n_dom)])

    def member_gather(x):
        return [x] + [member_swap(x, k) for k in range(1, M)]

    def member_gather_chips(x):
        parts = [None] * M
        for kf in range(n_feat):
            parts[kf * n_rep] = member_swap(x, kf * n_rep) if kf else x
        for kf in range(n_feat):
            for kr in range(1, n_rep):
                parts[kf * n_rep + kr] = member_swap(parts[kf * n_rep], kr)
        return parts

    def member_trade(parts):
        return [parts[0]] + [member_swap(parts[k], k) for k in range(1, M)]

    def member_sums(parts, me1, name):
        arrived = [parts[0]] + [member_swap(parts[kr], kr) for kr in range(1, n_rep)]

        def add_kernel(me_ref, *refs):
            for kf in range(n_feat):
                total = refs[0][kf].astype(F32)
                for kr in range(1, n_rep):
                    total += refs[kr][kf].astype(F32)
                refs[n_rep + kf][...] = total.astype(BF)

        halves = call(add_kernel, name, me1, arrived, [shape(parts[0].shape[1:])] * n_feat)
        return [halves[0]] + [member_swap(halves[kf], kf * n_rep) for kf in range(1, n_feat)]

    def dom_trade(parts):
        return [parts[0]] + [dom_swap(parts[k], k) for k in range(1, n_dom)]

    def per_device(
        grid_state,
        mesh_base,
        edge_state,
        enc_weight,
        edge_in_weight,
        edge_out_weight,
        node_in_weight,
        node_out_weight,
        node_grad,
        edge_grad,
        halo_rows,
        edge_send,
        edge_recv,
        grid_send,
        grid_recv,
    ):
        D = mesh_base.shape[1]
        N = mesh_base.shape[0]
        E = edge_state.shape[0]
        G = grid_state.shape[0]
        H = halo_rows.shape[2]
        S = grid_send.shape[2]
        NH = n_dom * H
        NS = n_dom * S
        C = D // M
        R = N // M
        T = 256
        PACK = 16
        assert NS == D
        rows_enc, rows_in, rows_out, rows_node = (
            enc_weight.shape[0],
            edge_in_weight.shape[0],
            edge_out_weight.shape[0],
            node_in_weight.shape[0],
        )
        me = lax.axis_index(("feat", "rep")).astype(jnp.int32)
        dom = lax.axis_index("dom").astype(jnp.int32)
        me1 = me.reshape(1)

        where = jnp.stack([me, dom])
        recv_row = edge_recv.reshape(1, E)

        def tables_kernel(where_ref, enc_ref, gs_ref, gr_ref, halo_ref, send_ref, *refs):
            pack_out, halo_out, send_out, gs, gr, halo, sent, sems = refs
            dom = where_ref[1]
            pairs = [
                (enc_ref, pack_out.at[:rows_enc, :]),
                (gs_ref.at[0], gs),
                (gr_ref.at[0], gr),
                (halo_ref.at[0], halo),
                (send_ref, sent),
            ]
            copies = [pltpu.make_async_copy(a, b, sems.at[i]) for i, (a, b) in enumerate(pairs)]
            for copy in copies:
                copy.start()
            for copy in copies:
                copy.wait()
            order = [pl.ds(dom ^ j, 1) for j in range(n_dom)]
            sends, recvs = lanes([gs[at, :] for at in order]), lanes([gr[at, :] for at in order])
            halo_out[...] = lanes([halo[at, :] for at in order])
            fill = jnp.zeros((PACK - 3, NS), jnp.int32)
            rows = stack([sends, recvs // 2, recvs % 2, fill])
            pack_out[rows_enc:, :] = rows.astype(F32).astype(BF)
            value = sent[...]
            away = jnp.maximum(value - N, 0)
            peer = away // H
            send_out[...] = jnp.where(value < N, value, N + (peer ^ dom) * H + (away - peer * H))

        pack, halo_row, send_row = call(
            tables_kernel,
            "tables",
            where,
            [enc_weight, grid_send, grid_recv, halo_rows, edge_send.reshape(1, E)],
            [shape((rows_enc + PACK, D)), shape((1, NH), jnp.int32), shape((1, E), jnp.int32)],
            scratch=[
                pltpu.VMEM((n_dom, S), jnp.int32),
                pltpu.VMEM((n_dom, S), jnp.int32),
                pltpu.VMEM((n_dom, H), jnp.int32),
                pltpu.VMEM((1, E), jnp.int32),
                pltpu.SemaphoreType.DMA((5,)),
            ],
            far=range(5),
        )

        state_parts = member_gather_chips(grid_state)
        pack_parts = member_gather_chips(pack)

        def relay(name, weights, arrived):
            rows = [w.shape[0] for w in weights]
            starts = [sum(rows[:i]) for i in range(len(rows))]

            def relay_kernel(me_ref, *refs):
                out, sems = refs[-2:]
                copies = [
                    pltpu.make_async_copy(refs[i], out.at[at : at + n, :], sems.at[i])
                    for i, (at, n) in enumerate(zip(starts, rows))
                ]
                for copy in copies:
                    copy.start()
                for copy in copies:
                    copy.wait()

            return call(
                relay_kernel,
                name,
                me1,
                list(weights) + [arrived],
                [shape((sum(rows), D))],
                scratch=[pltpu.SemaphoreType.DMA((len(rows),))],
                far=range(len(rows)),
                unread=(len(rows),),
            )[0]

        edge_in_own = relay("relay_edge", [edge_in_weight], state_parts[n_rep])
        in_parts = member_gather_chips(edge_in_own)

        def hots_kernel(me_ref, send_ref, recv_ref, sl_out, sh_out, r_out, slt_out, sht_out, rt_out):
            for i in range(E // T):
                at = slice(i * T, (i + 1) * T)
                sent, got = send_ref[:, at], recv_ref[:, at]
                sl_out[at, :] = hot_rows(sent, N)
                sh_out[at, :] = hot_rows(sent - N, NH)
                r_out[at, :] = hot_rows(got, N)
                slt_out[:, at] = hot_columns(sent, N)
                sht_out[:, at] = hot_columns(sent - N, NH)
                rt_out[:, at] = hot_columns(got, N)

        sl_hot, sh_hot, r_hot, slt_hot, sht_hot, rt_hot = call(
            hots_kernel,
            "edge_hots",
            me1,
            [send_row, recv_row],
            [shape((E, N)), shape((E, NH)), shape((E, N)), shape((N, E)), shape((NH, E)), shape((N, E))],
        )

        def grid_kernel(me_ref, *refs):
            states, packs = refs[:M], refs[M : 2 * M]
            enc_out, slope_out, table_out = refs[2 * M + 1 : 2 * M + 4]
            outs, (own, sem) = refs[2 * M + 4 : 2 * M + 4 + n_dom], refs[2 * M + 4 + n_dom :]
            me = me_ref[0]
            copy = pltpu.make_async_copy(states[0], own, sem)
            copy.start()
            for k in range(M):
                enc_out[rows_at(me ^ k, rows_enc), :] = packs[k][:rows_enc, :]
                rows = packs[k][rows_enc:, :].astype(F32).astype(jnp.int32)
                table_out[k, 0:1, :] = rows[0:1]
                table_out[k, 1:2, :] = 2 * rows[1:2] + rows[2:3]
            enc_cols = dot(enc_out[...], column_pick(me, D, C)).astype(BF)
            for k in list(range(1, M)) + [0]:
                if k == 0:
                    copy.wait()
                pre = dot(states[k][...] if k else own[...], enc_cols)
                logistic = jax.nn.sigmoid(pre)
                slope_out[k] = logistic * (1.0 + pre * (1.0 - logistic))
                message = (pre * logistic).astype(BF)
                rows = dot(hot_rows(table_out[k, 0:1, :], G), message).astype(BF)
                for j in range(n_dom):
                    outs[j][k * S : (k + 1) * S, :] = rows[j * S : (j + 1) * S]

        enc_full, grid_slope, slots, *outgoing = call(
            grid_kernel,
            "grid_messages",
            me1,
            state_parts + pack_parts + [edge_in_own],
            [shape((D, D)), shape((M, G, C), F32), shape((M, 2, NS), jnp.int32)]
            + [shape((M * S, C))] * n_dom,
            scratch=[pltpu.VMEM((G, D), BF), pltpu.SemaphoreType.DMA(())],
            flops=2 * M * G * D * C + 2 * M * NS * G * C,
            far=(0,),
            unread=(2 * M,),
        )
        incoming = dom_trade(outgoing)
        rest = relay("relay_rest", [edge_out_weight, node_in_weight, node_out_weight], incoming[1])
        rest_parts = member_gather_chips(rest)

        def encode_kernel(me_ref, base_ref, halo_ref, table_ref, *refs):
            arrived, state_out, outs = refs[:n_dom], refs[n_dom], refs[n_dom + 1 :]
            total = dot(base_ref[...], column_pick(me_ref[0], D, C))
            for k in range(M):
                rows = stack([arrived[j][k * S : (k + 1) * S, :] for j in range(n_dom)])
                total += dot(hot_columns(table_ref[k, 1:2, :], N), rows)
            state = total.astype(BF)
            state_out[...] = state
            rows = dot(hot_rows(halo_ref[...], N), state).astype(BF)
            for j in range(n_dom):
                outs[j][...] = rows[j * H : (j + 1) * H]

        state_cols, *halo_out = call(
            encode_kernel,
            "encode",
            me1,
            [mesh_base, halo_row, slots] + incoming,
            [shape((N, C))] + [shape((H, C))] * n_dom,
            flops=2 * M * N * NS * C,
        )
        halo_in = dom_trade(halo_out)
        state_parts2 = member_gather_chips(state_cols)
        halo_cols = jnp.concatenate(halo_in, axis=0)
        halo_parts = member_gather_chips(halo_cols)

        def local_kernel(me_ref, es_ref, send_ref, recv_ref, *refs):
            cols, weights = refs[:M], refs[M : 2 * M]
            pre_out, state_out, w_out, parts = refs[2 * M :]
            me = me_ref[0]
            for k in range(M):
                parts[me ^ k] = cols[k][...]
                w_out[rows_at(me ^ k, rows_in), :] = weights[k][...]
            state_out[...] = lanes([parts[j] for j in range(M)])
            for i in range(E // T):
                at = slice(i * T, (i + 1) * T)
                sent = dot(send_ref[at, :], state_out[...]).astype(BF)
                got = dot(recv_ref[at, :], state_out[...]).astype(BF)
                pre_out[at, :] = (
                    dot(es_ref[at, :], w_out[:D, :])
                    + dot(sent, w_out[D : 2 * D, :])
                    + dot(got, w_out[2 * D :, :])
                )

        local_pre, mesh_state, in_full = call(
            local_kernel,
            "edge_local",
            me1,
            [edge_state, sl_hot, r_hot] + state_parts2 + in_parts,
            [shape((E, D), F32), shape((N, D)), shape((3 * D, D))],
            scratch=[pltpu.VMEM((M, N, C), BF)],
            flops=2 * E * D * (3 * D + 2 * N),
        )

        def node_ahead_kernel(me_ref, state_ref, grad_ref, *refs):
            weights = refs[:M]
            out_full, node_in_full, pre_out, cot_out, node_out_full = refs[M:]
            me = me_ref[0]
            for k in range(M):
                first, second = rows_out, rows_out + rows_node
                out_full[rows_at(me ^ k, rows_out), :] = weights[k][:first, :]
                node_in_full[rows_at(me ^ k, rows_node), :] = weights[k][first:second, :]
                node_out_full[rows_at(me ^ k, rows_out), :] = weights[k][second:, :]
            mine = rows_at(me, R)
            pre_out[...] = dot(state_ref[mine, :], node_in_full[:D, :])
            cot_out[...] = dot_t(grad_ref[mine, :], node_out_full[...])

        out_full, node_in_full, node_pre, node_cot = call(
            node_ahead_kernel,
            "node_ahead",
            me1,
            [mesh_state, node_grad] + rest_parts,
            [shape((D, D)), shape((2 * D, D)), shape((R, D), F32), shape((R, D), F32)],
            scratch=[pltpu.VMEM((D, D), BF)],
            flops=4 * R * D * D,
        )

        def edge_kernel(me_ref, local_ref, es_ref, send_ref, recv_ref, w_ref, out_ref, *refs):
            cols = refs[:M]
            pre_out, outs = refs[M], refs[M + 1 : M + 1 + n_rep]
            parts, halo, new, total = refs[M + 1 + n_rep :]
            me = me_ref[0]
            for k in range(M):
                parts[me ^ k] = cols[k][...]
            halo[...] = lanes([parts[j] for j in range(M)])
            for i in range(E // T):
                at = slice(i * T, (i + 1) * T)
                sent = dot(send_ref[at, :], halo[...]).astype(BF)
                pre = local_ref[at, :] + dot(sent, w_ref[D : 2 * D, :])
                pre_out[at, :] = pre
                hidden = (pre * jax.nn.sigmoid(pre)).astype(BF)
                new[at, :] = (es_ref[at, :].astype(F32) + dot(hidden, out_ref[...])).astype(BF)
            for i in range(N // T):
                at = slice(i * T, (i + 1) * T)
                total[at, :] = dot(recv_ref[at, :], new[...]).astype(BF)
            for kr in range(n_rep):
                for kf in range(n_feat):
                    outs[kr][kf] = total[rows_at(me ^ (kf * n_rep + kr), R), :]

        edge_pre, *sums = call(
            edge_kernel,
            "edge_update",
            me1,
            [local_pre, edge_state, sh_hot, rt_hot, in_full, out_full] + halo_parts,
            [shape((E, D), F32)] + [shape((n_feat, R, D))] * n_rep,
            scratch=[
                pltpu.VMEM((M, NH, C), BF),
                pltpu.VMEM((NH, D), BF),
                pltpu.VMEM((E, D), BF),
                pltpu.VMEM((N, D), BF),
            ],
            flops=2 * E * D * (NH + D + D + N),
        )
        sums = member_sums(sums, me1, "node_sums")

        def node_kernel(me_ref, pre_ref, cot_ref, w_ref, grad_ref, *refs):
            first_out, second_out = refs[n_feat:]
            total = refs[0][...].astype(F32)
            for k in range(1, n_feat):
                total += refs[k][...].astype(F32)
            pre = pre_ref[...] + dot(total.astype(BF), w_ref[D:, :])
            dpre = (cot_ref[...] * silu_slope(pre)).astype(BF)
            second_out[...] = dot_t(dpre, w_ref[D:, :]).astype(BF)
            mine = grad_ref[rows_at(me_ref[0], R), :].astype(F32)
            first_out[...] = mine + dot_t(dpre, w_ref[:D, :])

        node_first, node_second = call(
            node_kernel,
            "node_backward",
            me1,
            [node_pre, node_cot, node_in_full, node_grad] + sums,
            [shape((R, D), F32), shape((R, D))],
            flops=6 * R * D * D,
        )
        second_parts = member_gather_chips(node_second)

        def edge_back_kernel(me_ref, grad_ref, pre_ref, send_ref, recv_ref, w_ref, out_ref, *refs):
            nodes = refs[:M]
            dpre_out, outs = refs[M], refs[M + 1 : M + 1 + n_rep]
            second, parts = refs[M + 1 + n_rep :]
            me = me_ref[0]
            for k in range(M):
                second[rows_at(me ^ k, R), :] = nodes[k][...]
            for i in range(E // T):
                at = slice(i * T, (i + 1) * T)
                got = dot(recv_ref[at, :], second[...])
                cot = (grad_ref[at, :].astype(F32) + got).astype(BF)
                dpre_out[at, :] = (dot_t(cot, out_ref[...]) * silu_slope(pre_ref[at, :])).astype(BF)
            for i in range(NH // T):
                at = slice(i * T, (i + 1) * T)
                sent = dot(send_ref[at, :], dpre_out[...]).astype(BF)
                halo = dot_t(sent, w_ref[D : 2 * D, :]).astype(BF)
                for j in range(M):
                    parts[j, at, :] = halo[:, j * C : (j + 1) * C]
            for kr in range(n_rep):
                for kf in range(n_feat):
                    outs[kr][kf] = parts[me ^ (kf * n_rep + kr)]

        edge_dpre, *halo_grads = call(
            edge_back_kernel,
            "edge_backward",
            me1,
            [edge_grad, edge_pre, sht_hot, r_hot, in_full, out_full] + second_parts,
            [shape((E, D))] + [shape((n_feat, NH, C))] * n_rep,
            scratch=[pltpu.VMEM((N, D), BF), pltpu.VMEM((M, NH, C), BF)],
            flops=2 * E * D * (N + D + NH) + 2 * NH * D * D,
        )
        halo_grads = member_sums(halo_grads, me1, "halo_pairs")

        def local_back_kernel(me_ref, dpre_ref, send_ref, recv_ref, w_ref, first_ref, *refs):
            outs, (total, parts) = refs[:n_rep], refs[n_rep:]
            me = me_ref[0]
            for i in range(N // T):
                at = slice(i * T, (i + 1) * T)
                sent = dot(send_ref[at, :], dpre_ref[...]).astype(BF)
                got = dot(recv_ref[at, :], dpre_ref[...]).astype(BF)
                total[at, :] = dot_t(sent, w_ref[D : 2 * D, :]) + dot_t(got, w_ref[2 * D :, :])
            total[rows_at(me, R), :] += first_ref[...]
            for j in range(M):
                parts[j] = total[:, j * C : (j + 1) * C].astype(BF)
            for kr in range(n_rep):
                for kf in range(n_feat):
                    outs[kr][kf] = parts[me ^ (kf * n_rep + kr)]

        local_grads = call(
            local_back_kernel,
            "local_backward",
            me1,
            [edge_dpre, slt_hot, rt_hot, in_full, node_first],
            [shape((n_feat, N, C))] * n_rep,
            scratch=[pltpu.VMEM((N, D), F32), pltpu.VMEM((M, N, C), BF)],
            flops=4 * E * D * N + 4 * N * D * D,
        )
        local_grads = member_sums(local_grads, me1, "local_pairs")

        def halo_sum_kernel(me_ref, *refs):
            total = refs[0][...].astype(F32)
            for k in range(1, n_feat):
                total += refs[k][...].astype(F32)
            for j in range(n_dom):
                refs[n_feat + j][...] = total[j * H : (j + 1) * H].astype(BF)

        halo_back = call(halo_sum_kernel, "halo_sums", me1, halo_grads, [shape((H, C))] * n_dom)
        halo_back = dom_trade(halo_back)

        def owed_kernel(me_ref, halo_ref, table_ref, *refs):
            local, back = refs[:n_feat], refs[n_feat : n_feat + n_dom]
            outs = refs[n_feat + n_dom :]
            total = local[0][...].astype(F32)
            for k in range(1, n_feat):
                total += local[k][...].astype(F32)
            rows = stack([back[j][...] for j in range(n_dom)])
            cot = (total + dot(hot_columns(halo_ref[...], N), rows)).astype(BF)
            for k in range(M):
                owed = dot(hot_rows(table_ref[k, 1:2, :], N), cot).astype(BF)
                for j in range(n_dom):
                    outs[j][k * S : (k + 1) * S, :] = owed[j * S : (j + 1) * S]

        owed = call(
            owed_kernel,
            "owed_rows",
            me1,
            [halo_row, slots] + local_grads + halo_back,
            [shape((M * S, C))] * n_dom,
            flops=2 * M * NS * N * C,
        )
        owed = dom_trade(owed)

        def grid_back_kernel(me_ref, slope_ref, table_ref, *refs):
            back, outs = refs[:n_dom], refs[n_dom:]
            for k in range(M):
                rows = stack([back[j][k * S : (k + 1) * S, :] for j in range(n_dom)])
                cot = dot(hot_columns(table_ref[k, 0:1, :], G), rows)
                outs[k][...] = (cot * slope_ref[k]).astype(BF)

        grid_dpre = call(
            grid_back_kernel,
            "grid_backward",
            me1,
            [grid_slope, slots] + owed,
            [shape((G, C))] * M,
            flops=2 * M * G * NS * C,
        )
        grid_dpre = member_trade(grid_dpre)

        def adjoint_kernel(me_ref, enc_ref, *refs):
            cols, out, parts = refs[:M], refs[M], refs[M + 1]
            for k in range(M):
                parts[me_ref[0] ^ k] = cols[k][...]
            out[...] = dot_t(lanes([parts[j] for j in range(M)]), enc_ref[...])

        return call(
            adjoint_kernel,
            "adjoint",
            me1,
            [enc_full] + grid_dpre,
            [shape((G, D), F32)],
            scratch=[pltpu.VMEM((M, G, C), BF)],
            flops=2 * G * D * D,
        )[0]

    return per_device


def solution(mesh):
    return jax.shard_map(
        make_per_device(mesh),
        mesh=mesh,
        in_specs=(
            P(("ens", "dom", "feat", "rep"), None),
            P("dom", None),
            P(("dom", "feat", "rep"), None),
            P(("feat", "rep"), None),
            P(("feat", "rep"), None),
            P(("feat", "rep"), None),
            P(("feat", "rep"), None),
            P(("feat", "rep"), None),
            P(("ens", "dom"), None),
            P(("ens", "dom", "feat", "rep"), None),
            P("dom", None, None),
            P(("dom", "feat", "rep")),
            P(("dom", "feat", "rep")),
            P(("dom", "feat", "rep"), None, None),
            P(("dom", "feat", "rep"), None, None),
        ),
        out_specs=P(("ens", "dom", "feat", "rep"), None),
        check_vma=False,
    )
```

```python
import jax
import jax.numpy as jnp
from jax import lax
from jax.experimental import pallas as pl
from jax.experimental.pallas import tpu as pltpu
from jax.sharding import PartitionSpec as P

BF = jnp.bfloat16
F32 = jnp.float32
SMEM = pl.BlockSpec(memory_space=pltpu.SMEM)
VMEM = pl.BlockSpec(memory_space=pltpu.VMEM)
HBM = pl.BlockSpec(memory_space=pltpu.HBM)
ANY = pl.BlockSpec(memory_space=pl.ANY)


def dot(a, b):
    return jnp.dot(a, b, preferred_element_type=F32)


def dot_t(a, b):
    return lax.dot_general(a, b, (((1,), (1,)), ((), ())), preferred_element_type=F32)


def silu_slope(values):
    logistic = jax.nn.sigmoid(values)
    return logistic * (1.0 + values * (1.0 - logistic))


def to_column(row):
    return jnp.transpose(jnp.broadcast_to(row, (8, row.shape[1])))[:, :1]


def hot_rows(row, depth):
    length = row.shape[1]
    return (to_column(row) == lax.broadcasted_iota(jnp.int32, (length, depth), 1)).astype(BF)


def hot_columns(row, depth):
    length = row.shape[1]
    return (row == lax.broadcasted_iota(jnp.int32, (depth, length), 0)).astype(BF)


def column_pick(me, depth, cols):
    at = lax.broadcasted_iota(jnp.int32, (depth, cols), 0) - me * cols
    return (at == lax.broadcasted_iota(jnp.int32, (depth, cols), 1)).astype(BF)


def rows_at(index, count):
    return pl.ds(pl.multiple_of(index * count, count), count)


def lanes(parts):
    return parts[0] if len(parts) == 1 else jnp.concatenate(parts, axis=1)


def stack(parts):
    return parts[0] if len(parts) == 1 else jnp.concatenate(parts, axis=0)


def call(body, name, me, ins, outs, scratch=(), flops=0, far=(), unread=()):
    size = lambda s: s.size * s.dtype.itemsize
    moved = sum(size(x) for x in ins) + sum(size(x) for x in outs)
    return pl.pallas_call(
        body,
        out_shape=list(outs),
        in_specs=[SMEM] + [HBM if i in far else ANY if i in unread else VMEM for i in range(len(ins))],
        out_specs=[VMEM] * len(outs),
        scratch_shapes=list(scratch),
        compiler_params=pltpu.CompilerParams(vmem_limit_bytes=24 * 2**20),
        cost_estimate=pl.CostEstimate(flops=flops, bytes_accessed=moved, transcendentals=0),
        name=name,
    )(me, *[pltpu.with_memory_space_constraint(x, pltpu.HBM) if i in far else x for i, x in enumerate(ins)])


def shape(dims, dtype=BF):
    return jax.ShapeDtypeStruct(tuple(dims), dtype)


def make_per_device(mesh):
    n_dom, n_feat, n_rep = mesh.shape["dom"], mesh.shape["feat"], mesh.shape["rep"]
    M = n_feat * n_rep

    def member_swap(x, k):
        return lax.ppermute(x, ("feat", "rep"), [(i, i ^ k) for i in range(M)])

    def dom_swap(x, k):
        return lax.ppermute(x, "dom", [(i, i ^ k) for i in range(n_dom)])

    def member_gather(x):
        return [x] + [member_swap(x, k) for k in range(1, M)]

    def member_gather_chips(x):
        parts = [None] * M
        for kf in range(n_feat):
            parts[kf * n_rep] = member_swap(x, kf * n_rep) if kf else x
        for kf in range(n_feat):
            for kr in range(1, n_rep):
                parts[kf * n_rep + kr] = member_swap(parts[kf * n_rep], kr)
        return parts

    def member_trade(parts):
        return [parts[0]] + [member_swap(parts[k], k) for k in range(1, M)]

    def member_sums(parts, me1, name):
        arrived = [parts[0]] + [member_swap(parts[kr], kr) for kr in range(1, n_rep)]

        def add_kernel(me_ref, *refs):
            for kf in range(n_feat):
                total = refs[0][kf].astype(F32)
                for kr in range(1, n_rep):
                    total += refs[kr][kf].astype(F32)
                refs[n_rep + kf][...] = total.astype(BF)

        halves = call(add_kernel, name, me1, arrived, [shape(parts[0].shape[1:])] * n_feat)
        return [halves[0]] + [member_swap(halves[kf], kf * n_rep) for kf in range(1, n_feat)]

    def dom_trade(parts):
        return [parts[0]] + [dom_swap(parts[k], k) for k in range(1, n_dom)]

    def per_device(
        grid_state,
        mesh_base,
        edge_state,
        enc_weight,
        edge_in_weight,
        edge_out_weight,
        node_in_weight,
        node_out_weight,
        node_grad,
        edge_grad,
        halo_rows,
        edge_send,
        edge_recv,
        grid_send,
        grid_recv,
    ):
        D = mesh_base.shape[1]
        N = mesh_base.shape[0]
        E = edge_state.shape[0]
        G = grid_state.shape[0]
        H = halo_rows.shape[2]
        S = grid_send.shape[2]
        NH = n_dom * H
        NS = n_dom * S
        C = D // M
        R = N // M
        T = 256
        PACK = 16
        assert NS == D
        rows_enc, rows_in, rows_out, rows_node = (
            enc_weight.shape[0],
            edge_in_weight.shape[0],
            edge_out_weight.shape[0],
            node_in_weight.shape[0],
        )
        me = lax.axis_index(("feat", "rep")).astype(jnp.int32)
        dom = lax.axis_index("dom").astype(jnp.int32)
        me1 = me.reshape(1)

        where = jnp.stack([me, dom])
        recv_row = edge_recv.reshape(1, E)

        def tables_kernel(where_ref, enc_ref, gs_ref, gr_ref, halo_ref, send_ref, *refs):
            pack_out, halo_out, send_out, gs, gr, halo, sent, sems = refs
            dom = where_ref[1]
            pairs = [
                (enc_ref, pack_out.at[:rows_enc, :]),
                (gs_ref.at[0], gs),
                (gr_ref.at[0], gr),
                (halo_ref.at[0], halo),
                (send_ref, sent),
            ]
            copies = [pltpu.make_async_copy(a, b, sems.at[i]) for i, (a, b) in enumerate(pairs)]
            for copy in copies:
                copy.start()
            for copy in copies:
                copy.wait()
            order = [pl.ds(dom ^ j, 1) for j in range(n_dom)]
            sends, recvs = lanes([gs[at, :] for at in order]), lanes([gr[at, :] for at in order])
            halo_out[...] = lanes([halo[at, :] for at in order])
            fill = jnp.zeros((PACK - 3, NS), jnp.int32)
            rows = stack([sends, recvs // 2, recvs % 2, fill])
            pack_out[rows_enc:, :] = rows.astype(F32).astype(BF)
            value = sent[...]
            away = jnp.maximum(value - N, 0)
            peer = away // H
            send_out[...] = jnp.where(value < N, value, N + (peer ^ dom) * H + (away - peer * H))

        pack, halo_row, send_row = call(
            tables_kernel,
            "tables",
            where,
            [enc_weight, grid_send, grid_recv, halo_rows, edge_send.reshape(1, E)],
            [shape((rows_enc + PACK, D)), shape((1, NH), jnp.int32), shape((1, E), jnp.int32)],
            scratch=[
                pltpu.VMEM((n_dom, S), jnp.int32),
                pltpu.VMEM((n_dom, S), jnp.int32),
                pltpu.VMEM((n_dom, H), jnp.int32),
                pltpu.VMEM((1, E), jnp.int32),
                pltpu.SemaphoreType.DMA((5,)),
            ],
            far=range(5),
        )

        state_parts = member_gather_chips(grid_state)
        pack_parts = member_gather_chips(pack)

        def grid_kernel(me_ref, *refs):
            states, packs = refs[:M], refs[M : 2 * M]
            enc_out, slope_out, table_out = refs[2 * M : 2 * M + 3]
            outs, (own, sem) = refs[2 * M + 3 : 2 * M + 3 + n_dom], refs[2 * M + 3 + n_dom :]
            me = me_ref[0]
            copy = pltpu.make_async_copy(states[0], own, sem)
            copy.start()
            for k in range(M):
                enc_out[rows_at(me ^ k, rows_enc), :] = packs[k][:rows_enc, :]
                rows = packs[k][rows_enc:, :].astype(F32).astype(jnp.int32)
                table_out[k, 0:1, :] = rows[0:1]
                table_out[k, 1:2, :] = 2 * rows[1:2] + rows[2:3]
            enc_cols = dot(enc_out[...], column_pick(me, D, C)).astype(BF)
            for k in list(range(1, M)) + [0]:
                if k == 0:
                    copy.wait()
                pre = dot(states[k][...] if k else own[...], enc_cols)
                logistic = jax.nn.sigmoid(pre)
                slope_out[k] = logistic * (1.0 + pre * (1.0 - logistic))
                message = (pre * logistic).astype(BF)
                rows = dot(hot_rows(table_out[k, 0:1, :], G), message).astype(BF)
                for j in range(n_dom):
                    outs[j][k * S : (k + 1) * S, :] = rows[j * S : (j + 1) * S]

        enc_full, grid_slope, slots, *outgoing = call(
            grid_kernel,
            "grid_messages",
            me1,
            state_parts + pack_parts,
            [shape((D, D)), shape((M, G, C), F32), shape((M, 2, NS), jnp.int32)]
            + [shape((M * S, C))] * n_dom,
            scratch=[pltpu.VMEM((G, D), BF), pltpu.SemaphoreType.DMA(())],
            flops=2 * M * G * D * C + 2 * M * NS * G * C,
            far=(0,),
        )
        incoming = dom_trade(outgoing)
        near, others = range(n_rep), range(n_rep, M)

        def hots_kernel(me_ref, send_ref, recv_ref, after_ref, sl_out, sh_out, r_out, slt_out, sht_out, rt_out):
            for i in range(E // T):
                at = slice(i * T, (i + 1) * T)
                sent, got = send_ref[:, at], recv_ref[:, at]
                sl_out[at, :] = hot_rows(sent, N)
                sh_out[at, :] = hot_rows(sent - N, NH)
                r_out[at, :] = hot_rows(got, N)
                slt_out[:, at] = hot_columns(sent, N)
                sht_out[:, at] = hot_columns(sent - N, NH)
                rt_out[:, at] = hot_columns(got, N)

        sl_hot, sh_hot, r_hot, slt_hot, sht_hot, rt_hot = call(
            hots_kernel,
            "edge_hots",
            me1,
            [send_row, recv_row, grid_slope],
            [shape((E, N)), shape((E, NH)), shape((E, N)), shape((N, E)), shape((NH, E)), shape((N, E))],
            unread=(2,),
        )

        firsts = [kf * n_rep for kf in range(1, n_feat)]

        def relay_kernel(me_ref, in_ref, out_ref, after_ref, edge_out, sems):
            pairs = [(in_ref, edge_out.at[:rows_in, :]), (out_ref, edge_out.at[rows_in:, :])]
            copies = [pltpu.make_async_copy(a, b, sems.at[i]) for i, (a, b) in enumerate(pairs)]
            for copy in copies:
                copy.start()
            for copy in copies:
                copy.wait()

        edge_own = call(
            relay_kernel,
            "relay",
            me1,
            [edge_in_weight, edge_out_weight, sl_hot],
            [shape((rows_in + rows_out, D))],
            scratch=[pltpu.SemaphoreType.DMA((2,))],
            far=range(2),
            unread=(2,),
        )[0]
        edge_chips = [edge_own] + [member_swap(edge_own, k) for k in firsts]

        def encode_kernel(me_ref, base_ref, table_ref, *refs):
            arrived, state_out = refs[:n_dom], refs[-1]
            total = dot(base_ref[...], column_pick(me_ref[0], D, C))
            for k in range(M):
                rows = stack([arrived[j][k * S : (k + 1) * S, :] for j in range(n_dom)])
                total += dot(hot_columns(table_ref[k, 1:2, :], N), rows)
            state_out[...] = total.astype(BF)

        state_cols = call(
            encode_kernel,
            "encode",
            me1,
            [mesh_base, slots] + incoming + [sl_hot],
            [shape((N, C))],
            flops=2 * M * N * NS * C,
            unread=(2 + n_dom,),
        )[0]
        state_parts2 = member_gather_chips(state_cols)

        def halo_kernel(me_ref, state_ref, halo_ref, *outs):
            rows = dot(hot_rows(halo_ref[...], N), state_ref[...]).astype(BF)
            for j in range(n_dom):
                outs[j][...] = rows[j * H : (j + 1) * H]

        halo_out = call(
            halo_kernel,
            "halo_rows",
            me1,
            [state_cols, halo_row],
            [shape((H, C))] * n_dom,
            flops=2 * N * NH * C,
        )
        halo_in = dom_trade(halo_out)

        def join_kernel(me_ref, *refs):
            for j in range(n_dom):
                refs[-1][j * H : (j + 1) * H, :] = refs[j][...]

        halo_cols = call(
            join_kernel,
            "halo_join",
            me1,
            halo_in + [state_parts2[n_rep]],
            [shape((NH, C))],
            unread=(n_dom,),
        )[0]
        halo_parts = member_gather_chips(halo_cols)

        def weights_kernel(me_ref, in_ref, out_ref, *refs):
            chips, (pair_out, node_out, sems) = refs[:n_feat], refs[-3:]
            pairs = [(in_ref, node_out.at[:rows_node, :]), (out_ref, node_out.at[rows_node:, :])]
            copies = [pltpu.make_async_copy(a, b, sems.at[i]) for i, (a, b) in enumerate(pairs)]
            for copy in copies:
                copy.start()
            for kf in range(n_feat):
                pair_out[kf] = chips[kf][...]
            for copy in copies:
                copy.wait()

        edge_pair, node_own = call(
            weights_kernel,
            "join_weights",
            me1,
            [node_in_weight, node_out_weight] + edge_chips + [halo_cols],
            [shape((n_feat, rows_in + rows_out, D)), shape((rows_node + rows_out, D))],
            scratch=[pltpu.SemaphoreType.DMA((2,))],
            far=range(2),
            unread=(2 + n_feat,),
        )
        edge_pairs = [edge_pair] + [member_swap(edge_pair, kr) for kr in range(1, n_rep)]
        node_chips = [node_own] + [member_swap(node_own, k) for k in firsts]


        def local_kernel(me_ref, es_ref, send_ref, recv_ref, *refs):
            cols, weights = refs[:M], refs[M : M + n_rep]
            pre_out, state_out, w_out, out_out, parts = refs[M + n_rep :]
            me = me_ref[0]
            for k in range(M):
                kf, kr = divmod(k, n_rep)
                parts[me ^ k] = cols[k][...]
                w_out[rows_at(me ^ k, rows_in), :] = weights[kr][kf, :rows_in, :]
                out_out[rows_at(me ^ k, rows_out), :] = weights[kr][kf, rows_in:, :]
            state_out[...] = lanes([parts[j] for j in range(M)])
            for i in range(E // T):
                at = slice(i * T, (i + 1) * T)
                sent = dot(send_ref[at, :], state_out[...]).astype(BF)
                got = dot(recv_ref[at, :], state_out[...]).astype(BF)
                pre_out[at, :] = (
                    dot(es_ref[at, :], w_out[:D, :])
                    + dot(sent, w_out[D : 2 * D, :])
                    + dot(got, w_out[2 * D :, :])
                )

        local_pre, mesh_state, in_full, out_full = call(
            local_kernel,
            "edge_local",
            me1,
            [edge_state, sl_hot, r_hot] + state_parts2 + edge_pairs,
            [shape((E, D), F32), shape((N, D)), shape((3 * D, D)), shape((D, D))],
            scratch=[pltpu.VMEM((M, N, C), BF)],
            flops=2 * E * D * (3 * D + 2 * N),
        )

        def edge_kernel(me_ref, local_ref, es_ref, send_ref, recv_ref, w_ref, out_ref, *refs):
            cols = refs[:M]
            pre_out, outs = refs[M], refs[M + 1 : M + 1 + n_rep]
            parts, halo, new, total = refs[M + 1 + n_rep :]
            me = me_ref[0]
            for k in range(M):
                parts[me ^ k] = cols[k][...]
            halo[...] = lanes([parts[j] for j in range(M)])
            for i in range(E // T):
                at = slice(i * T, (i + 1) * T)
                sent = dot(send_ref[at, :], halo[...]).astype(BF)
                pre = local_ref[at, :] + dot(sent, w_ref[D : 2 * D, :])
                pre_out[at, :] = pre
                hidden = (pre * jax.nn.sigmoid(pre)).astype(BF)
                new[at, :] = (es_ref[at, :].astype(F32) + dot(hidden, out_ref[...])).astype(BF)
            for i in range(N // T):
                at = slice(i * T, (i + 1) * T)
                total[at, :] = dot(recv_ref[at, :], new[...]).astype(BF)
            for kr in range(n_rep):
                for kf in range(n_feat):
                    outs[kr][kf] = total[rows_at(me ^ (kf * n_rep + kr), R), :]

        edge_pre, *sums = call(
            edge_kernel,
            "edge_update",
            me1,
            [local_pre, edge_state, sh_hot, rt_hot, in_full, out_full] + halo_parts,
            [shape((E, D), F32)] + [shape((n_feat, R, D))] * n_rep,
            scratch=[
                pltpu.VMEM((M, NH, C), BF),
                pltpu.VMEM((NH, D), BF),
                pltpu.VMEM((E, D), BF),
                pltpu.VMEM((N, D), BF),
            ],
            flops=2 * E * D * (NH + D + D + N),
        )
        def node_weights_kernel(me_ref, *refs):
            for kf in range(n_feat):
                refs[-1][kf] = refs[kf][...]

        node_pair = call(
            node_weights_kernel,
            "join_node_weights",
            me1,
            node_chips + [sums[0]],
            [shape((n_feat, rows_node + rows_out, D))],
            unread=(n_feat,),
        )[0]
        node_pairs = [node_pair] + [member_swap(node_pair, kr) for kr in range(1, n_rep)]

        def node_ahead_kernel(me_ref, state_ref, grad_ref, *refs):
            weights = refs[:n_rep]
            node_in_full, pre_out, cot_out, node_out_full = refs[n_rep:]
            me = me_ref[0]
            for k in range(M):
                kf, kr = divmod(k, n_rep)
                node_in_full[rows_at(me ^ k, rows_node), :] = weights[kr][kf, :rows_node, :]
                node_out_full[rows_at(me ^ k, rows_out), :] = weights[kr][kf, rows_node:, :]
            mine = rows_at(me, R)
            pre_out[...] = dot(state_ref[mine, :], node_in_full[:D, :])
            cot_out[...] = dot_t(grad_ref[mine, :], node_out_full[...])

        node_in_full, node_pre, node_cot = call(
            node_ahead_kernel,
            "node_ahead",
            me1,
            [mesh_state, node_grad] + node_pairs,
            [shape((2 * D, D)), shape((R, D), F32), shape((R, D), F32)],
            scratch=[pltpu.VMEM((D, D), BF)],
            flops=4 * R * D * D,
        )

        sums = member_sums(sums, me1, "node_sums")

        def node_kernel(me_ref, pre_ref, cot_ref, w_ref, grad_ref, *refs):
            first_out, second_out = refs[n_feat:]
            total = refs[0][...].astype(F32)
            for k in range(1, n_feat):
                total += refs[k][...].astype(F32)
            pre = pre_ref[...] + dot(total.astype(BF), w_ref[D:, :])
            dpre = (cot_ref[...] * silu_slope(pre)).astype(BF)
            second_out[...] = dot_t(dpre, w_ref[D:, :]).astype(BF)
            mine = grad_ref[rows_at(me_ref[0], R), :].astype(F32)
            first_out[...] = mine + dot_t(dpre, w_ref[:D, :])

        node_first, node_second = call(
            node_kernel,
            "node_backward",
            me1,
            [node_pre, node_cot, node_in_full, node_grad] + sums,
            [shape((R, D), F32), shape((R, D))],
            flops=6 * R * D * D,
        )
        second_parts = member_gather_chips(node_second)

        def edge_back_kernel(me_ref, grad_ref, pre_ref, send_ref, recv_ref, w_ref, out_ref, *refs):
            nodes = refs[:M]
            dpre_out, outs = refs[M], refs[M + 1 : M + 1 + n_rep]
            second, parts = refs[M + 1 + n_rep :]
            me = me_ref[0]
            for k in range(M):
                second[rows_at(me ^ k, R), :] = nodes[k][...]
            for i in range(E // T):
                at = slice(i * T, (i + 1) * T)
                got = dot(recv_ref[at, :], second[...])
                cot = (grad_ref[at, :].astype(F32) + got).astype(BF)
                dpre_out[at, :] = (dot_t(cot, out_ref[...]) * silu_slope(pre_ref[at, :])).astype(BF)
            for i in range(NH // T):
                at = slice(i * T, (i + 1) * T)
                sent = dot(send_ref[at, :], dpre_out[...]).astype(BF)
                halo = dot_t(sent, w_ref[D : 2 * D, :]).astype(BF)
                for j in range(M):
                    parts[j, at, :] = halo[:, j * C : (j + 1) * C]
            for kr in range(n_rep):
                for kf in range(n_feat):
                    outs[kr][kf] = parts[me ^ (kf * n_rep + kr)]

        edge_dpre, *halo_grads = call(
            edge_back_kernel,
            "edge_backward",
            me1,
            [edge_grad, edge_pre, sht_hot, r_hot, in_full, out_full] + second_parts,
            [shape((E, D))] + [shape((n_feat, NH, C))] * n_rep,
            scratch=[pltpu.VMEM((N, D), BF), pltpu.VMEM((M, NH, C), BF)],
            flops=2 * E * D * (N + D + NH) + 2 * NH * D * D,
        )
        halo_grads = member_sums(halo_grads, me1, "halo_pairs")

        def local_back_kernel(me_ref, dpre_ref, send_ref, recv_ref, w_ref, first_ref, *refs):
            outs, (total, parts) = refs[:n_rep], refs[n_rep:]
            me = me_ref[0]
            for i in range(N // T):
                at = slice(i * T, (i + 1) * T)
                sent = dot(send_ref[at, :], dpre_ref[...]).astype(BF)
                got = dot(recv_ref[at, :], dpre_ref[...]).astype(BF)
                total[at, :] = dot_t(sent, w_ref[D : 2 * D, :]) + dot_t(got, w_ref[2 * D :, :])
            total[rows_at(me, R), :] += first_ref[...]
            for j in range(M):
                parts[j] = total[:, j * C : (j + 1) * C].astype(BF)
            for kr in range(n_rep):
                for kf in range(n_feat):
                    outs[kr][kf] = parts[me ^ (kf * n_rep + kr)]

        local_grads = call(
            local_back_kernel,
            "local_backward",
            me1,
            [edge_dpre, slt_hot, rt_hot, in_full, node_first],
            [shape((n_feat, N, C))] * n_rep,
            scratch=[pltpu.VMEM((N, D), F32), pltpu.VMEM((M, N, C), BF)],
            flops=4 * E * D * N + 4 * N * D * D,
        )
        local_grads = member_sums(local_grads, me1, "local_pairs")

        def halo_sum_kernel(me_ref, *refs):
            total = refs[0][...].astype(F32)
            for k in range(1, n_feat):
                total += refs[k][...].astype(F32)
            for j in range(n_dom):
                refs[n_feat + j][...] = total[j * H : (j + 1) * H].astype(BF)

        halo_back = call(halo_sum_kernel, "halo_sums", me1, halo_grads, [shape((H, C))] * n_dom)
        halo_back = dom_trade(halo_back)

        def owed_kernel(me_ref, halo_ref, table_ref, *refs):
            local, back = refs[:n_feat], refs[n_feat : n_feat + n_dom]
            first, second = refs[n_feat + n_dom : -n_dom], refs[-n_dom:]
            total = local[0][...].astype(F32)
            for k in range(1, n_feat):
                total += local[k][...].astype(F32)
            rows = stack([back[j][...] for j in range(n_dom)])
            cot = (total + dot(hot_columns(halo_ref[...], N), rows)).astype(BF)
            for k in range(M):
                owed = dot(hot_rows(table_ref[k, 1:2, :], N), cot).astype(BF)
                outs, at = (first, k) if k < n_rep else (second, k - n_rep)
                for j in range(n_dom):
                    outs[j][at * S : (at + 1) * S, :] = owed[j * S : (j + 1) * S]

        owed = call(
            owed_kernel,
            "owed_rows",
            me1,
            [halo_row, slots] + local_grads + halo_back,
            [shape((n_rep * S, C))] * n_dom + [shape((len(others) * S, C))] * n_dom,
            flops=2 * M * NS * N * C,
        )
        far_owed = dom_trade(owed[n_dom:])
        near_owed = dom_trade(owed[:n_dom])

        def grid_back(name, members, back, after=()):
            def kernel(me_ref, slope_ref, table_ref, *refs):
                arrived, outs = refs[:n_dom], refs[n_dom + len(after) :]
                for at, k in enumerate(members):
                    rows = stack([arrived[j][at * S : (at + 1) * S, :] for j in range(n_dom)])
                    cot = dot(hot_columns(table_ref[k, 0:1, :], G), rows)
                    outs[at][...] = (cot * slope_ref[k]).astype(BF)

            return call(
                kernel,
                name,
                me1,
                [grid_slope, slots] + back + list(after),
                [shape((G, C))] * len(members),
                flops=2 * len(members) * G * NS * C,
                unread=range(2 + n_dom, 2 + n_dom + len(after)),
            )

        far_dpre = grid_back("grid_back_far", others, far_owed)
        near_dpre = grid_back("grid_back_near", near, near_owed, far_dpre[:1])
        far_dpre = [member_swap(x, k) for x, k in zip(far_dpre, others)]
        near_dpre = [member_swap(x, k) if k else x for x, k in zip(near_dpre, near)]
        grid_dpre = near_dpre + far_dpre

        def adjoint_kernel(me_ref, enc_ref, *refs):
            cols, out, parts = refs[:M], refs[M], refs[M + 1]
            for k in range(M):
                parts[me_ref[0] ^ k] = cols[k][...]
            out[...] = dot_t(lanes([parts[j] for j in range(M)]), enc_ref[...])

        return call(
            adjoint_kernel,
            "adjoint",
            me1,
            [enc_full] + grid_dpre,
            [shape((G, D), F32)],
            scratch=[pltpu.VMEM((M, G, C), BF)],
            flops=2 * G * D * D,
        )[0]

    return per_device


def solution(mesh):
    return jax.shard_map(
        make_per_device(mesh),
        mesh=mesh,
        in_specs=(
            P(("ens", "dom", "feat", "rep"), None),
            P("dom", None),
            P(("dom", "feat", "rep"), None),
            P(("feat", "rep"), None),
            P(("feat", "rep"), None),
            P(("feat", "rep"), None),
            P(("feat", "rep"), None),
            P(("feat", "rep"), None),
            P(("ens", "dom"), None),
            P(("ens", "dom", "feat", "rep"), None),
            P("dom", None, None),
            P(("dom", "feat", "rep")),
            P(("dom", "feat", "rep")),
            P(("dom", "feat", "rep"), None, None),
            P(("dom", "feat", "rep"), None, None),
        ),
        out_specs=P(("ens", "dom", "feat", "rep"), None),
        check_vma=False,
    )
```

```python
import jax
import jax.numpy as jnp
from jax import lax
from jax.experimental import pallas as pl
from jax.experimental.pallas import tpu as pltpu
from jax.sharding import PartitionSpec as P

BF = jnp.bfloat16
F32 = jnp.float32
SMEM = pl.BlockSpec(memory_space=pltpu.SMEM)
VMEM = pl.BlockSpec(memory_space=pltpu.VMEM)
HBM = pl.BlockSpec(memory_space=pltpu.HBM)
ANY = pl.BlockSpec(memory_space=pl.ANY)


def dot(a, b):
    return jnp.dot(a, b, preferred_element_type=F32)


def dot_t(a, b):
    return lax.dot_general(a, b, (((1,), (1,)), ((), ())), preferred_element_type=F32)


def silu_slope(values):
    logistic = jax.nn.sigmoid(values)
    return logistic * (1.0 + values * (1.0 - logistic))


def to_column(row):
    return jnp.transpose(jnp.broadcast_to(row, (8, row.shape[1])))[:, :1]


def hot_rows(row, depth):
    length = row.shape[1]
    return (to_column(row) == lax.broadcasted_iota(jnp.int32, (length, depth), 1)).astype(BF)


def hot_columns(row, depth):
    length = row.shape[1]
    return (row == lax.broadcasted_iota(jnp.int32, (depth, length), 0)).astype(BF)


def column_pick(me, depth, cols):
    at = lax.broadcasted_iota(jnp.int32, (depth, cols), 0) - me * cols
    return (at == lax.broadcasted_iota(jnp.int32, (depth, cols), 1)).astype(BF)


def rows_at(index, count):
    return pl.ds(pl.multiple_of(index * count, count), count)


def lanes(parts):
    return parts[0] if len(parts) == 1 else jnp.concatenate(parts, axis=1)


def stack(parts):
    return parts[0] if len(parts) == 1 else jnp.concatenate(parts, axis=0)


def call(body, name, me, ins, outs, scratch=(), flops=0, far=(), unread=()):
    size = lambda s: s.size * s.dtype.itemsize
    moved = sum(size(x) for x in ins) + sum(size(x) for x in outs)
    result = pl.pallas_call(
        body,
        out_shape=list(outs),
        in_specs=[SMEM] + [HBM if i in far else ANY if i in unread else VMEM for i in range(len(ins))],
        out_specs=[VMEM] * len(outs),
        scratch_shapes=list(scratch),
        compiler_params=pltpu.CompilerParams(vmem_limit_bytes=24 * 2**20),
        cost_estimate=pl.CostEstimate(flops=flops, bytes_accessed=moved, transcendentals=0),
        name=name,
    )(me, *[pltpu.with_memory_space_constraint(x, pltpu.HBM) if i in far else x for i, x in enumerate(ins)])
    return list(result)


def shape(dims, dtype=BF):
    return jax.ShapeDtypeStruct(tuple(dims), dtype)


def make_per_device(mesh):
    n_dom, n_feat, n_rep = mesh.shape["dom"], mesh.shape["feat"], mesh.shape["rep"]
    M = n_feat * n_rep

    def member_swap(x, k):
        return lax.ppermute(x, ("feat", "rep"), [(i, i ^ k) for i in range(M)])

    def dom_swap(x, k):
        return lax.ppermute(x, "dom", [(i, i ^ k) for i in range(n_dom)])

    def member_gather(x):
        return [x] + [member_swap(x, k) for k in range(1, M)]

    def member_gather_chips(x):
        parts = [None] * M
        for kf in range(n_feat):
            parts[kf * n_rep] = member_swap(x, kf * n_rep) if kf else x
        for kf in range(n_feat):
            for kr in range(1, n_rep):
                parts[kf * n_rep + kr] = member_swap(parts[kf * n_rep], kr)
        return parts

    def member_trade(parts):
        return [parts[0]] + [member_swap(parts[k], k) for k in range(1, M)]

    def member_sums(parts, me1, name):
        arrived = [parts[0]] + [member_swap(parts[kr], kr) for kr in range(1, n_rep)]

        def add_kernel(me_ref, *refs):
            for kf in range(n_feat):
                total = refs[0][kf].astype(F32)
                for kr in range(1, n_rep):
                    total += refs[kr][kf].astype(F32)
                refs[n_rep + kf][...] = total.astype(BF)

        halves = call(add_kernel, name, me1, arrived, [shape(parts[0].shape[1:])] * n_feat)
        return [halves[0]] + [member_swap(halves[kf], kf * n_rep) for kf in range(1, n_feat)]

    def dom_trade(parts):
        return [parts[0]] + [dom_swap(parts[k], k) for k in range(1, n_dom)]

    def per_device(
        grid_state,
        mesh_base,
        edge_state,
        enc_weight,
        edge_in_weight,
        edge_out_weight,
        node_in_weight,
        node_out_weight,
        node_grad,
        edge_grad,
        halo_rows,
        edge_send,
        edge_recv,
        grid_send,
        grid_recv,
    ):
        D = mesh_base.shape[1]
        N = mesh_base.shape[0]
        E = edge_state.shape[0]
        G = grid_state.shape[0]
        H = halo_rows.shape[2]
        S = grid_send.shape[2]
        NH = n_dom * H
        NS = n_dom * S
        C = D // M
        R = N // M
        T = 256
        PACK = 16
        assert NS == D
        rows_enc, rows_in, rows_out, rows_node = (
            enc_weight.shape[0],
            edge_in_weight.shape[0],
            edge_out_weight.shape[0],
            node_in_weight.shape[0],
        )
        me = lax.axis_index(("feat", "rep")).astype(jnp.int32)
        dom = lax.axis_index("dom").astype(jnp.int32)
        me1 = me.reshape(1)

        where = jnp.stack([me, dom])
        recv_row = edge_recv.reshape(1, E)

        def tables_kernel(where_ref, enc_ref, gs_ref, gr_ref, halo_ref, send_ref, *refs):
            pack_out, halo_out, send_out, gs, gr, halo, sent, sems = refs
            dom = where_ref[1]
            pairs = [
                (enc_ref, pack_out.at[:rows_enc, :]),
                (gs_ref.at[0], gs),
                (gr_ref.at[0], gr),
                (halo_ref.at[0], halo),
                (send_ref, sent),
            ]
            copies = [pltpu.make_async_copy(a, b, sems.at[i]) for i, (a, b) in enumerate(pairs)]
            for copy in copies:
                copy.start()
            for copy in copies:
                copy.wait()
            order = [pl.ds(dom ^ j, 1) for j in range(n_dom)]
            sends, recvs = lanes([gs[at, :] for at in order]), lanes([gr[at, :] for at in order])
            halo_out[...] = lanes([halo[at, :] for at in order])
            fill = jnp.zeros((PACK - 3, NS), jnp.int32)
            rows = stack([sends, recvs // 2, recvs % 2, fill])
            pack_out[rows_enc:, :] = rows.astype(F32).astype(BF)
            value = sent[...]
            away = jnp.maximum(value - N, 0)
            peer = away // H
            send_out[...] = jnp.where(value < N, value, N + (peer ^ dom) * H + (away - peer * H))

        pack, halo_row, send_row = call(
            tables_kernel,
            "tables",
            where,
            [enc_weight, grid_send, grid_recv, halo_rows, edge_send.reshape(1, E)],
            [shape((rows_enc + PACK, D)), shape((1, NH), jnp.int32), shape((1, E), jnp.int32)],
            scratch=[
                pltpu.VMEM((n_dom, S), jnp.int32),
                pltpu.VMEM((n_dom, S), jnp.int32),
                pltpu.VMEM((n_dom, H), jnp.int32),
                pltpu.VMEM((1, E), jnp.int32),
                pltpu.SemaphoreType.DMA((5,)),
            ],
            far=range(5),
        )

        state_parts = member_gather_chips(grid_state)
        pack_parts = member_gather_chips(pack)

        def hots_kernel(me_ref, send_ref, recv_ref, sl_out, sh_out, r_out, slt_out, sht_out, rt_out):
            for i in range(E // T):
                at = slice(i * T, (i + 1) * T)
                sent, got = send_ref[:, at], recv_ref[:, at]
                sl_out[at, :] = hot_rows(sent, N)
                sh_out[at, :] = hot_rows(sent - N, NH)
                r_out[at, :] = hot_rows(got, N)
                slt_out[:, at] = hot_columns(sent, N)
                sht_out[:, at] = hot_columns(sent - N, NH)
                rt_out[:, at] = hot_columns(got, N)

        sl_hot, sh_hot, r_hot, slt_hot, sht_hot, rt_hot = call(
            hots_kernel,
            "edge_hots",
            me1,
            [send_row, recv_row],
            [shape((E, N)), shape((E, NH)), shape((E, N)), shape((N, E)), shape((NH, E)), shape((N, E))],
        )

        firsts = [kf * n_rep for kf in range(1, n_feat)]

        def stacked(pairs, out, sems):
            copies, at = [], 0
            for i, ref in enumerate(pairs):
                copies.append(pltpu.make_async_copy(ref, out.at[at : at + ref.shape[0], :], sems.at[i]))
                at += ref.shape[0]
            return copies

        def grid_kernel(me_ref, *refs):
            states, packs = refs[:M], refs[M : 2 * M]
            enc_out, slope_out, table_out, edge_out = refs[2 * M + 3 : 2 * M + 7]
            outs, (own, sem, sems) = refs[2 * M + 7 : 2 * M + 7 + n_dom], refs[2 * M + 7 + n_dom :]
            me = me_ref[0]
            copy = pltpu.make_async_copy(states[0], own, sem)
            copy.start()
            weight_copies = stacked(refs[2 * M : 2 * M + 2], edge_out, sems)
            for each in weight_copies:
                each.start()
            for k in range(M):
                enc_out[rows_at(me ^ k, rows_enc), :] = packs[k][:rows_enc, :]
                rows = packs[k][rows_enc:, :].astype(F32).astype(jnp.int32)
                table_out[k, 0:1, :] = rows[0:1]
                table_out[k, 1:2, :] = 2 * rows[1:2] + rows[2:3]
            enc_cols = dot(enc_out[...], column_pick(me, D, C)).astype(BF)
            for k in list(range(1, M)) + [0]:
                if k == 0:
                    copy.wait()
                pre = dot(states[k][...] if k else own[...], enc_cols)
                logistic = jax.nn.sigmoid(pre)
                slope_out[k] = logistic * (1.0 + pre * (1.0 - logistic))
                message = (pre * logistic).astype(BF)
                rows = dot(hot_rows(table_out[k, 0:1, :], G), message).astype(BF)
                for j in range(n_dom):
                    outs[j][k * S : (k + 1) * S, :] = rows[j * S : (j + 1) * S]
            for each in weight_copies:
                each.wait()

        enc_full, grid_slope, slots, edge_own, *outgoing = call(
            grid_kernel,
            "grid_messages",
            me1,
            state_parts + pack_parts + [edge_in_weight, edge_out_weight, sl_hot],
            [shape((D, D)), shape((M, G, C), F32), shape((M, 2, NS), jnp.int32), shape((rows_in + rows_out, D))]
            + [shape((M * S, C))] * n_dom,
            scratch=[pltpu.VMEM((G, D), BF), pltpu.SemaphoreType.DMA(()), pltpu.SemaphoreType.DMA((2,))],
            flops=2 * M * G * D * C + 2 * M * NS * G * C,
            far=(0, 2 * M, 2 * M + 1),
            unread=(2 * M + 2,),
        )
        incoming = dom_trade(outgoing)
        near, others = range(n_rep), range(n_rep, M)
        edge_chips = [edge_own] + [member_swap(edge_own, k) for k in firsts]

        def encode_kernel(me_ref, base_ref, table_ref, *refs):
            arrived, state_out = refs[:n_dom], refs[-1]
            total = dot(base_ref[...], column_pick(me_ref[0], D, C))
            for k in range(M):
                rows = stack([arrived[j][k * S : (k + 1) * S, :] for j in range(n_dom)])
                total += dot(hot_columns(table_ref[k, 1:2, :], N), rows)
            state_out[...] = total.astype(BF)

        state_cols = call(
            encode_kernel,
            "encode",
            me1,
            [mesh_base, slots] + incoming,
            [shape((N, C))],
            flops=2 * M * N * NS * C,
        )[0]
        state_chips = [state_cols] + [member_swap(state_cols, k) for k in firsts]

        def halo_kernel(me_ref, state_ref, halo_ref, *outs):
            rows = dot(hot_rows(halo_ref[...], N), state_ref[...]).astype(BF)
            for j in range(n_dom):
                outs[j][...] = rows[j * H : (j + 1) * H]

        halo_out = call(
            halo_kernel,
            "halo_rows",
            me1,
            [state_cols, halo_row],
            [shape((H, C))] * n_dom,
            flops=2 * N * NH * C,
        )
        halo_in = dom_trade(halo_out)
        core_swaps = lambda x: [x] + [member_swap(x, kr) for kr in range(1, n_rep)]

        def pair_kernel(me_ref, *refs):
            for kf in range(n_feat):
                refs[-1][kf] = refs[kf][...]

        def join_kernel(me_ref, *refs):
            halo, chips, weights = refs[:n_dom], refs[n_dom : n_dom + n_feat], refs[n_dom + n_feat : -3]
            halo_out_ref, pair_out, weights_out = refs[-3:]
            for j in range(n_dom):
                halo_out_ref[j * H : (j + 1) * H, :] = halo[j][...]
            for kf in range(n_feat):
                pair_out[kf] = chips[kf][...]
                weights_out[kf] = weights[kf][...]

        halo_cols, state_pair, edge_pair = call(
            join_kernel,
            "halo_join",
            me1,
            halo_in + state_chips + edge_chips,
            [shape((NH, C)), shape((n_feat, N, C)), shape((n_feat, rows_in + rows_out, D))],
        )
        halo_chips = [halo_cols] + [member_swap(halo_cols, k) for k in firsts]
        state_pairs = core_swaps(state_pair)
        edge_pairs = core_swaps(edge_pair)

        def local_kernel(me_ref, in_ref, out_ref, es_ref, send_ref, recv_ref, *refs):
            cols, weights = refs[:n_rep], refs[n_rep : 2 * n_rep]
            pre_out, state_out, w_out, out_out, node_out, parts, sems = refs[2 * n_rep :]
            copies = stacked([in_ref, out_ref], node_out, sems)
            for copy in copies:
                copy.start()
            me = me_ref[0]
            for k in range(M):
                kf, kr = divmod(k, n_rep)
                parts[me ^ k] = cols[kr][kf]
                w_out[rows_at(me ^ k, rows_in), :] = weights[kr][kf, :rows_in, :]
                out_out[rows_at(me ^ k, rows_out), :] = weights[kr][kf, rows_in:, :]
            state_out[...] = lanes([parts[j] for j in range(M)])
            for i in range(E // T):
                at = slice(i * T, (i + 1) * T)
                sent = dot(send_ref[at, :], state_out[...]).astype(BF)
                got = dot(recv_ref[at, :], state_out[...]).astype(BF)
                pre_out[at, :] = (
                    dot(es_ref[at, :], w_out[:D, :])
                    + dot(sent, w_out[D : 2 * D, :])
                    + dot(got, w_out[2 * D :, :])
                )
            for copy in copies:
                copy.wait()

        local_pre, mesh_state, in_full, out_full, node_own = call(
            local_kernel,
            "edge_local",
            me1,
            [node_in_weight, node_out_weight, edge_state, sl_hot, r_hot] + state_pairs + edge_pairs,
            [shape((E, D), F32), shape((N, D)), shape((3 * D, D)), shape((D, D))]
            + [shape((rows_node + rows_out, D))],
            scratch=[pltpu.VMEM((M, N, C), BF), pltpu.SemaphoreType.DMA((2,))],
            flops=2 * E * D * (3 * D + 2 * N),
            far=range(2),
        )
        node_chips = [node_own] + [member_swap(node_own, k) for k in firsts]

        halo_pair = call(
            pair_kernel,
            "halo_pair",
            me1,
            halo_chips + [local_pre],
            [shape((n_feat, NH, C))],
            unread=(n_feat,),
        )[0]
        halo_pairs = core_swaps(halo_pair)

        def edge_kernel(me_ref, local_ref, es_ref, send_ref, recv_ref, w_ref, out_ref, *refs):
            cols = refs[:n_rep]
            pre_out, outs = refs[n_rep], refs[n_rep + 1 : 2 * n_rep + 1]
            parts, halo, new, total = refs[2 * n_rep + 1 :]
            me = me_ref[0]
            for k in range(M):
                kf, kr = divmod(k, n_rep)
                parts[me ^ k] = cols[kr][kf]
            halo[...] = lanes([parts[j] for j in range(M)])
            for i in range(E // T):
                at = slice(i * T, (i + 1) * T)
                sent = dot(send_ref[at, :], halo[...]).astype(BF)
                pre = local_ref[at, :] + dot(sent, w_ref[D : 2 * D, :])
                pre_out[at, :] = pre
                hidden = (pre * jax.nn.sigmoid(pre)).astype(BF)
                new[at, :] = (es_ref[at, :].astype(F32) + dot(hidden, out_ref[...])).astype(BF)
            for i in range(N // T):
                at = slice(i * T, (i + 1) * T)
                total[at, :] = dot(recv_ref[at, :], new[...]).astype(BF)
            for kr in range(n_rep):
                for kf in range(n_feat):
                    outs[kr][kf] = total[rows_at(me ^ (kf * n_rep + kr), R), :]

        edge_pre, *sums = call(
            edge_kernel,
            "edge_update",
            me1,
            [local_pre, edge_state, sh_hot, rt_hot, in_full, out_full] + halo_pairs,
            [shape((E, D), F32)] + [shape((n_feat, R, D))] * n_rep,
            scratch=[
                pltpu.VMEM((M, NH, C), BF),
                pltpu.VMEM((NH, D), BF),
                pltpu.VMEM((E, D), BF),
                pltpu.VMEM((N, D), BF),
            ],
            flops=2 * E * D * (NH + D + D + N),
        )
        sums = member_sums(sums, me1, "node_sums")

        node_pair = call(
            pair_kernel,
            "node_pair",
            me1,
            node_chips + [sums[0]],
            [shape((n_feat, rows_node + rows_out, D))],
            unread=(n_feat,),
        )[0]
        node_pairs = core_swaps(node_pair)

        def node_ahead_kernel(me_ref, state_ref, grad_ref, *refs):
            weights = refs[:n_rep]
            node_in_full, pre_out, cot_out, node_out_full = refs[n_rep:]
            me = me_ref[0]
            for k in range(M):
                kf, kr = divmod(k, n_rep)
                node_in_full[rows_at(me ^ k, rows_node), :] = weights[kr][kf, :rows_node, :]
                node_out_full[rows_at(me ^ k, rows_out), :] = weights[kr][kf, rows_node:, :]
            mine = rows_at(me, R)
            pre_out[...] = dot(state_ref[mine, :], node_in_full[:D, :])
            cot_out[...] = dot_t(grad_ref[mine, :], node_out_full[...])

        node_in_full, node_pre, node_cot = call(
            node_ahead_kernel,
            "node_ahead",
            me1,
            [mesh_state, node_grad] + node_pairs,
            [shape((2 * D, D)), shape((R, D), F32), shape((R, D), F32)],
            scratch=[pltpu.VMEM((D, D), BF)],
            flops=4 * R * D * D,
        )

        def node_kernel(me_ref, pre_ref, cot_ref, w_ref, grad_ref, *refs):
            first_out, second_out = refs[n_feat:]
            total = refs[0][...].astype(F32)
            for k in range(1, n_feat):
                total += refs[k][...].astype(F32)
            pre = pre_ref[...] + dot(total.astype(BF), w_ref[D:, :])
            dpre = (cot_ref[...] * silu_slope(pre)).astype(BF)
            second_out[...] = dot_t(dpre, w_ref[D:, :]).astype(BF)
            mine = grad_ref[rows_at(me_ref[0], R), :].astype(F32)
            first_out[...] = mine + dot_t(dpre, w_ref[:D, :])

        node_first, node_second = call(
            node_kernel,
            "node_backward",
            me1,
            [node_pre, node_cot, node_in_full, node_grad] + sums,
            [shape((R, D), F32), shape((R, D))],
            flops=6 * R * D * D,
        )
        second_parts = member_gather_chips(node_second)

        def edge_back_kernel(me_ref, grad_ref, pre_ref, send_ref, recv_ref, w_ref, out_ref, *refs):
            nodes = refs[:M]
            dpre_out, outs = refs[M], refs[M + 1 : M + 1 + n_rep]
            second, parts = refs[M + 1 + n_rep :]
            me = me_ref[0]
            for k in range(M):
                second[rows_at(me ^ k, R), :] = nodes[k][...]
            for i in range(E // T):
                at = slice(i * T, (i + 1) * T)
                got = dot(recv_ref[at, :], second[...])
                cot = (grad_ref[at, :].astype(F32) + got).astype(BF)
                dpre_out[at, :] = (dot_t(cot, out_ref[...]) * silu_slope(pre_ref[at, :])).astype(BF)
            for i in range(NH // T):
                at = slice(i * T, (i + 1) * T)
                sent = dot(send_ref[at, :], dpre_out[...]).astype(BF)
                halo = dot_t(sent, w_ref[D : 2 * D, :]).astype(BF)
                for j in range(M):
                    parts[j, at, :] = halo[:, j * C : (j + 1) * C]
            for kr in range(n_rep):
                for kf in range(n_feat):
                    outs[kr][kf] = parts[me ^ (kf * n_rep + kr)]

        edge_dpre, *halo_grads = call(
            edge_back_kernel,
            "edge_backward",
            me1,
            [edge_grad, edge_pre, sht_hot, r_hot, in_full, out_full] + second_parts,
            [shape((E, D))] + [shape((n_feat, NH, C))] * n_rep,
            scratch=[pltpu.VMEM((N, D), BF), pltpu.VMEM((M, NH, C), BF)],
            flops=2 * E * D * (N + D + NH) + 2 * NH * D * D,
        )
        halo_grads = member_sums(halo_grads, me1, "halo_pairs")

        def local_back_kernel(me_ref, dpre_ref, send_ref, recv_ref, w_ref, first_ref, *refs):
            outs, (total, parts) = refs[:n_rep], refs[n_rep:]
            me = me_ref[0]
            for i in range(N // T):
                at = slice(i * T, (i + 1) * T)
                sent = dot(send_ref[at, :], dpre_ref[...]).astype(BF)
                got = dot(recv_ref[at, :], dpre_ref[...]).astype(BF)
                total[at, :] = dot_t(sent, w_ref[D : 2 * D, :]) + dot_t(got, w_ref[2 * D :, :])
            total[rows_at(me, R), :] += first_ref[...]
            for j in range(M):
                parts[j] = total[:, j * C : (j + 1) * C].astype(BF)
            for kr in range(n_rep):
                for kf in range(n_feat):
                    outs[kr][kf] = parts[me ^ (kf * n_rep + kr)]

        local_grads = call(
            local_back_kernel,
            "local_backward",
            me1,
            [edge_dpre, slt_hot, rt_hot, in_full, node_first],
            [shape((n_feat, N, C))] * n_rep,
            scratch=[pltpu.VMEM((N, D), F32), pltpu.VMEM((M, N, C), BF)],
            flops=4 * E * D * N + 4 * N * D * D,
        )
        local_grads = member_sums(local_grads, me1, "local_pairs")

        def halo_sum_kernel(me_ref, *refs):
            total = refs[0][...].astype(F32)
            for k in range(1, n_feat):
                total += refs[k][...].astype(F32)
            for j in range(n_dom):
                refs[n_feat + j][...] = total[j * H : (j + 1) * H].astype(BF)

        halo_back = call(halo_sum_kernel, "halo_sums", me1, halo_grads, [shape((H, C))] * n_dom)
        halo_back = dom_trade(halo_back)

        def owed_kernel(me_ref, halo_ref, table_ref, *refs):
            local, back = refs[:n_feat], refs[n_feat : n_feat + n_dom]
            first, second = refs[n_feat + n_dom : -n_dom], refs[-n_dom:]
            total = local[0][...].astype(F32)
            for k in range(1, n_feat):
                total += local[k][...].astype(F32)
            rows = stack([back[j][...] for j in range(n_dom)])
            cot = (total + dot(hot_columns(halo_ref[...], N), rows)).astype(BF)
            for k in range(M):
                owed = dot(hot_rows(table_ref[k, 1:2, :], N), cot).astype(BF)
                outs, at = (first, k) if k < n_rep else (second, k - n_rep)
                for j in range(n_dom):
                    outs[j][at * S : (at + 1) * S, :] = owed[j * S : (j + 1) * S]

        owed = call(
            owed_kernel,
            "owed_rows",
            me1,
            [halo_row, slots] + local_grads + halo_back,
            [shape((n_rep * S, C))] * n_dom + [shape((len(others) * S, C))] * n_dom,
            flops=2 * M * NS * N * C,
        )
        far_owed = dom_trade(owed[n_dom:])
        near_owed = dom_trade(owed[:n_dom])

        def cotangents(table_ref, slope_ref, arrived, at, k):
            rows = stack([arrived[j][at * S : (at + 1) * S, :] for j in range(n_dom)])
            cot = dot(hot_columns(table_ref[k, 0:1, :], G), rows)
            return (cot * slope_ref[k]).astype(BF)

        def grid_back(name, members, back, after):
            def kernel(me_ref, slope_ref, table_ref, *refs):
                outs = refs[n_dom + len(after) :]
                for at, k in enumerate(members):
                    outs[at][...] = cotangents(table_ref, slope_ref, refs[:n_dom], at, k)

            return call(
                kernel,
                name,
                me1,
                [grid_slope, slots] + back + after,
                [shape((G, C))] * len(members),
                flops=2 * len(members) * G * NS * C,
                unread=range(2 + n_dom, 2 + n_dom + len(after)),
            )

        far_dpre = grid_back("grid_back_far", others, far_owed, [])
        near_dpre = grid_back("grid_back_near", near, near_owed, far_dpre[:1])
        far_dpre = [member_swap(x, k) for x, k in zip(far_dpre, others)]

        def far_join_kernel(me_ref, *refs):
            for at in range(len(others)):
                refs[-1][at] = refs[at][...]

        far_dpre = call(
            far_join_kernel,
            "far_join",
            me1,
            far_dpre + near_dpre[:1],
            [shape((len(others), G, C))],
            unread=(len(others),),
        )
        near_dpre = [member_swap(x, k) if k else x for x, k in zip(near_dpre, near)]

        def adjoint_kernel(me_ref, enc_ref, far_ref, *refs):
            cols, (out, parts) = refs[:n_rep], refs[n_rep:]
            for k in range(M):
                parts[me_ref[0] ^ k] = cols[k][...] if k < n_rep else far_ref[k - n_rep]
            out[...] = dot_t(lanes([parts[j] for j in range(M)]), enc_ref[...])

        return call(
            adjoint_kernel,
            "adjoint",
            me1,
            [enc_full] + far_dpre + near_dpre,
            [shape((G, D), F32)],
            scratch=[pltpu.VMEM((M, G, C), BF)],
            flops=2 * G * D * D,
        )[0]

    return per_device


def solution(mesh):
    return jax.shard_map(
        make_per_device(mesh),
        mesh=mesh,
        in_specs=(
            P(("ens", "dom", "feat", "rep"), None),
            P("dom", None),
            P(("dom", "feat", "rep"), None),
            P(("feat", "rep"), None),
            P(("feat", "rep"), None),
            P(("feat", "rep"), None),
            P(("feat", "rep"), None),
            P(("feat", "rep"), None),
            P(("ens", "dom"), None),
            P(("ens", "dom", "feat", "rep"), None),
            P("dom", None, None),
            P(("dom", "feat", "rep")),
            P(("dom", "feat", "rep")),
            P(("dom", "feat", "rep"), None, None),
            P(("dom", "feat", "rep"), None, None),
        ),
        out_specs=P(("ens", "dom", "feat", "rep"), None),
        check_vma=False,
    )
```

```python
import jax
import jax.numpy as jnp
from jax import lax
from jax.experimental import pallas as pl
from jax.experimental.pallas import tpu as pltpu
from jax.sharding import PartitionSpec as P

BF = jnp.bfloat16
F32 = jnp.float32
SMEM = pl.BlockSpec(memory_space=pltpu.SMEM)
VMEM = pl.BlockSpec(memory_space=pltpu.VMEM)
HBM = pl.BlockSpec(memory_space=pltpu.HBM)
ANY = pl.BlockSpec(memory_space=pl.ANY)


def dot(a, b):
    return jnp.dot(a, b, preferred_element_type=F32)


def dot_t(a, b):
    return lax.dot_general(a, b, (((1,), (1,)), ((), ())), preferred_element_type=F32)


def silu_slope(values):
    logistic = jax.nn.sigmoid(values)
    return logistic * (1.0 + values * (1.0 - logistic))


def to_column(row):
    return jnp.transpose(jnp.broadcast_to(row, (8, row.shape[1])))[:, :1]


def hot_rows(row, depth):
    length = row.shape[1]
    return (to_column(row) == lax.broadcasted_iota(jnp.int32, (length, depth), 1)).astype(BF)


def hot_columns(row, depth):
    length = row.shape[1]
    return (row == lax.broadcasted_iota(jnp.int32, (depth, length), 0)).astype(BF)


def column_pick(me, depth, cols):
    at = lax.broadcasted_iota(jnp.int32, (depth, cols), 0) - me * cols
    return (at == lax.broadcasted_iota(jnp.int32, (depth, cols), 1)).astype(BF)


def rows_at(index, count):
    return pl.ds(pl.multiple_of(index * count, count), count)


def lanes(parts):
    return parts[0] if len(parts) == 1 else jnp.concatenate(parts, axis=1)


def stack(parts):
    return parts[0] if len(parts) == 1 else jnp.concatenate(parts, axis=0)


def call(body, name, me, ins, outs, scratch=(), flops=0, far=(), unread=()):
    size = lambda s: s.size * s.dtype.itemsize
    moved = sum(size(x) for x in ins) + sum(size(x) for x in outs)
    result = pl.pallas_call(
        body,
        out_shape=list(outs),
        in_specs=[SMEM] + [HBM if i in far else ANY if i in unread else VMEM for i in range(len(ins))],
        out_specs=[VMEM] * len(outs),
        scratch_shapes=list(scratch),
        compiler_params=pltpu.CompilerParams(vmem_limit_bytes=24 * 2**20),
        cost_estimate=pl.CostEstimate(flops=flops, bytes_accessed=moved, transcendentals=0),
        name=name,
    )(me, *[pltpu.with_memory_space_constraint(x, pltpu.HBM) if i in far else x for i, x in enumerate(ins)])
    return list(result)


def shape(dims, dtype=BF):
    return jax.ShapeDtypeStruct(tuple(dims), dtype)


def make_per_device(mesh):
    n_dom, n_feat, n_rep = mesh.shape["dom"], mesh.shape["feat"], mesh.shape["rep"]
    M = n_feat * n_rep

    def member_swap(x, k):
        return lax.ppermute(x, ("feat", "rep"), [(i, i ^ k) for i in range(M)])

    def dom_swap(x, k):
        return lax.ppermute(x, "dom", [(i, i ^ k) for i in range(n_dom)])

    def member_gather(x):
        return [x] + [member_swap(x, k) for k in range(1, M)]

    def member_gather_chips(x):
        parts = [None] * M
        for kf in range(n_feat):
            parts[kf * n_rep] = member_swap(x, kf * n_rep) if kf else x
        for kf in range(n_feat):
            for kr in range(1, n_rep):
                parts[kf * n_rep + kr] = member_swap(parts[kf * n_rep], kr)
        return parts

    def member_trade(parts):
        return [parts[0]] + [member_swap(parts[k], k) for k in range(1, M)]

    def member_sums(parts, me1, name):
        arrived = [parts[0]] + [member_swap(parts[kr], kr) for kr in range(1, n_rep)]

        def add_kernel(me_ref, *refs):
            for kf in range(n_feat):
                total = refs[0][kf].astype(F32)
                for kr in range(1, n_rep):
                    total += refs[kr][kf].astype(F32)
                refs[n_rep + kf][...] = total.astype(BF)

        halves = call(add_kernel, name, me1, arrived, [shape(parts[0].shape[1:])] * n_feat)
        return [halves[0]] + [member_swap(halves[kf], kf * n_rep) for kf in range(1, n_feat)]

    def dom_trade(parts):
        return [parts[0]] + [dom_swap(parts[k], k) for k in range(1, n_dom)]

    def per_device(
        grid_state,
        mesh_base,
        edge_state,
        enc_weight,
        edge_in_weight,
        edge_out_weight,
        node_in_weight,
        node_out_weight,
        node_grad,
        edge_grad,
        halo_rows,
        edge_send,
        edge_recv,
        grid_send,
        grid_recv,
    ):
        D = mesh_base.shape[1]
        N = mesh_base.shape[0]
        E = edge_state.shape[0]
        G = grid_state.shape[0]
        H = halo_rows.shape[2]
        S = grid_send.shape[2]
        NH = n_dom * H
        NS = n_dom * S
        C = D // M
        R = N // M
        T = 256
        PACK = 16
        assert NS == D
        rows_enc, rows_in, rows_out, rows_node = (
            enc_weight.shape[0],
            edge_in_weight.shape[0],
            edge_out_weight.shape[0],
            node_in_weight.shape[0],
        )
        rows_edge, rows_mlp = rows_in + rows_out, rows_node + rows_out
        me = lax.axis_index(("feat", "rep")).astype(jnp.int32)
        dom = lax.axis_index("dom").astype(jnp.int32)
        me1 = me.reshape(1)

        where = jnp.stack([me, dom])
        recv_row = edge_recv.reshape(1, E)

        def tables_kernel(where_ref, enc_ref, gs_ref, gr_ref, halo_ref, send_ref, *refs):
            pack_out, halo_out, send_out, gs, gr, halo, sent, sems = refs
            dom = where_ref[1]
            pairs = [
                (enc_ref, pack_out.at[:rows_enc, :]),
                (gs_ref.at[0], gs),
                (gr_ref.at[0], gr),
                (halo_ref.at[0], halo),
                (send_ref, sent),
            ]
            copies = [pltpu.make_async_copy(a, b, sems.at[i]) for i, (a, b) in enumerate(pairs)]
            for copy in copies:
                copy.start()
            for copy in copies:
                copy.wait()
            order = [pl.ds(dom ^ j, 1) for j in range(n_dom)]
            sends, recvs = lanes([gs[at, :] for at in order]), lanes([gr[at, :] for at in order])
            halo_out[...] = lanes([halo[at, :] for at in order])
            fill = jnp.zeros((PACK - 3, NS), jnp.int32)
            rows = stack([sends, recvs // 2, recvs % 2, fill])
            pack_out[rows_enc:, :] = rows.astype(F32).astype(BF)
            value = sent[...]
            away = jnp.maximum(value - N, 0)
            peer = away // H
            send_out[...] = jnp.where(value < N, value, N + (peer ^ dom) * H + (away - peer * H))

        pack, halo_row, send_row = call(
            tables_kernel,
            "tables",
            where,
            [enc_weight, grid_send, grid_recv, halo_rows, edge_send.reshape(1, E)],
            [shape((rows_enc + PACK, D)), shape((1, NH), jnp.int32), shape((1, E), jnp.int32)],
            scratch=[
                pltpu.VMEM((n_dom, S), jnp.int32),
                pltpu.VMEM((n_dom, S), jnp.int32),
                pltpu.VMEM((n_dom, H), jnp.int32),
                pltpu.VMEM((1, E), jnp.int32),
                pltpu.SemaphoreType.DMA((5,)),
            ],
            far=range(5),
        )

        def hots_kernel(me_ref, state_ref, send_ref, recv_ref, *refs):
            sl_out, sh_out, r_out, slt_out, sht_out, rt_out, state_out, sem = refs
            copy = pltpu.make_async_copy(state_ref, state_out, sem)
            copy.start()
            for i in range(E // T):
                at = slice(i * T, (i + 1) * T)
                sent, got = send_ref[:, at], recv_ref[:, at]
                sl_out[at, :] = hot_rows(sent, N)
                sh_out[at, :] = hot_rows(sent - N, NH)
                r_out[at, :] = hot_rows(got, N)
                slt_out[:, at] = hot_columns(sent, N)
                sht_out[:, at] = hot_columns(sent - N, NH)
                rt_out[:, at] = hot_columns(got, N)
            copy.wait()

        sl_hot, sh_hot, r_hot, slt_hot, sht_hot, rt_hot, state_own = call(
            hots_kernel,
            "edge_hots",
            me1,
            [grid_state, send_row, recv_row],
            [shape((E, N)), shape((E, NH)), shape((E, N)), shape((N, E)), shape((NH, E)), shape((N, E))]
            + [shape((G, D))],
            scratch=[pltpu.SemaphoreType.DMA(())],
            far=(0,),
        )

        state_parts = [state_own] + [None] * (M - 1)
        for kf in range(n_feat):
            if kf:
                state_parts[kf * n_rep] = member_swap(grid_state, kf * n_rep)
            for kr in range(1, n_rep):
                state_parts[kf * n_rep + kr] = member_swap(state_parts[kf * n_rep], kr)
        pack_parts = member_gather_chips(pack)

        firsts = [kf * n_rep for kf in range(1, n_feat)]

        def stacked(pairs, out, sems):
            copies, at = [], 0
            for i, ref in enumerate(pairs):
                copies.append(pltpu.make_async_copy(ref, out.at[at : at + ref.shape[0], :], sems.at[i]))
                at += ref.shape[0]
            return copies

        def grid_kernel(me_ref, *refs):
            states, packs = refs[:M], refs[M : 2 * M]
            enc_out, slope_out, table_out, weights_out = refs[2 * M + 4 : 2 * M + 8]
            outs, sems = refs[2 * M + 8 : 2 * M + 8 + n_dom], refs[-1]
            me = me_ref[0]
            weight_copies = stacked(refs[2 * M : 2 * M + 4], weights_out, sems)
            for each in weight_copies:
                each.start()
            for k in range(M):
                enc_out[rows_at(me ^ k, rows_enc), :] = packs[k][:rows_enc, :]
                rows = packs[k][rows_enc:, :].astype(F32).astype(jnp.int32)
                table_out[k, 0:1, :] = rows[0:1]
                table_out[k, 1:2, :] = 2 * rows[1:2] + rows[2:3]
            enc_cols = dot(enc_out[...], column_pick(me, D, C)).astype(BF)
            for k in range(M):
                pre = dot(states[k][...], enc_cols)
                logistic = jax.nn.sigmoid(pre)
                slope_out[k] = logistic * (1.0 + pre * (1.0 - logistic))
                message = (pre * logistic).astype(BF)
                rows = dot(hot_rows(table_out[k, 0:1, :], G), message).astype(BF)
                for j in range(n_dom):
                    outs[j][k * S : (k + 1) * S, :] = rows[j * S : (j + 1) * S]
            for each in weight_copies:
                each.wait()

        enc_full, grid_slope, slots, weights_own, *outgoing = call(
            grid_kernel,
            "grid_messages",
            me1,
            state_parts + pack_parts + [edge_in_weight, edge_out_weight, node_in_weight, node_out_weight],
            [shape((D, D)), shape((M, G, C), F32), shape((M, 2, NS), jnp.int32), shape((rows_edge + rows_mlp, D))]
            + [shape((M * S, C))] * n_dom,
            scratch=[pltpu.SemaphoreType.DMA((4,))],
            flops=2 * M * G * D * C + 2 * M * NS * G * C,
            far=range(2 * M, 2 * M + 4),
        )
        incoming = dom_trade(outgoing)
        near, others = range(n_rep), range(n_rep, M)
        weight_chips = [weights_own] + [member_swap(weights_own, k) for k in firsts]

        def encode_kernel(me_ref, base_ref, table_ref, *refs):
            arrived, state_out = refs[:n_dom], refs[-1]
            total = dot(base_ref[...], column_pick(me_ref[0], D, C))
            for k in range(M):
                rows = stack([arrived[j][k * S : (k + 1) * S, :] for j in range(n_dom)])
                total += dot(hot_columns(table_ref[k, 1:2, :], N), rows)
            state_out[...] = total.astype(BF)

        state_cols = call(
            encode_kernel,
            "encode",
            me1,
            [mesh_base, slots] + incoming,
            [shape((N, C))],
            flops=2 * M * N * NS * C,
        )[0]
        state_chips = [state_cols] + [member_swap(state_cols, k) for k in firsts]

        def halo_kernel(me_ref, state_ref, halo_ref, *outs):
            rows = dot(hot_rows(halo_ref[...], N), state_ref[...]).astype(BF)
            for j in range(n_dom):
                outs[j][...] = rows[j * H : (j + 1) * H]

        halo_out = call(
            halo_kernel,
            "halo_rows",
            me1,
            [state_cols, halo_row],
            [shape((H, C))] * n_dom,
            flops=2 * N * NH * C,
        )
        halo_in = dom_trade(halo_out)
        core_swaps = lambda x: [x] + [member_swap(x, kr) for kr in range(1, n_rep)]

        def pair_kernel(me_ref, *refs):
            for kf in range(n_feat):
                refs[-1][kf] = refs[kf][...]

        def join_kernel(me_ref, *refs):
            halo, chips, weights = refs[:n_dom], refs[n_dom : n_dom + n_feat], refs[n_dom + n_feat : -4]
            halo_out_ref, pair_out, edge_out, node_out = refs[-4:]
            for j in range(n_dom):
                halo_out_ref[j * H : (j + 1) * H, :] = halo[j][...]
            for kf in range(n_feat):
                pair_out[kf] = chips[kf][...]
                edge_out[kf] = weights[kf][:rows_edge, :]
                node_out[kf] = weights[kf][rows_edge:, :]

        halo_cols, state_pair, edge_pair, node_pair = call(
            join_kernel,
            "halo_join",
            me1,
            halo_in + state_chips + weight_chips,
            [shape((NH, C)), shape((n_feat, N, C))]
            + [shape((n_feat, rows_edge, D)), shape((n_feat, rows_mlp, D))],
        )
        halo_chips = [halo_cols] + [member_swap(halo_cols, k) for k in firsts]
        state_pairs = core_swaps(state_pair)
        edge_pairs = core_swaps(edge_pair)
        node_pairs = core_swaps(node_pair)

        def local_kernel(me_ref, es_ref, send_ref, recv_ref, *refs):
            cols, weights = refs[:n_rep], refs[n_rep : 2 * n_rep]
            pre_out, state_out, w_out, out_out, parts = refs[2 * n_rep :]
            me = me_ref[0]
            for k in range(M):
                kf, kr = divmod(k, n_rep)
                parts[me ^ k] = cols[kr][kf]
                w_out[rows_at(me ^ k, rows_in), :] = weights[kr][kf, :rows_in, :]
                out_out[rows_at(me ^ k, rows_out), :] = weights[kr][kf, rows_in:, :]
            state_out[...] = lanes([parts[j] for j in range(M)])
            for i in range(E // T):
                at = slice(i * T, (i + 1) * T)
                sent = dot(send_ref[at, :], state_out[...]).astype(BF)
                got = dot(recv_ref[at, :], state_out[...]).astype(BF)
                pre_out[at, :] = (
                    dot(es_ref[at, :], w_out[:D, :])
                    + dot(sent, w_out[D : 2 * D, :])
                    + dot(got, w_out[2 * D :, :])
                )

        local_pre, mesh_state, in_full, out_full = call(
            local_kernel,
            "edge_local",
            me1,
            [edge_state, sl_hot, r_hot] + state_pairs + edge_pairs,
            [shape((E, D), F32), shape((N, D)), shape((3 * D, D)), shape((D, D))],
            scratch=[pltpu.VMEM((M, N, C), BF)],
            flops=2 * E * D * (3 * D + 2 * N),
        )

        halo_pair = call(
            pair_kernel,
            "halo_pair",
            me1,
            halo_chips + [local_pre],
            [shape((n_feat, NH, C))],
            unread=(n_feat,),
        )[0]
        halo_pairs = core_swaps(halo_pair)

        def edge_kernel(me_ref, local_ref, es_ref, send_ref, recv_ref, w_ref, out_ref, *refs):
            cols = refs[:n_rep]
            pre_out, outs = refs[n_rep], refs[n_rep + 1 : 2 * n_rep + 1]
            parts, halo, new, total = refs[2 * n_rep + 1 :]
            me = me_ref[0]
            for k in range(M):
                kf, kr = divmod(k, n_rep)
                parts[me ^ k] = cols[kr][kf]
            halo[...] = lanes([parts[j] for j in range(M)])
            for i in range(E // T):
                at = slice(i * T, (i + 1) * T)
                sent = dot(send_ref[at, :], halo[...]).astype(BF)
                pre = local_ref[at, :] + dot(sent, w_ref[D : 2 * D, :])
                pre_out[at, :] = pre
                hidden = (pre * jax.nn.sigmoid(pre)).astype(BF)
                new[at, :] = (es_ref[at, :].astype(F32) + dot(hidden, out_ref[...])).astype(BF)
            for i in range(N // T):
                at = slice(i * T, (i + 1) * T)
                total[at, :] = dot(recv_ref[at, :], new[...]).astype(BF)
            for kr in range(n_rep):
                for kf in range(n_feat):
                    outs[kr][kf] = total[rows_at(me ^ (kf * n_rep + kr), R), :]

        edge_pre, *sums = call(
            edge_kernel,
            "edge_update",
            me1,
            [local_pre, edge_state, sh_hot, rt_hot, in_full, out_full] + halo_pairs,
            [shape((E, D), F32)] + [shape((n_feat, R, D))] * n_rep,
            scratch=[
                pltpu.VMEM((M, NH, C), BF),
                pltpu.VMEM((NH, D), BF),
                pltpu.VMEM((E, D), BF),
                pltpu.VMEM((N, D), BF),
            ],
            flops=2 * E * D * (NH + D + D + N),
        )
        sums = member_sums(sums, me1, "node_sums")

        def node_ahead_kernel(me_ref, state_ref, grad_ref, *refs):
            weights = refs[:n_rep]
            node_in_full, pre_out, cot_out, node_out_full = refs[n_rep + 1 :]
            me = me_ref[0]
            for k in range(M):
                kf, kr = divmod(k, n_rep)
                node_in_full[rows_at(me ^ k, rows_node), :] = weights[kr][kf, :rows_node, :]
                node_out_full[rows_at(me ^ k, rows_out), :] = weights[kr][kf, rows_node:, :]
            mine = rows_at(me, R)
            pre_out[...] = dot(state_ref[mine, :], node_in_full[:D, :])
            cot_out[...] = dot_t(grad_ref[mine, :], node_out_full[...])

        node_in_full, node_pre, node_cot = call(
            node_ahead_kernel,
            "node_ahead",
            me1,
            [mesh_state, node_grad] + node_pairs + [sums[0]],
            [shape((2 * D, D)), shape((R, D), F32), shape((R, D), F32)],
            scratch=[pltpu.VMEM((D, D), BF)],
            flops=4 * R * D * D,
            unread=(2 + n_rep,),
        )

        def node_kernel(me_ref, pre_ref, cot_ref, w_ref, grad_ref, *refs):
            first_out, second_out = refs[n_feat:]
            total = refs[0][...].astype(F32)
            for k in range(1, n_feat):
                total += refs[k][...].astype(F32)
            pre = pre_ref[...] + dot(total.astype(BF), w_ref[D:, :])
            dpre = (cot_ref[...] * silu_slope(pre)).astype(BF)
            second_out[...] = dot_t(dpre, w_ref[D:, :]).astype(BF)
            mine = grad_ref[rows_at(me_ref[0], R), :].astype(F32)
            first_out[...] = mine + dot_t(dpre, w_ref[:D, :])

        node_first, node_second = call(
            node_kernel,
            "node_backward",
            me1,
            [node_pre, node_cot, node_in_full, node_grad] + sums,
            [shape((R, D), F32), shape((R, D))],
            flops=6 * R * D * D,
        )
        second_parts = member_gather_chips(node_second)

        def edge_back_kernel(me_ref, grad_ref, pre_ref, send_ref, recv_ref, w_ref, out_ref, *refs):
            nodes = refs[:M]
            dpre_out, outs = refs[M], refs[M + 1 : M + 1 + n_rep]
            second, parts = refs[M + 1 + n_rep :]
            me = me_ref[0]
            for k in range(M):
                second[rows_at(me ^ k, R), :] = nodes[k][...]
            for i in range(E // T):
                at = slice(i * T, (i + 1) * T)
                got = dot(recv_ref[at, :], second[...])
                cot = (grad_ref[at, :].astype(F32) + got).astype(BF)
                dpre_out[at, :] = (dot_t(cot, out_ref[...]) * silu_slope(pre_ref[at, :])).astype(BF)
            for i in range(NH // T):
                at = slice(i * T, (i + 1) * T)
                sent = dot(send_ref[at, :], dpre_out[...]).astype(BF)
                halo = dot_t(sent, w_ref[D : 2 * D, :]).astype(BF)
                for j in range(M):
                    parts[j, at, :] = halo[:, j * C : (j + 1) * C]
            for kr in range(n_rep):
                for kf in range(n_feat):
                    outs[kr][kf] = parts[me ^ (kf * n_rep + kr)]

        edge_dpre, *halo_grads = call(
            edge_back_kernel,
            "edge_backward",
            me1,
            [edge_grad, edge_pre, sht_hot, r_hot, in_full, out_full] + second_parts,
            [shape((E, D))] + [shape((n_feat, NH, C))] * n_rep,
            scratch=[pltpu.VMEM((N, D), BF), pltpu.VMEM((M, NH, C), BF)],
            flops=2 * E * D * (N + D + NH) + 2 * NH * D * D,
        )
        halo_grads = member_sums(halo_grads, me1, "halo_pairs")

        def local_back_kernel(me_ref, dpre_ref, send_ref, recv_ref, w_ref, first_ref, *refs):
            outs, (total, parts) = refs[:n_rep], refs[n_rep:]
            me = me_ref[0]
            for i in range(N // T):
                at = slice(i * T, (i + 1) * T)
                sent = dot(send_ref[at, :], dpre_ref[...]).astype(BF)
                got = dot(recv_ref[at, :], dpre_ref[...]).astype(BF)
                total[at, :] = dot_t(sent, w_ref[D : 2 * D, :]) + dot_t(got, w_ref[2 * D :, :])
            total[rows_at(me, R), :] += first_ref[...]
            for j in range(M):
                parts[j] = total[:, j * C : (j + 1) * C].astype(BF)
            for kr in range(n_rep):
                for kf in range(n_feat):
                    outs[kr][kf] = parts[me ^ (kf * n_rep + kr)]

        local_grads = call(
            local_back_kernel,
            "local_backward",
            me1,
            [edge_dpre, slt_hot, rt_hot, in_full, node_first],
            [shape((n_feat, N, C))] * n_rep,
            scratch=[pltpu.VMEM((N, D), F32), pltpu.VMEM((M, N, C), BF)],
            flops=4 * E * D * N + 4 * N * D * D,
        )
        local_grads = member_sums(local_grads, me1, "local_pairs")

        def halo_sum_kernel(me_ref, *refs):
            total = refs[0][...].astype(F32)
            for k in range(1, n_feat):
                total += refs[k][...].astype(F32)
            for j in range(n_dom):
                refs[n_feat + j][...] = total[j * H : (j + 1) * H].astype(BF)

        halo_back = call(halo_sum_kernel, "halo_sums", me1, halo_grads, [shape((H, C))] * n_dom)
        halo_back = dom_trade(halo_back)

        def owed_kernel(me_ref, halo_ref, table_ref, *refs):
            local, back = refs[:n_feat], refs[n_feat : n_feat + n_dom]
            first, second = refs[n_feat + n_dom : -n_dom], refs[-n_dom:]
            total = local[0][...].astype(F32)
            for k in range(1, n_feat):
                total += local[k][...].astype(F32)
            rows = stack([back[j][...] for j in range(n_dom)])
            cot = (total + dot(hot_columns(halo_ref[...], N), rows)).astype(BF)
            for k in range(M):
                owed = dot(hot_rows(table_ref[k, 1:2, :], N), cot).astype(BF)
                outs, at = (first, k) if k < n_rep else (second, k - n_rep)
                for j in range(n_dom):
                    outs[j][at * S : (at + 1) * S, :] = owed[j * S : (j + 1) * S]

        owed = call(
            owed_kernel,
            "owed_rows",
            me1,
            [halo_row, slots] + local_grads + halo_back,
            [shape((n_rep * S, C))] * n_dom + [shape((len(others) * S, C))] * n_dom,
            flops=2 * M * NS * N * C,
        )
        far_owed = dom_trade(owed[n_dom:])
        near_owed = dom_trade(owed[:n_dom])

        def cotangents(table_ref, slope_ref, arrived, at, k):
            rows = stack([arrived[j][at * S : (at + 1) * S, :] for j in range(n_dom)])
            cot = dot(hot_columns(table_ref[k, 0:1, :], G), rows)
            return (cot * slope_ref[k]).astype(BF)

        def grid_back(name, members, back, after):
            def kernel(me_ref, slope_ref, table_ref, *refs):
                outs = refs[n_dom + len(after) :]
                for at, k in enumerate(members):
                    outs[at][...] = cotangents(table_ref, slope_ref, refs[:n_dom], at, k)

            return call(
                kernel,
                name,
                me1,
                [grid_slope, slots] + back + after,
                [shape((G, C))] * len(members),
                flops=2 * len(members) * G * NS * C,
                unread=range(2 + n_dom, 2 + n_dom + len(after)),
            )

        far_dpre = grid_back("grid_back_far", others, far_owed, [])
        near_dpre = grid_back("grid_back_near", near, near_owed, far_dpre[:1])
        far_dpre = [member_swap(x, k) for x, k in zip(far_dpre, others)]

        def far_join_kernel(me_ref, *refs):
            for at in range(len(others)):
                refs[-1][at] = refs[at][...]

        far_dpre = call(
            far_join_kernel,
            "far_join",
            me1,
            far_dpre + near_dpre[:1],
            [shape((len(others), G, C))],
            unread=(len(others),),
        )
        near_dpre = [member_swap(x, k) if k else x for x, k in zip(near_dpre, near)]

        def adjoint_kernel(me_ref, enc_ref, far_ref, *refs):
            cols, (out, parts) = refs[:n_rep], refs[n_rep:]
            for k in range(M):
                parts[me_ref[0] ^ k] = cols[k][...] if k < n_rep else far_ref[k - n_rep]
            out[...] = dot_t(lanes([parts[j] for j in range(M)]), enc_ref[...])

        return call(
            adjoint_kernel,
            "adjoint",
            me1,
            [enc_full] + far_dpre + near_dpre,
            [shape((G, D), F32)],
            scratch=[pltpu.VMEM((M, G, C), BF)],
            flops=2 * G * D * D,
        )[0]

    return per_device


def solution(mesh):
    return jax.shard_map(
        make_per_device(mesh),
        mesh=mesh,
        in_specs=(
            P(("ens", "dom", "feat", "rep"), None),
            P("dom", None),
            P(("dom", "feat", "rep"), None),
            P(("feat", "rep"), None),
            P(("feat", "rep"), None),
            P(("feat", "rep"), None),
            P(("feat", "rep"), None),
            P(("feat", "rep"), None),
            P(("ens", "dom"), None),
            P(("ens", "dom", "feat", "rep"), None),
            P("dom", None, None),
            P(("dom", "feat", "rep")),
            P(("dom", "feat", "rep")),
            P(("dom", "feat", "rep"), None, None),
            P(("dom", "feat", "rep"), None, None),
        ),
        out_specs=P(("ens", "dom", "feat", "rep"), None),
        check_vma=False,
    )
```

```python
import jax
import jax.numpy as jnp
from jax import lax
from jax.experimental import pallas as pl
from jax.experimental.pallas import tpu as pltpu
from jax.sharding import PartitionSpec as P

BF = jnp.bfloat16
F32 = jnp.float32
SMEM = pl.BlockSpec(memory_space=pltpu.SMEM)
VMEM = pl.BlockSpec(memory_space=pltpu.VMEM)
HBM = pl.BlockSpec(memory_space=pltpu.HBM)
ANY = pl.BlockSpec(memory_space=pl.ANY)


def dot(a, b):
    return jnp.dot(a, b, preferred_element_type=F32)


def dot_t(a, b):
    return lax.dot_general(a, b, (((1,), (1,)), ((), ())), preferred_element_type=F32)


def silu_slope(values):
    logistic = jax.nn.sigmoid(values)
    return logistic * (1.0 + values * (1.0 - logistic))


def to_column(row):
    return jnp.transpose(jnp.broadcast_to(row, (8, row.shape[1])))[:, :1]


def hot_rows(row, depth):
    length = row.shape[1]
    return (to_column(row) == lax.broadcasted_iota(jnp.int32, (length, depth), 1)).astype(BF)


def hot_columns(row, depth):
    length = row.shape[1]
    return (row == lax.broadcasted_iota(jnp.int32, (depth, length), 0)).astype(BF)


def column_pick(me, depth, cols):
    at = lax.broadcasted_iota(jnp.int32, (depth, cols), 0) - me * cols
    return (at == lax.broadcasted_iota(jnp.int32, (depth, cols), 1)).astype(BF)


def rows_at(index, count):
    return pl.ds(pl.multiple_of(index * count, count), count)


def lanes(parts):
    return parts[0] if len(parts) == 1 else jnp.concatenate(parts, axis=1)


def stack(parts):
    return parts[0] if len(parts) == 1 else jnp.concatenate(parts, axis=0)


def call(body, name, me, ins, outs, scratch=(), flops=0, far=(), unread=()):
    size = lambda s: s.size * s.dtype.itemsize
    moved = sum(size(x) for x in ins) + sum(size(x) for x in outs)
    result = pl.pallas_call(
        body,
        out_shape=list(outs),
        in_specs=[SMEM] + [HBM if i in far else ANY if i in unread else VMEM for i in range(len(ins))],
        out_specs=[VMEM] * len(outs),
        scratch_shapes=list(scratch),
        compiler_params=pltpu.CompilerParams(vmem_limit_bytes=24 * 2**20),
        cost_estimate=pl.CostEstimate(flops=flops, bytes_accessed=moved, transcendentals=0),
        name=name,
    )(me, *[pltpu.with_memory_space_constraint(x, pltpu.HBM) if i in far else x for i, x in enumerate(ins)])
    return list(result)


def shape(dims, dtype=BF):
    return jax.ShapeDtypeStruct(tuple(dims), dtype)


def make_per_device(mesh):
    n_dom, n_feat, n_rep = mesh.shape["dom"], mesh.shape["feat"], mesh.shape["rep"]
    M = n_feat * n_rep

    def member_swap(x, k):
        return lax.ppermute(x, ("feat", "rep"), [(i, i ^ k) for i in range(M)])

    def dom_swap(x, k):
        return lax.ppermute(x, "dom", [(i, i ^ k) for i in range(n_dom)])

    def member_gather(x):
        return [x] + [member_swap(x, k) for k in range(1, M)]

    def member_gather_chips(x):
        parts = [None] * M
        for kf in range(n_feat):
            parts[kf * n_rep] = member_swap(x, kf * n_rep) if kf else x
        for kf in range(n_feat):
            for kr in range(1, n_rep):
                parts[kf * n_rep + kr] = member_swap(parts[kf * n_rep], kr)
        return parts

    def member_trade(parts):
        return [parts[0]] + [member_swap(parts[k], k) for k in range(1, M)]

    def member_sums(parts, me1, name):
        arrived = [parts[0]] + [member_swap(parts[kr], kr) for kr in range(1, n_rep)]

        def add_kernel(me_ref, *refs):
            for kf in range(n_feat):
                total = refs[0][kf].astype(F32)
                for kr in range(1, n_rep):
                    total += refs[kr][kf].astype(F32)
                refs[n_rep + kf][...] = total.astype(BF)

        halves = call(add_kernel, name, me1, arrived, [shape(parts[0].shape[1:])] * n_feat)
        return [halves[0]] + [member_swap(halves[kf], kf * n_rep) for kf in range(1, n_feat)]

    def dom_trade(parts):
        swapped = [dom_swap(parts[k], k) for k in reversed(range(1, n_dom))]
        return [parts[0]] + swapped[::-1]

    def far_first(parts):
        return [parts[0]] + list(parts[:0:-1])

    def per_device(
        grid_state,
        mesh_base,
        edge_state,
        enc_weight,
        edge_in_weight,
        edge_out_weight,
        node_in_weight,
        node_out_weight,
        node_grad,
        edge_grad,
        halo_rows,
        edge_send,
        edge_recv,
        grid_send,
        grid_recv,
    ):
        D = mesh_base.shape[1]
        N = mesh_base.shape[0]
        E = edge_state.shape[0]
        G = grid_state.shape[0]
        H = halo_rows.shape[2]
        S = grid_send.shape[2]
        NH = n_dom * H
        NS = n_dom * S
        C = D // M
        R = N // M
        T = 256
        PACK = 16
        assert NS == D
        rows_enc, rows_in, rows_out, rows_node = (
            enc_weight.shape[0],
            edge_in_weight.shape[0],
            edge_out_weight.shape[0],
            node_in_weight.shape[0],
        )
        rows_edge, rows_mlp = rows_in + rows_out, rows_node + rows_out
        me = lax.axis_index(("feat", "rep")).astype(jnp.int32)
        dom = lax.axis_index("dom").astype(jnp.int32)
        me1 = me.reshape(1)

        where = jnp.stack([me, dom])
        recv_row = edge_recv.reshape(1, E)

        def tables_kernel(where_ref, enc_ref, gs_ref, gr_ref, halo_ref, send_ref, *refs):
            pack_out, halo_out, send_out, gs, gr, halo, sent, sems = refs
            dom = where_ref[1]
            pairs = [
                (enc_ref, pack_out.at[:rows_enc, :]),
                (gs_ref.at[0], gs),
                (gr_ref.at[0], gr),
                (halo_ref.at[0], halo),
                (send_ref, sent),
            ]
            copies = [pltpu.make_async_copy(a, b, sems.at[i]) for i, (a, b) in enumerate(pairs)]
            for copy in copies:
                copy.start()
            for copy in copies:
                copy.wait()
            order = [pl.ds(dom ^ j, 1) for j in range(n_dom)]
            sends, recvs = lanes([gs[at, :] for at in order]), lanes([gr[at, :] for at in order])
            halo_out[...] = lanes([halo[at, :] for at in order])
            fill = jnp.zeros((PACK - 3, NS), jnp.int32)
            rows = stack([sends, recvs // 2, recvs % 2, fill])
            pack_out[rows_enc:, :] = rows.astype(F32).astype(BF)
            value = sent[...]
            away = jnp.maximum(value - N, 0)
            peer = away // H
            send_out[...] = jnp.where(value < N, value, N + (peer ^ dom) * H + (away - peer * H))

        pack, halo_row, send_row = call(
            tables_kernel,
            "tables",
            where,
            [enc_weight, grid_send, grid_recv, halo_rows, edge_send.reshape(1, E)],
            [shape((rows_enc + PACK, D)), shape((1, NH), jnp.int32), shape((1, E), jnp.int32)],
            scratch=[
                pltpu.VMEM((n_dom, S), jnp.int32),
                pltpu.VMEM((n_dom, S), jnp.int32),
                pltpu.VMEM((n_dom, H), jnp.int32),
                pltpu.VMEM((1, E), jnp.int32),
                pltpu.SemaphoreType.DMA((5,)),
            ],
            far=range(5),
        )

        def hots_kernel(me_ref, state_ref, send_ref, recv_ref, *refs):
            sl_out, sh_out, r_out, slt_out, sht_out, rt_out, state_out, sem = refs
            copy = pltpu.make_async_copy(state_ref, state_out, sem)
            copy.start()
            for i in range(E // T):
                at = slice(i * T, (i + 1) * T)
                sent, got = send_ref[:, at], recv_ref[:, at]
                sl_out[at, :] = hot_rows(sent, N)
                sh_out[at, :] = hot_rows(sent - N, NH)
                r_out[at, :] = hot_rows(got, N)
                slt_out[:, at] = hot_columns(sent, N)
                sht_out[:, at] = hot_columns(sent - N, NH)
                rt_out[:, at] = hot_columns(got, N)
            copy.wait()

        sl_hot, sh_hot, r_hot, slt_hot, sht_hot, rt_hot, state_own = call(
            hots_kernel,
            "edge_hots",
            me1,
            [grid_state, send_row, recv_row],
            [shape((E, N)), shape((E, NH)), shape((E, N)), shape((N, E)), shape((NH, E)), shape((N, E))]
            + [shape((G, D))],
            scratch=[pltpu.SemaphoreType.DMA(())],
            far=(0,),
        )

        state_parts = [state_own] + [None] * (M - 1)
        for kf in range(n_feat):
            if kf:
                state_parts[kf * n_rep] = member_swap(grid_state, kf * n_rep)
            for kr in range(1, n_rep):
                state_parts[kf * n_rep + kr] = member_swap(state_parts[kf * n_rep], kr)
        pack_parts = member_gather_chips(pack)

        firsts = [kf * n_rep for kf in range(1, n_feat)]

        def stacked(pairs, out, sems):
            copies, at = [], 0
            for i, ref in enumerate(pairs):
                copies.append(pltpu.make_async_copy(ref, out.at[at : at + ref.shape[0], :], sems.at[i]))
                at += ref.shape[0]
            return copies

        def grid_kernel(me_ref, *refs):
            states, packs = refs[:M], refs[M : 2 * M]
            enc_out, slope_out, table_out, weights_out = refs[2 * M + 4 : 2 * M + 8]
            outs, sems = refs[2 * M + 8 : 2 * M + 8 + n_dom], refs[-1]
            me = me_ref[0]
            weight_copies = stacked(refs[2 * M : 2 * M + 4], weights_out, sems)
            for each in weight_copies:
                each.start()
            for k in range(M):
                enc_out[rows_at(me ^ k, rows_enc), :] = packs[k][:rows_enc, :]
                rows = packs[k][rows_enc:, :].astype(F32).astype(jnp.int32)
                table_out[k, 0:1, :] = rows[0:1]
                table_out[k, 1:2, :] = 2 * rows[1:2] + rows[2:3]
            enc_cols = dot(enc_out[...], column_pick(me, D, C)).astype(BF)
            for k in range(M):
                pre = dot(states[k][...], enc_cols)
                logistic = jax.nn.sigmoid(pre)
                slope_out[k] = logistic * (1.0 + pre * (1.0 - logistic))
                message = (pre * logistic).astype(BF)
                rows = dot(hot_rows(table_out[k, 0:1, :], G), message).astype(BF)
                for j in range(n_dom):
                    outs[j][k * S : (k + 1) * S, :] = rows[j * S : (j + 1) * S]
            for each in weight_copies:
                each.wait()

        enc_full, grid_slope, slots, weights_own, *outgoing = call(
            grid_kernel,
            "grid_messages",
            me1,
            state_parts + pack_parts + [edge_in_weight, edge_out_weight, node_in_weight, node_out_weight],
            [shape((D, D)), shape((M, G, C), F32), shape((M, 2, NS), jnp.int32), shape((rows_edge + rows_mlp, D))]
            + [shape((M * S, C))] * n_dom,
            scratch=[pltpu.SemaphoreType.DMA((4,))],
            flops=2 * M * G * D * C + 2 * M * NS * G * C,
            far=range(2 * M, 2 * M + 4),
        )
        incoming = dom_trade(outgoing)
        near, others = range(n_rep), range(n_rep, M)
        weight_chips = [weights_own] + [member_swap(weights_own, k) for k in firsts]

        def encode_kernel(me_ref, base_ref, table_ref, *refs):
            arrived, state_out = far_first(refs[:n_dom]), refs[-1]
            total = dot(base_ref[...], column_pick(me_ref[0], D, C))
            for k in range(M):
                rows = stack([arrived[j][k * S : (k + 1) * S, :] for j in range(n_dom)])
                total += dot(hot_columns(table_ref[k, 1:2, :], N), rows)
            state_out[...] = total.astype(BF)

        state_cols = call(
            encode_kernel,
            "encode",
            me1,
            [mesh_base, slots] + far_first(incoming),
            [shape((N, C))],
            flops=2 * M * N * NS * C,
        )[0]
        state_chips = [state_cols] + [member_swap(state_cols, k) for k in firsts]

        def halo_kernel(me_ref, state_ref, halo_ref, *outs):
            rows = dot(hot_rows(halo_ref[...], N), state_ref[...]).astype(BF)
            for j in range(n_dom):
                outs[j][...] = rows[j * H : (j + 1) * H]

        halo_out = call(
            halo_kernel,
            "halo_rows",
            me1,
            [state_cols, halo_row],
            [shape((H, C))] * n_dom,
            flops=2 * N * NH * C,
        )
        halo_in = dom_trade(halo_out)
        core_swaps = lambda x: [x] + [member_swap(x, kr) for kr in range(1, n_rep)]

        def pair_kernel(me_ref, *refs):
            for kf in range(n_feat):
                refs[-1][kf] = refs[kf][...]

        def join_kernel(me_ref, *refs):
            halo, chips, weights = far_first(refs[:n_dom]), refs[n_dom : n_dom + n_feat], refs[n_dom + n_feat : -4]
            halo_out_ref, pair_out, edge_out, node_out = refs[-4:]
            for j in range(n_dom):
                halo_out_ref[j * H : (j + 1) * H, :] = halo[j][...]
            for kf in range(n_feat):
                pair_out[kf] = chips[kf][...]
                edge_out[kf] = weights[kf][:rows_edge, :]
                node_out[kf] = weights[kf][rows_edge:, :]

        halo_cols, state_pair, edge_pair, node_pair = call(
            join_kernel,
            "halo_join",
            me1,
            far_first(halo_in) + state_chips + weight_chips,
            [shape((NH, C)), shape((n_feat, N, C))]
            + [shape((n_feat, rows_edge, D)), shape((n_feat, rows_mlp, D))],
        )
        halo_chips = [halo_cols] + [member_swap(halo_cols, k) for k in firsts]
        state_pairs = core_swaps(state_pair)
        edge_pairs = core_swaps(edge_pair)
        node_pairs = core_swaps(node_pair)

        def local_kernel(me_ref, es_ref, send_ref, recv_ref, *refs):
            cols, weights = refs[:n_rep], refs[n_rep : 2 * n_rep]
            pre_out, state_out, w_out, out_out, parts = refs[2 * n_rep :]
            me = me_ref[0]
            for k in range(M):
                kf, kr = divmod(k, n_rep)
                parts[me ^ k] = cols[kr][kf]
                w_out[rows_at(me ^ k, rows_in), :] = weights[kr][kf, :rows_in, :]
                out_out[rows_at(me ^ k, rows_out), :] = weights[kr][kf, rows_in:, :]
            state_out[...] = lanes([parts[j] for j in range(M)])
            for i in range(E // T):
                at = slice(i * T, (i + 1) * T)
                sent = dot(send_ref[at, :], state_out[...]).astype(BF)
                got = dot(recv_ref[at, :], state_out[...]).astype(BF)
                pre_out[at, :] = (
                    dot(es_ref[at, :], w_out[:D, :])
                    + dot(sent, w_out[D : 2 * D, :])
                    + dot(got, w_out[2 * D :, :])
                )

        local_pre, mesh_state, in_full, out_full = call(
            local_kernel,
            "edge_local",
            me1,
            [edge_state, sl_hot, r_hot] + state_pairs + edge_pairs,
            [shape((E, D), F32), shape((N, D)), shape((3 * D, D)), shape((D, D))],
            scratch=[pltpu.VMEM((M, N, C), BF)],
            flops=2 * E * D * (3 * D + 2 * N),
        )

        halo_pair = call(
            pair_kernel,
            "halo_pair",
            me1,
            halo_chips + [local_pre],
            [shape((n_feat, NH, C))],
            unread=(n_feat,),
        )[0]
        halo_pairs = core_swaps(halo_pair)

        def edge_kernel(me_ref, local_ref, es_ref, send_ref, recv_ref, w_ref, out_ref, *refs):
            cols = refs[:n_rep]
            pre_out, outs = refs[n_rep], refs[n_rep + 1 : 2 * n_rep + 1]
            parts, halo, new, total = refs[2 * n_rep + 1 :]
            me = me_ref[0]
            for k in range(M):
                kf, kr = divmod(k, n_rep)
                parts[me ^ k] = cols[kr][kf]
            halo[...] = lanes([parts[j] for j in range(M)])
            for i in range(E // T):
                at = slice(i * T, (i + 1) * T)
                sent = dot(send_ref[at, :], halo[...]).astype(BF)
                pre = local_ref[at, :] + dot(sent, w_ref[D : 2 * D, :])
                pre_out[at, :] = pre
                hidden = (pre * jax.nn.sigmoid(pre)).astype(BF)
                new[at, :] = (es_ref[at, :].astype(F32) + dot(hidden, out_ref[...])).astype(BF)
            for i in range(N // T):
                at = slice(i * T, (i + 1) * T)
                total[at, :] = dot(recv_ref[at, :], new[...]).astype(BF)
            for kr in range(n_rep):
                for kf in range(n_feat):
                    outs[kr][kf] = total[rows_at(me ^ (kf * n_rep + kr), R), :]

        edge_pre, *sums = call(
            edge_kernel,
            "edge_update",
            me1,
            [local_pre, edge_state, sh_hot, rt_hot, in_full, out_full] + halo_pairs,
            [shape((E, D), F32)] + [shape((n_feat, R, D))] * n_rep,
            scratch=[
                pltpu.VMEM((M, NH, C), BF),
                pltpu.VMEM((NH, D), BF),
                pltpu.VMEM((E, D), BF),
                pltpu.VMEM((N, D), BF),
            ],
            flops=2 * E * D * (NH + D + D + N),
        )
        sums = member_sums(sums, me1, "node_sums")

        def node_ahead_kernel(me_ref, state_ref, grad_ref, *refs):
            weights = refs[:n_rep]
            node_in_full, pre_out, cot_out, node_out_full = refs[n_rep + 1 :]
            me = me_ref[0]
            for k in range(M):
                kf, kr = divmod(k, n_rep)
                node_in_full[rows_at(me ^ k, rows_node), :] = weights[kr][kf, :rows_node, :]
                node_out_full[rows_at(me ^ k, rows_out), :] = weights[kr][kf, rows_node:, :]
            mine = rows_at(me, R)
            pre_out[...] = dot(state_ref[mine, :], node_in_full[:D, :])
            cot_out[...] = dot_t(grad_ref[mine, :], node_out_full[...])

        node_in_full, node_pre, node_cot = call(
            node_ahead_kernel,
            "node_ahead",
            me1,
            [mesh_state, node_grad] + node_pairs + [sums[0]],
            [shape((2 * D, D)), shape((R, D), F32), shape((R, D), F32)],
            scratch=[pltpu.VMEM((D, D), BF)],
            flops=4 * R * D * D,
            unread=(2 + n_rep,),
        )

        def node_kernel(me_ref, pre_ref, cot_ref, w_ref, grad_ref, *refs):
            first_out, second_out = refs[n_feat:]
            total = refs[0][...].astype(F32)
            for k in range(1, n_feat):
                total += refs[k][...].astype(F32)
            pre = pre_ref[...] + dot(total.astype(BF), w_ref[D:, :])
            dpre = (cot_ref[...] * silu_slope(pre)).astype(BF)
            second_out[...] = dot_t(dpre, w_ref[D:, :]).astype(BF)
            mine = grad_ref[rows_at(me_ref[0], R), :].astype(F32)
            first_out[...] = mine + dot_t(dpre, w_ref[:D, :])

        node_first, node_second = call(
            node_kernel,
            "node_backward",
            me1,
            [node_pre, node_cot, node_in_full, node_grad] + sums,
            [shape((R, D), F32), shape((R, D))],
            flops=6 * R * D * D,
        )
        second_parts = member_gather_chips(node_second)

        def edge_back_kernel(me_ref, grad_ref, pre_ref, send_ref, recv_ref, w_ref, out_ref, *refs):
            nodes = refs[:M]
            dpre_out, outs = refs[M], refs[M + 1 : M + 1 + n_rep]
            second, parts = refs[M + 1 + n_rep :]
            me = me_ref[0]
            for k in range(M):
                second[rows_at(me ^ k, R), :] = nodes[k][...]
            for i in range(E // T):
                at = slice(i * T, (i + 1) * T)
                got = dot(recv_ref[at, :], second[...])
                cot = (grad_ref[at, :].astype(F32) + got).astype(BF)
                dpre_out[at, :] = (dot_t(cot, out_ref[...]) * silu_slope(pre_ref[at, :])).astype(BF)
            for i in range(NH // T):
                at = slice(i * T, (i + 1) * T)
                sent = dot(send_ref[at, :], dpre_out[...]).astype(BF)
                halo = dot_t(sent, w_ref[D : 2 * D, :]).astype(BF)
                for j in range(M):
                    parts[j, at, :] = halo[:, j * C : (j + 1) * C]
            for kr in range(n_rep):
                for kf in range(n_feat):
                    outs[kr][kf] = parts[me ^ (kf * n_rep + kr)]

        edge_dpre, *halo_grads = call(
            edge_back_kernel,
            "edge_backward",
            me1,
            [edge_grad, edge_pre, sht_hot, r_hot, in_full, out_full] + second_parts,
            [shape((E, D))] + [shape((n_feat, NH, C))] * n_rep,
            scratch=[pltpu.VMEM((N, D), BF), pltpu.VMEM((M, NH, C), BF)],
            flops=2 * E * D * (N + D + NH) + 2 * NH * D * D,
        )
        halo_grads = member_sums(halo_grads, me1, "halo_pairs")

        def local_back_kernel(me_ref, dpre_ref, send_ref, recv_ref, w_ref, first_ref, *refs):
            outs, (total, parts) = refs[:n_rep], refs[n_rep:]
            me = me_ref[0]
            for i in range(N // T):
                at = slice(i * T, (i + 1) * T)
                sent = dot(send_ref[at, :], dpre_ref[...]).astype(BF)
                got = dot(recv_ref[at, :], dpre_ref[...]).astype(BF)
                total[at, :] = dot_t(sent, w_ref[D : 2 * D, :]) + dot_t(got, w_ref[2 * D :, :])
            total[rows_at(me, R), :] += first_ref[...]
            for j in range(M):
                parts[j] = total[:, j * C : (j + 1) * C].astype(BF)
            for kr in range(n_rep):
                for kf in range(n_feat):
                    outs[kr][kf] = parts[me ^ (kf * n_rep + kr)]

        local_grads = call(
            local_back_kernel,
            "local_backward",
            me1,
            [edge_dpre, slt_hot, rt_hot, in_full, node_first],
            [shape((n_feat, N, C))] * n_rep,
            scratch=[pltpu.VMEM((N, D), F32), pltpu.VMEM((M, N, C), BF)],
            flops=4 * E * D * N + 4 * N * D * D,
        )
        local_grads = member_sums(local_grads, me1, "local_pairs")

        def halo_sum_kernel(me_ref, *refs):
            total = refs[0][...].astype(F32)
            for k in range(1, n_feat):
                total += refs[k][...].astype(F32)
            for j in range(n_dom):
                refs[n_feat + j][...] = total[j * H : (j + 1) * H].astype(BF)

        halo_back = call(halo_sum_kernel, "halo_sums", me1, halo_grads, [shape((H, C))] * n_dom)
        halo_back = dom_trade(halo_back)

        def owed_kernel(me_ref, halo_ref, table_ref, *refs):
            local, back = refs[:n_feat], far_first(refs[n_feat : n_feat + n_dom])
            first, second = refs[n_feat + n_dom : -n_dom], refs[-n_dom:]
            total = local[0][...].astype(F32)
            for k in range(1, n_feat):
                total += local[k][...].astype(F32)
            rows = stack([back[j][...] for j in range(n_dom)])
            cot = (total + dot(hot_columns(halo_ref[...], N), rows)).astype(BF)
            for k in range(M):
                owed = dot(hot_rows(table_ref[k, 1:2, :], N), cot).astype(BF)
                outs, at = (first, k) if k < n_rep else (second, k - n_rep)
                for j in range(n_dom):
                    outs[j][at * S : (at + 1) * S, :] = owed[j * S : (j + 1) * S]

        owed = call(
            owed_kernel,
            "owed_rows",
            me1,
            [halo_row, slots] + local_grads + far_first(halo_back),
            [shape((n_rep * S, C))] * n_dom + [shape((len(others) * S, C))] * n_dom,
            flops=2 * M * NS * N * C,
        )
        far_owed = dom_trade(owed[n_dom:])
        near_owed = dom_trade(owed[:n_dom])

        def cotangents(table_ref, slope_ref, arrived, at, k):
            rows = stack([arrived[j][at * S : (at + 1) * S, :] for j in range(n_dom)])
            cot = dot(hot_columns(table_ref[k, 0:1, :], G), rows)
            return (cot * slope_ref[k]).astype(BF)

        def grid_back(name, members, back, after):
            def kernel(me_ref, slope_ref, table_ref, *refs):
                outs = refs[n_dom + len(after) :]
                for at, k in enumerate(members):
                    outs[at][...] = cotangents(table_ref, slope_ref, far_first(refs[:n_dom]), at, k)

            return call(
                kernel,
                name,
                me1,
                [grid_slope, slots] + far_first(back) + after,
                [shape((G, C))] * len(members),
                flops=2 * len(members) * G * NS * C,
                unread=range(2 + n_dom, 2 + n_dom + len(after)),
            )

        far_dpre = grid_back("grid_back_far", others, far_owed, [])
        near_dpre = grid_back("grid_back_near", near, near_owed, far_dpre[:1])
        far_dpre = [member_swap(x, k) for x, k in zip(far_dpre, others)]

        def far_join_kernel(me_ref, *refs):
            for at in range(len(others)):
                refs[-1][at] = refs[at][...]

        far_dpre = call(
            far_join_kernel,
            "far_join",
            me1,
            far_dpre + near_dpre[:1],
            [shape((len(others), G, C))],
            unread=(len(others),),
        )
        near_dpre = [member_swap(x, k) if k else x for x, k in zip(near_dpre, near)]

        def adjoint_kernel(me_ref, enc_ref, far_ref, *refs):
            cols, (out, parts) = refs[:n_rep], refs[n_rep:]
            for k in range(M):
                parts[me_ref[0] ^ k] = cols[k][...] if k < n_rep else far_ref[k - n_rep]
            out[...] = dot_t(lanes([parts[j] for j in range(M)]), enc_ref[...])

        return call(
            adjoint_kernel,
            "adjoint",
            me1,
            [enc_full] + far_dpre + near_dpre,
            [shape((G, D), F32)],
            scratch=[pltpu.VMEM((M, G, C), BF)],
            flops=2 * G * D * D,
        )[0]

    return per_device


def solution(mesh):
    return jax.shard_map(
        make_per_device(mesh),
        mesh=mesh,
        in_specs=(
            P(("ens", "dom", "feat", "rep"), None),
            P("dom", None),
            P(("dom", "feat", "rep"), None),
            P(("feat", "rep"), None),
            P(("feat", "rep"), None),
            P(("feat", "rep"), None),
            P(("feat", "rep"), None),
            P(("feat", "rep"), None),
            P(("ens", "dom"), None),
            P(("ens", "dom", "feat", "rep"), None),
            P("dom", None, None),
            P(("dom", "feat", "rep")),
            P(("dom", "feat", "rep")),
            P(("dom", "feat", "rep"), None, None),
            P(("dom", "feat", "rep"), None, None),
        ),
        out_specs=P(("ens", "dom", "feat", "rep"), None),
        check_vma=False,
    )
```

```python
import jax
import jax.numpy as jnp
from jax import lax
from jax.experimental import pallas as pl
from jax.experimental.pallas import tpu as pltpu
from jax.sharding import PartitionSpec as P

BF = jnp.bfloat16
F32 = jnp.float32
SMEM = pl.BlockSpec(memory_space=pltpu.SMEM)
VMEM = pl.BlockSpec(memory_space=pltpu.VMEM)
HBM = pl.BlockSpec(memory_space=pltpu.HBM)
ANY = pl.BlockSpec(memory_space=pl.ANY)


def dot(a, b):
    return jnp.dot(a, b, preferred_element_type=F32)


def dot_t(a, b):
    return lax.dot_general(a, b, (((1,), (1,)), ((), ())), preferred_element_type=F32)


def silu_slope(values):
    logistic = jax.nn.sigmoid(values)
    return logistic * (1.0 + values * (1.0 - logistic))


def to_column(row):
    return jnp.transpose(jnp.broadcast_to(row, (8, row.shape[1])))[:, :1]


def hot_rows(row, depth):
    length = row.shape[1]
    return (to_column(row) == lax.broadcasted_iota(jnp.int32, (length, depth), 1)).astype(BF)


def hot_columns(row, depth):
    length = row.shape[1]
    return (row == lax.broadcasted_iota(jnp.int32, (depth, length), 0)).astype(BF)


def column_pick(me, depth, cols):
    at = lax.broadcasted_iota(jnp.int32, (depth, cols), 0) - me * cols
    return (at == lax.broadcasted_iota(jnp.int32, (depth, cols), 1)).astype(BF)


def rows_at(index, count):
    return pl.ds(pl.multiple_of(index * count, count), count)


def lanes(parts):
    return parts[0] if len(parts) == 1 else jnp.concatenate(parts, axis=1)


def stack(parts):
    return parts[0] if len(parts) == 1 else jnp.concatenate(parts, axis=0)


def call(body, name, me, ins, outs, scratch=(), flops=0, far=(), unread=()):
    size = lambda s: s.size * s.dtype.itemsize
    moved = sum(size(x) for x in ins) + sum(size(x) for x in outs)
    result = pl.pallas_call(
        body,
        out_shape=list(outs),
        in_specs=[SMEM] + [HBM if i in far else ANY if i in unread else VMEM for i in range(len(ins))],
        out_specs=[VMEM] * len(outs),
        scratch_shapes=list(scratch),
        compiler_params=pltpu.CompilerParams(vmem_limit_bytes=24 * 2**20),
        cost_estimate=pl.CostEstimate(flops=flops, bytes_accessed=moved, transcendentals=0),
        name=name,
    )(me, *[pltpu.with_memory_space_constraint(x, pltpu.HBM) if i in far else x for i, x in enumerate(ins)])
    return list(result)


def shape(dims, dtype=BF):
    return jax.ShapeDtypeStruct(tuple(dims), dtype)


def make_per_device(mesh):
    n_dom, n_feat, n_rep = mesh.shape["dom"], mesh.shape["feat"], mesh.shape["rep"]
    M = n_feat * n_rep

    def member_swap(x, k):
        return lax.ppermute(x, ("feat", "rep"), [(i, i ^ k) for i in range(M)])

    def dom_swap(x, k):
        return lax.ppermute(x, "dom", [(i, i ^ k) for i in range(n_dom)])

    def member_gather(x):
        return [x] + [member_swap(x, k) for k in range(1, M)]

    def member_gather_chips(x):
        parts = [None] * M
        for kf in range(n_feat):
            parts[kf * n_rep] = member_swap(x, kf * n_rep) if kf else x
        for kf in range(n_feat):
            for kr in range(1, n_rep):
                parts[kf * n_rep + kr] = member_swap(parts[kf * n_rep], kr)
        return parts

    def member_trade(parts):
        return [parts[0]] + [member_swap(parts[k], k) for k in range(1, M)]

    def member_sums(parts, me1, name):
        arrived = [parts[0]] + [member_swap(parts[kr], kr) for kr in range(1, n_rep)]

        def add_kernel(me_ref, *refs):
            for kf in range(n_feat):
                total = refs[0][kf].astype(F32)
                for kr in range(1, n_rep):
                    total += refs[kr][kf].astype(F32)
                refs[n_rep + kf][...] = total.astype(BF)

        halves = call(add_kernel, name, me1, arrived, [shape(parts[0].shape[1:])] * n_feat)
        return [halves[0]] + [member_swap(halves[kf], kf * n_rep) for kf in range(1, n_feat)]

    def dom_trade(parts):
        swapped = [dom_swap(parts[k], k) for k in reversed(range(1, n_dom))]
        return [parts[0]] + swapped[::-1]

    def far_first(parts):
        return [parts[0]] + list(parts[:0:-1])

    def per_device(
        grid_state,
        mesh_base,
        edge_state,
        enc_weight,
        edge_in_weight,
        edge_out_weight,
        node_in_weight,
        node_out_weight,
        node_grad,
        edge_grad,
        halo_rows,
        edge_send,
        edge_recv,
        grid_send,
        grid_recv,
    ):
        D = mesh_base.shape[1]
        N = mesh_base.shape[0]
        E = edge_state.shape[0]
        G = grid_state.shape[0]
        H = halo_rows.shape[2]
        S = grid_send.shape[2]
        NH = n_dom * H
        NS = n_dom * S
        C = D // M
        R = N // M
        T = 512
        PACK = 16
        assert NS == D
        rows_enc, rows_in, rows_out, rows_node = (
            enc_weight.shape[0],
            edge_in_weight.shape[0],
            edge_out_weight.shape[0],
            node_in_weight.shape[0],
        )
        rows_edge, rows_mlp = rows_in + rows_out, rows_node + rows_out
        me = lax.axis_index(("feat", "rep")).astype(jnp.int32)
        dom = lax.axis_index("dom").astype(jnp.int32)
        me1 = me.reshape(1)

        where = jnp.stack([me, dom])
        recv_row = edge_recv.reshape(1, E)

        def tables_kernel(where_ref, enc_ref, gs_ref, gr_ref, halo_ref, send_ref, *refs):
            pack_out, halo_out, send_out, gs, gr, halo, sent, sems = refs
            dom = where_ref[1]
            pairs = [
                (enc_ref, pack_out.at[:rows_enc, :]),
                (gs_ref.at[0], gs),
                (gr_ref.at[0], gr),
                (halo_ref.at[0], halo),
                (send_ref, sent),
            ]
            copies = [pltpu.make_async_copy(a, b, sems.at[i]) for i, (a, b) in enumerate(pairs)]
            for copy in copies:
                copy.start()
            for copy in copies:
                copy.wait()
            order = [pl.ds(dom ^ j, 1) for j in range(n_dom)]
            sends, recvs = lanes([gs[at, :] for at in order]), lanes([gr[at, :] for at in order])
            halo_out[...] = lanes([halo[at, :] for at in order])
            fill = jnp.zeros((PACK - 3, NS), jnp.int32)
            rows = stack([sends, recvs // 2, recvs % 2, fill])
            pack_out[rows_enc:, :] = rows.astype(F32).astype(BF)
            value = sent[...]
            away = jnp.maximum(value - N, 0)
            peer = away // H
            send_out[...] = jnp.where(value < N, value, N + (peer ^ dom) * H + (away - peer * H))

        pack, halo_row, send_row = call(
            tables_kernel,
            "tables",
            where,
            [enc_weight, grid_send, grid_recv, halo_rows, edge_send.reshape(1, E)],
            [shape((rows_enc + PACK, D)), shape((1, NH), jnp.int32), shape((1, E), jnp.int32)],
            scratch=[
                pltpu.VMEM((n_dom, S), jnp.int32),
                pltpu.VMEM((n_dom, S), jnp.int32),
                pltpu.VMEM((n_dom, H), jnp.int32),
                pltpu.VMEM((1, E), jnp.int32),
                pltpu.SemaphoreType.DMA((5,)),
            ],
            far=range(5),
        )

        def hots_kernel(me_ref, state_ref, send_ref, recv_ref, *refs):
            sl_out, sh_out, r_out, slt_out, sht_out, rt_out, state_out, sem = refs
            copy = pltpu.make_async_copy(state_ref, state_out, sem)
            copy.start()
            for i in range(E // T):
                at = slice(i * T, (i + 1) * T)
                sent, got = send_ref[:, at], recv_ref[:, at]
                sl_out[at, :] = hot_rows(sent, N)
                sh_out[at, :] = hot_rows(sent - N, NH)
                r_out[at, :] = hot_rows(got, N)
                slt_out[:, at] = hot_columns(sent, N)
                sht_out[:, at] = hot_columns(sent - N, NH)
                rt_out[:, at] = hot_columns(got, N)
            copy.wait()

        sl_hot, sh_hot, r_hot, slt_hot, sht_hot, rt_hot, state_own = call(
            hots_kernel,
            "edge_hots",
            me1,
            [grid_state, send_row, recv_row],
            [shape((E, N)), shape((E, NH)), shape((E, N)), shape((N, E)), shape((NH, E)), shape((N, E))]
            + [shape((G, D))],
            scratch=[pltpu.SemaphoreType.DMA(())],
            far=(0,),
        )

        state_parts = [state_own] + [None] * (M - 1)
        for kf in range(n_feat):
            if kf:
                state_parts[kf * n_rep] = member_swap(grid_state, kf * n_rep)
            for kr in range(1, n_rep):
                state_parts[kf * n_rep + kr] = member_swap(state_parts[kf * n_rep], kr)
        pack_parts = member_gather_chips(pack)

        firsts = [kf * n_rep for kf in range(1, n_feat)]

        def stacked(pairs, out, sems):
            copies, at = [], 0
            for i, ref in enumerate(pairs):
                copies.append(pltpu.make_async_copy(ref, out.at[at : at + ref.shape[0], :], sems.at[i]))
                at += ref.shape[0]
            return copies

        def grid_kernel(me_ref, *refs):
            states, packs = refs[:M], refs[M : 2 * M]
            enc_out, slope_out, table_out, weights_out = refs[2 * M + 4 : 2 * M + 8]
            outs, sems = refs[2 * M + 8 : 2 * M + 8 + n_dom], refs[-1]
            me = me_ref[0]
            weight_copies = stacked(refs[2 * M : 2 * M + 4], weights_out, sems)
            for each in weight_copies:
                each.start()
            for k in range(M):
                enc_out[rows_at(me ^ k, rows_enc), :] = packs[k][:rows_enc, :]
                rows = packs[k][rows_enc:, :].astype(F32).astype(jnp.int32)
                table_out[k, 0:1, :] = rows[0:1]
                table_out[k, 1:2, :] = 2 * rows[1:2] + rows[2:3]
            enc_cols = dot(enc_out[...], column_pick(me, D, C)).astype(BF)
            for k in range(M):
                pre = dot(states[k][...], enc_cols)
                logistic = jax.nn.sigmoid(pre)
                slope_out[k] = logistic * (1.0 + pre * (1.0 - logistic))
                message = (pre * logistic).astype(BF)
                rows = dot(hot_rows(table_out[k, 0:1, :], G), message).astype(BF)
                for j in range(n_dom):
                    outs[j][k * S : (k + 1) * S, :] = rows[j * S : (j + 1) * S]
            for each in weight_copies:
                each.wait()

        enc_full, grid_slope, slots, weights_own, *outgoing = call(
            grid_kernel,
            "grid_messages",
            me1,
            state_parts + pack_parts + [edge_in_weight, edge_out_weight, node_in_weight, node_out_weight],
            [shape((D, D)), shape((M, G, C), F32), shape((M, 2, NS), jnp.int32), shape((rows_edge + rows_mlp, D))]
            + [shape((M * S, C))] * n_dom,
            scratch=[pltpu.SemaphoreType.DMA((4,))],
            flops=2 * M * G * D * C + 2 * M * NS * G * C,
            far=range(2 * M, 2 * M + 4),
        )
        incoming = dom_trade(outgoing)
        near, others = range(n_rep), range(n_rep, M)
        weight_chips = [weights_own] + [member_swap(weights_own, k) for k in firsts]

        def encode_kernel(me_ref, base_ref, table_ref, *refs):
            arrived, state_out = far_first(refs[:n_dom]), refs[-1]
            total = dot(base_ref[...], column_pick(me_ref[0], D, C))
            for k in range(M):
                rows = stack([arrived[j][k * S : (k + 1) * S, :] for j in range(n_dom)])
                total += dot(hot_columns(table_ref[k, 1:2, :], N), rows)
            state_out[...] = total.astype(BF)

        state_cols = call(
            encode_kernel,
            "encode",
            me1,
            [mesh_base, slots] + far_first(incoming),
            [shape((N, C))],
            flops=2 * M * N * NS * C,
        )[0]
        state_chips = [state_cols] + [member_swap(state_cols, k) for k in firsts]

        def halo_kernel(me_ref, state_ref, halo_ref, *outs):
            rows = dot(hot_rows(halo_ref[...], N), state_ref[...]).astype(BF)
            for j in range(n_dom):
                outs[j][...] = rows[j * H : (j + 1) * H]

        halo_out = call(
            halo_kernel,
            "halo_rows",
            me1,
            [state_cols, halo_row],
            [shape((H, C))] * n_dom,
            flops=2 * N * NH * C,
        )
        halo_in = dom_trade(halo_out)
        core_swaps = lambda x: [x] + [member_swap(x, kr) for kr in range(1, n_rep)]

        def pair_kernel(me_ref, *refs):
            for kf in range(n_feat):
                refs[-1][kf] = refs[kf][...]

        def join_kernel(me_ref, *refs):
            halo, chips, weights = far_first(refs[:n_dom]), refs[n_dom : n_dom + n_feat], refs[n_dom + n_feat : -4]
            halo_out_ref, pair_out, edge_out, node_out = refs[-4:]
            for j in range(n_dom):
                halo_out_ref[j * H : (j + 1) * H, :] = halo[j][...]
            for kf in range(n_feat):
                pair_out[kf] = chips[kf][...]
                edge_out[kf] = weights[kf][:rows_edge, :]
                node_out[kf] = weights[kf][rows_edge:, :]

        halo_cols, state_pair, edge_pair, node_pair = call(
            join_kernel,
            "halo_join",
            me1,
            far_first(halo_in) + state_chips + weight_chips,
            [shape((NH, C)), shape((n_feat, N, C))]
            + [shape((n_feat, rows_edge, D)), shape((n_feat, rows_mlp, D))],
        )
        halo_chips = [halo_cols] + [member_swap(halo_cols, k) for k in firsts]
        state_pairs = core_swaps(state_pair)
        edge_pairs = core_swaps(edge_pair)
        node_pairs = core_swaps(node_pair)

        def local_kernel(me_ref, es_ref, send_ref, recv_ref, *refs):
            cols, weights = refs[:n_rep], refs[n_rep : 2 * n_rep]
            pre_out, state_out, w_out, out_out, parts = refs[2 * n_rep :]
            me = me_ref[0]
            for k in range(M):
                kf, kr = divmod(k, n_rep)
                parts[me ^ k] = cols[kr][kf]
                w_out[rows_at(me ^ k, rows_in), :] = weights[kr][kf, :rows_in, :]
                out_out[rows_at(me ^ k, rows_out), :] = weights[kr][kf, rows_in:, :]
            state_out[...] = lanes([parts[j] for j in range(M)])
            for i in range(E // T):
                at = slice(i * T, (i + 1) * T)
                sent = dot(send_ref[at, :], state_out[...]).astype(BF)
                got = dot(recv_ref[at, :], state_out[...]).astype(BF)
                pre_out[at, :] = (
                    dot(es_ref[at, :], w_out[:D, :])
                    + dot(sent, w_out[D : 2 * D, :])
                    + dot(got, w_out[2 * D :, :])
                )

        local_pre, mesh_state, in_full, out_full = call(
            local_kernel,
            "edge_local",
            me1,
            [edge_state, sl_hot, r_hot] + state_pairs + edge_pairs,
            [shape((E, D), F32), shape((N, D)), shape((3 * D, D)), shape((D, D))],
            scratch=[pltpu.VMEM((M, N, C), BF)],
            flops=2 * E * D * (3 * D + 2 * N),
        )

        halo_pair = call(
            pair_kernel,
            "halo_pair",
            me1,
            halo_chips + [local_pre],
            [shape((n_feat, NH, C))],
            unread=(n_feat,),
        )[0]
        halo_pairs = core_swaps(halo_pair)

        def edge_kernel(me_ref, local_ref, es_ref, send_ref, recv_ref, w_ref, out_ref, *refs):
            cols = refs[:n_rep]
            pre_out, outs = refs[n_rep], refs[n_rep + 1 : 2 * n_rep + 1]
            parts, halo, new, total = refs[2 * n_rep + 1 :]
            me = me_ref[0]
            for k in range(M):
                kf, kr = divmod(k, n_rep)
                parts[me ^ k] = cols[kr][kf]
            halo[...] = lanes([parts[j] for j in range(M)])
            for i in range(E // T):
                at = slice(i * T, (i + 1) * T)
                sent = dot(send_ref[at, :], halo[...]).astype(BF)
                pre = local_ref[at, :] + dot(sent, w_ref[D : 2 * D, :])
                pre_out[at, :] = pre
                hidden = (pre * jax.nn.sigmoid(pre)).astype(BF)
                new[at, :] = (es_ref[at, :].astype(F32) + dot(hidden, out_ref[...])).astype(BF)
            for i in range(N // T):
                at = slice(i * T, (i + 1) * T)
                total[at, :] = dot(recv_ref[at, :], new[...]).astype(BF)
            for kr in range(n_rep):
                for kf in range(n_feat):
                    outs[kr][kf] = total[rows_at(me ^ (kf * n_rep + kr), R), :]

        edge_pre, *sums = call(
            edge_kernel,
            "edge_update",
            me1,
            [local_pre, edge_state, sh_hot, rt_hot, in_full, out_full] + halo_pairs,
            [shape((E, D), F32)] + [shape((n_feat, R, D))] * n_rep,
            scratch=[
                pltpu.VMEM((M, NH, C), BF),
                pltpu.VMEM((NH, D), BF),
                pltpu.VMEM((E, D), BF),
                pltpu.VMEM((N, D), BF),
            ],
            flops=2 * E * D * (NH + D + D + N),
        )
        sums = member_sums(sums, me1, "node_sums")

        def node_ahead_kernel(me_ref, state_ref, grad_ref, *refs):
            weights = refs[:n_rep]
            node_in_full, pre_out, cot_out, node_out_full = refs[n_rep + 1 :]
            me = me_ref[0]
            for k in range(M):
                kf, kr = divmod(k, n_rep)
                node_in_full[rows_at(me ^ k, rows_node), :] = weights[kr][kf, :rows_node, :]
                node_out_full[rows_at(me ^ k, rows_out), :] = weights[kr][kf, rows_node:, :]
            mine = rows_at(me, R)
            pre_out[...] = dot(state_ref[mine, :], node_in_full[:D, :])
            cot_out[...] = dot_t(grad_ref[mine, :], node_out_full[...])

        node_in_full, node_pre, node_cot = call(
            node_ahead_kernel,
            "node_ahead",
            me1,
            [mesh_state, node_grad] + node_pairs + [sums[0]],
            [shape((2 * D, D)), shape((R, D), F32), shape((R, D), F32)],
            scratch=[pltpu.VMEM((D, D), BF)],
            flops=4 * R * D * D,
            unread=(2 + n_rep,),
        )

        def node_kernel(me_ref, pre_ref, cot_ref, w_ref, grad_ref, *refs):
            first_out, second_out = refs[n_feat:]
            total = refs[0][...].astype(F32)
            for k in range(1, n_feat):
                total += refs[k][...].astype(F32)
            pre = pre_ref[...] + dot(total.astype(BF), w_ref[D:, :])
            dpre = (cot_ref[...] * silu_slope(pre)).astype(BF)
            second_out[...] = dot_t(dpre, w_ref[D:, :]).astype(BF)
            mine = grad_ref[rows_at(me_ref[0], R), :].astype(F32)
            first_out[...] = mine + dot_t(dpre, w_ref[:D, :])

        node_first, node_second = call(
            node_kernel,
            "node_backward",
            me1,
            [node_pre, node_cot, node_in_full, node_grad] + sums,
            [shape((R, D), F32), shape((R, D))],
            flops=6 * R * D * D,
        )
        second_parts = member_gather_chips(node_second)

        def edge_back_kernel(me_ref, grad_ref, pre_ref, send_ref, recv_ref, w_ref, out_ref, *refs):
            nodes = refs[:M]
            dpre_out, outs = refs[M], refs[M + 1 : M + 1 + n_rep]
            second, parts = refs[M + 1 + n_rep :]
            me = me_ref[0]
            for k in range(M):
                second[rows_at(me ^ k, R), :] = nodes[k][...]
            for i in range(E // T):
                at = slice(i * T, (i + 1) * T)
                got = dot(recv_ref[at, :], second[...])
                cot = (grad_ref[at, :].astype(F32) + got).astype(BF)
                dpre_out[at, :] = (dot_t(cot, out_ref[...]) * silu_slope(pre_ref[at, :])).astype(BF)
            for i in range(NH // T):
                at = slice(i * T, (i + 1) * T)
                sent = dot(send_ref[at, :], dpre_out[...]).astype(BF)
                halo = dot_t(sent, w_ref[D : 2 * D, :]).astype(BF)
                for j in range(M):
                    parts[j, at, :] = halo[:, j * C : (j + 1) * C]
            for kr in range(n_rep):
                for kf in range(n_feat):
                    outs[kr][kf] = parts[me ^ (kf * n_rep + kr)]

        edge_dpre, *halo_grads = call(
            edge_back_kernel,
            "edge_backward",
            me1,
            [edge_grad, edge_pre, sht_hot, r_hot, in_full, out_full] + second_parts,
            [shape((E, D))] + [shape((n_feat, NH, C))] * n_rep,
            scratch=[pltpu.VMEM((N, D), BF), pltpu.VMEM((M, NH, C), BF)],
            flops=2 * E * D * (N + D + NH) + 2 * NH * D * D,
        )
        halo_grads = member_sums(halo_grads, me1, "halo_pairs")

        def local_back_kernel(me_ref, dpre_ref, send_ref, recv_ref, w_ref, first_ref, *refs):
            outs, (total, parts) = refs[:n_rep], refs[n_rep:]
            me = me_ref[0]
            for i in range(N // T):
                at = slice(i * T, (i + 1) * T)
                sent = dot(send_ref[at, :], dpre_ref[...]).astype(BF)
                got = dot(recv_ref[at, :], dpre_ref[...]).astype(BF)
                total[at, :] = dot_t(sent, w_ref[D : 2 * D, :]) + dot_t(got, w_ref[2 * D :, :])
            total[rows_at(me, R), :] += first_ref[...]
            for j in range(M):
                parts[j] = total[:, j * C : (j + 1) * C].astype(BF)
            for kr in range(n_rep):
                for kf in range(n_feat):
                    outs[kr][kf] = parts[me ^ (kf * n_rep + kr)]

        local_grads = call(
            local_back_kernel,
            "local_backward",
            me1,
            [edge_dpre, slt_hot, rt_hot, in_full, node_first],
            [shape((n_feat, N, C))] * n_rep,
            scratch=[pltpu.VMEM((N, D), F32), pltpu.VMEM((M, N, C), BF)],
            flops=4 * E * D * N + 4 * N * D * D,
        )
        local_grads = member_sums(local_grads, me1, "local_pairs")

        def halo_sum_kernel(me_ref, *refs):
            total = refs[0][...].astype(F32)
            for k in range(1, n_feat):
                total += refs[k][...].astype(F32)
            for j in range(n_dom):
                refs[n_feat + j][...] = total[j * H : (j + 1) * H].astype(BF)

        halo_back = call(halo_sum_kernel, "halo_sums", me1, halo_grads, [shape((H, C))] * n_dom)
        halo_back = dom_trade(halo_back)

        def owed_kernel(me_ref, halo_ref, table_ref, *refs):
            local, back = refs[:n_feat], far_first(refs[n_feat : n_feat + n_dom])
            first, second = refs[n_feat + n_dom : -n_dom], refs[-n_dom:]
            total = local[0][...].astype(F32)
            for k in range(1, n_feat):
                total += local[k][...].astype(F32)
            rows = stack([back[j][...] for j in range(n_dom)])
            cot = (total + dot(hot_columns(halo_ref[...], N), rows)).astype(BF)
            for k in range(M):
                owed = dot(hot_rows(table_ref[k, 1:2, :], N), cot).astype(BF)
                outs, at = (first, k) if k < n_rep else (second, k - n_rep)
                for j in range(n_dom):
                    outs[j][at * S : (at + 1) * S, :] = owed[j * S : (j + 1) * S]

        owed = call(
            owed_kernel,
            "owed_rows",
            me1,
            [halo_row, slots] + local_grads + far_first(halo_back),
            [shape((n_rep * S, C))] * n_dom + [shape((len(others) * S, C))] * n_dom,
            flops=2 * M * NS * N * C,
        )
        far_owed = dom_trade(owed[n_dom:])
        near_owed = dom_trade(owed[:n_dom])

        def cotangents(table_ref, slope_ref, arrived, at, k):
            rows = stack([arrived[j][at * S : (at + 1) * S, :] for j in range(n_dom)])
            cot = dot(hot_columns(table_ref[k, 0:1, :], G), rows)
            return (cot * slope_ref[k]).astype(BF)

        def grid_back(name, members, back, after):
            def kernel(me_ref, slope_ref, table_ref, *refs):
                outs = refs[n_dom + len(after) :]
                for at, k in enumerate(members):
                    outs[at][...] = cotangents(table_ref, slope_ref, far_first(refs[:n_dom]), at, k)

            return call(
                kernel,
                name,
                me1,
                [grid_slope, slots] + far_first(back) + after,
                [shape((G, C))] * len(members),
                flops=2 * len(members) * G * NS * C,
                unread=range(2 + n_dom, 2 + n_dom + len(after)),
            )

        far_dpre = grid_back("grid_back_far", others, far_owed, [])
        near_dpre = grid_back("grid_back_near", near, near_owed, far_dpre[:1])
        far_dpre = [member_swap(x, k) for x, k in zip(far_dpre, others)]

        def far_join_kernel(me_ref, *refs):
            for at in range(len(others)):
                refs[-1][at] = refs[at][...]

        far_dpre = call(
            far_join_kernel,
            "far_join",
            me1,
            far_dpre + near_dpre[:1],
            [shape((len(others), G, C))],
            unread=(len(others),),
        )
        near_dpre = [member_swap(x, k) if k else x for x, k in zip(near_dpre, near)]

        def adjoint_kernel(me_ref, enc_ref, far_ref, *refs):
            cols, (out, parts) = refs[:n_rep], refs[n_rep:]
            for k in range(M):
                parts[me_ref[0] ^ k] = cols[k][...] if k < n_rep else far_ref[k - n_rep]
            out[...] = dot_t(lanes([parts[j] for j in range(M)]), enc_ref[...])

        return call(
            adjoint_kernel,
            "adjoint",
            me1,
            [enc_full] + far_dpre + near_dpre,
            [shape((G, D), F32)],
            scratch=[pltpu.VMEM((M, G, C), BF)],
            flops=2 * G * D * D,
        )[0]

    return per_device


def solution(mesh):
    return jax.shard_map(
        make_per_device(mesh),
        mesh=mesh,
        in_specs=(
            P(("ens", "dom", "feat", "rep"), None),
            P("dom", None),
            P(("dom", "feat", "rep"), None),
            P(("feat", "rep"), None),
            P(("feat", "rep"), None),
            P(("feat", "rep"), None),
            P(("feat", "rep"), None),
            P(("feat", "rep"), None),
            P(("ens", "dom"), None),
            P(("ens", "dom", "feat", "rep"), None),
            P("dom", None, None),
            P(("dom", "feat", "rep")),
            P(("dom", "feat", "rep")),
            P(("dom", "feat", "rep"), None, None),
            P(("dom", "feat", "rep"), None, None),
        ),
        out_specs=P(("ens", "dom", "feat", "rep"), None),
        check_vma=False,
    )
```
